256 devices in a mesh: segment: 4 (over y_hi, core), face: 64 (over x, z, y_lo).
Axes of the slice: x: 4, y: 4 (y_hi: 2, y_lo: 2; y = y_hi * 2 + y_lo), z: 8, core: 2. Of those that a mesh axis runs over, the one named last changes fastest.
Arguments:
- states: float32 [4, 9, 32768], P('segment', None, 'face'), may hold values from -6 to 6
- gru_state: float32 [4, 180, 8192], P('segment', None, 'face'), may hold values from -1 to 1
- neighbours: int32 [128, 4], P('face'), may hold values from 0 to 127, as said below
- orient: int32 [128, 4], P('face'), may hold values from 0 to 7
- embed_weight: bfloat16 [90, 9], replicated, may hold values from -2 to 2
- enc_fine_depth: bfloat16 [90, 49], replicated, may hold values from -0.875 to 0.875
- enc_fine_expand: bfloat16 [360, 90], replicated, may hold values from -0.625 to 0.625
- enc_fine_shrink: bfloat16 [90, 360], replicated, may hold values from -0.3125 to 0.3125
- down_weight: bfloat16 [180, 90], replicated, may hold values from -0.625 to 0.625
- encoder_rough_spatial_kernel: bfloat16 [180, 49], replicated, may hold values from -0.875 to 0.875
- enc_coarse_expand: bfloat16 [720, 180], replicated, may hold values from -0.4375 to 0.4375
- enc_coarse_shrink: bfloat16 [180, 720], replicated, may hold values from -0.21875 to 0.21875
- gru_weight: bfloat16 [3, 180, 360], replicated, may hold values from -0.3125 to 0.3125
- dec_coarse_depth: bfloat16 [180, 49], replicated, may hold values from -0.875 to 0.875
- dec_coarse_expand: bfloat16 [720, 180], replicated, may hold values from -0.4375 to 0.4375
- dec_coarse_shrink: bfloat16 [180, 720], replicated, may hold values from -0.21875 to 0.21875
- up_weight: bfloat16 [90, 180], replicated, may hold values from -0.4375 to 0.4375
- combine_weight: bfloat16 [90, 180], replicated, may hold values from -0.4375 to 0.4375
- dec_fine_depth: bfloat16 [90, 49], replicated, may hold values from -0.875 to 0.875
- dec_fine_expand: bfloat16 [360, 90], replicated, may hold values from -0.625 to 0.625
- dec_fine_shrink: bfloat16 [90, 360], replicated, may hold values from -0.3125 to 0.3125
- head_weight: bfloat16 [9, 90], replicated, may hold values from -0.625 to 0.625
Outputs:
- forecast: float32 [2, 4, 9, 32768], P(None, 'segment', None, 'face')
- gru_final: float32 [4, 180, 8192], P('segment', None, 'face')
The draws below stay inside these ranges and needn't reach their ends.
Inputs may be any that keep to these rules, and one draw needn't show every extreme that they name: Tiles come in blocks of 2 consecutive ids, the blocks forming a closed loop; for a tile of block b, neighbours[t, 0] lies in block b - 1 and neighbours[t, 2] in block b + 1 (cyclically), neighbours[t, 1] and neighbours[t, 3] in block b.
All inputs are finite; a program needn't handle non-finite values.
Results may differ from the reference program's by a relative error of at most 0.025.
Values may be sent and summed in bfloat16 or wider, within the bound.
A program may use at most 64 MiB of HBM per device.

```python
import jax
import jax.numpy as jnp
from jax import lax

FIELDS = 9
C0 = 90
C1 = 180
SIDE0 = 16
SIDE1 = 8
TILE_DEV = 2
STEPS = 2
MEMBERS = 4
TILES = 128
CELLS = 32768
CELLS1 = 8192


def draw_neighbours(key, part):
    key = jax.random.fold_in(key, 11)
    first_key, second_key = jax.random.split(key)
    block_total = TILES // TILE_DEV
    tile_ids = jnp.arange(TILES, dtype=jnp.int32)
    block_numbers = tile_ids // TILE_DEV
    inner_ids = tile_ids % TILE_DEV
    north_pick = jax.random.randint(first_key, (TILES,), 0, TILE_DEV, dtype=jnp.int32)
    south_pick = jax.random.randint(second_key, (TILES,), 0, TILE_DEV, dtype=jnp.int32)
    north_ids = (block_numbers - 1 + block_total) % block_total * TILE_DEV + north_pick
    south_ids = (block_numbers + 1) % block_total * TILE_DEV + south_pick
    east_ids = block_numbers * TILE_DEV + (inner_ids + 1) % TILE_DEV
    west_ids = block_numbers * TILE_DEV + (inner_ids - 1 + TILE_DEV) % TILE_DEV
    return jnp.stack([north_ids, east_ids, south_ids, west_ids], 1).astype(jnp.int32)


def draw_orient(key, part):
    key = jax.random.fold_in(key, 23)
    return jax.random.randint(key, (TILES, 4), 0, 8, dtype=jnp.int32)


def shard_levels(rng, extent, shards, least, top_value):
    factor_of, own = 1.0, jax.random.fold_in(rng, 6)
    for dim, shards_of in shards:
        steps = jnp.exp(jax.random.uniform(jax.random.fold_in(own, dim), (shards_of,), jnp.float32, least / len(shards), top_value / len(shards)))
        factor_of = factor_of * jnp.repeat(steps, extent[dim] // shards_of).reshape([-1 if axis == dim else 1 for axis in range(len(extent))])
    return factor_of


def bell_draw(stream_key, shape, scale, bound, cuts=(), held_as=jnp.bfloat16):
    loudness = shard_levels(stream_key, shape, cuts, -0.22, 0.18) if cuts else 1.0
    entries = jax.random.normal(stream_key, shape, jnp.float32) * scale * loudness
    return jnp.minimum(jnp.maximum(entries, -bound), bound).astype(held_as)


def setup_inputs(seed: int = 0) -> dict:
    arg_keys = jax.random.split(jax.random.key(seed), 23)
    return {
        "states": bell_draw(arg_keys[0], (MEMBERS, FIELDS, CELLS), 1.0, 6.0, ((0, 4), (2, 64)), jnp.float32),
        "gru_state": jnp.clip(jax.random.uniform(arg_keys[1], (MEMBERS, C1, CELLS1), jnp.float32, -1.0, 1.0) * shard_levels(arg_keys[1], (MEMBERS, C1, CELLS1), ((0, 4), (2, 64)), -0.4, 0.0), -1.0, 1.0),
        "neighbours": draw_neighbours(jax.random.fold_in(arg_keys[22], 71), 0),
        "orient": draw_orient(jax.random.fold_in(arg_keys[22], 71), 0),
        "embed_weight": bell_draw(arg_keys[4], (C0, FIELDS), FIELDS ** -0.5, 2.0),
        "enc_fine_depth": bell_draw(arg_keys[5], (C0, 49), 49 ** -0.5, 0.875),
        "enc_fine_expand": bell_draw(arg_keys[6], (4 * C0, C0), C0 ** -0.5, 0.625),
        "enc_fine_shrink": bell_draw(arg_keys[7], (C0, 4 * C0), (4 * C0) ** -0.5, 0.3125),
        "down_weight": bell_draw(arg_keys[8], (C1, C0), C0 ** -0.5, 0.625),
        "encoder_rough_spatial_kernel": bell_draw(arg_keys[9], (C1, 49), 49 ** -0.5, 0.875),
        "enc_coarse_expand": bell_draw(arg_keys[10], (4 * C1, C1), C1 ** -0.5, 0.4375),
        "enc_coarse_shrink": bell_draw(arg_keys[11], (C1, 4 * C1), (4 * C1) ** -0.5, 0.21875),
        "gru_weight": bell_draw(arg_keys[12], (3, C1, 2 * C1), (2 * C1) ** -0.5, 0.3125),
        "dec_coarse_depth": bell_draw(arg_keys[13], (C1, 49), 49 ** -0.5, 0.875),
        "dec_coarse_expand": bell_draw(arg_keys[14], (4 * C1, C1), C1 ** -0.5, 0.4375),
        "dec_coarse_shrink": bell_draw(arg_keys[15], (C1, 4 * C1), (4 * C1) ** -0.5, 0.21875),
        "up_weight": bell_draw(arg_keys[16], (C0, C1), C1 ** -0.5, 0.4375),
        "combine_weight": bell_draw(arg_keys[17], (C0, 2 * C0), (2 * C0) ** -0.5, 0.4375),
        "dec_fine_depth": bell_draw(arg_keys[18], (C0, 49), 49 ** -0.5, 0.875),
        "dec_fine_expand": bell_draw(arg_keys[19], (4 * C0, C0), C0 ** -0.5, 0.625),
        "dec_fine_shrink": bell_draw(arg_keys[20], (C0, 4 * C0), (4 * C0) ** -0.5, 0.3125),
        "head_weight": bell_draw(arg_keys[21], (FIELDS, C0), C0 ** -0.5, 0.625),
    }


def tile_view(features, tile_side):
    return features.reshape(features.shape[0], features.shape[1] // (tile_side * tile_side), tile_side, tile_side)

def edge_rims(tiles):
    north_rim = jnp.stack([tiles[:, :, k, :] for k in range(3)], 0)
    east_rim = jnp.stack([tiles[:, :, :, -1 - k] for k in range(3)], 0)
    south_rim = jnp.stack([tiles[:, :, -1 - k, :] for k in range(3)], 0)
    west_rim = jnp.stack([tiles[:, :, :, k] for k in range(3)], 0)
    return jnp.transpose(jnp.stack([north_rim, east_rim, south_rim, west_rim], 0), (3, 0, 1, 2, 4))

def pick_halo(source, anchor, orient):
    chosen = source[anchor, orient // 2]
    flipped = (orient % 2 == 1)[:, :, None, None, None]
    return jnp.where(flipped, chosen[..., ::-1], chosen)

def depthwise(tiles, halo, kernel_taps):
    channels, tile_count, tile_side = (tiles.shape[0], tiles.shape[1], tiles.shape[2])
    rim_set = jnp.transpose(halo.astype(jnp.float32), (1, 2, 3, 0, 4))
    north_rim = jnp.transpose(rim_set[0, ::-1], (1, 2, 0, 3))
    south_rim = jnp.transpose(rim_set[2], (1, 2, 0, 3))
    east_rim = jnp.transpose(rim_set[1], (1, 2, 3, 0))
    west_rim = jnp.transpose(rim_set[3, ::-1], (1, 2, 3, 0))
    corner = jnp.zeros((channels, tile_count, 3, 3), jnp.float32)
    middle = jnp.concatenate([west_rim, tiles.astype(jnp.float32), east_rim], 3)
    upper_rows = jnp.concatenate([corner, north_rim, corner], 3)
    lowest_level = jnp.concatenate([corner, south_rim, corner], 3)
    padded = jnp.concatenate([upper_rows, middle, lowest_level], 2)
    kernel = kernel_taps.astype(jnp.float32)
    summed = jnp.zeros(tiles.shape, jnp.float32)
    for u in range(7):
        for v in range(7):
            summed = summed + kernel[:, u * 7 + v][:, None, None, None] * padded[:, :, u:u + tile_side, v:v + tile_side]
    return summed

def convnext_finish(features, tile_side, halo, depth, expand, shrink):
    spread = depthwise(tile_view(features, tile_side), halo, depth).reshape(features.shape)
    center = lax.optimization_barrier(jnp.mean(spread, 0, keepdims=True))
    varied = lax.optimization_barrier(jnp.mean(jnp.square(spread - center), 0, keepdims=True))
    normed = ((spread - center) * lax.rsqrt(varied + 1e-06)).astype(jnp.bfloat16)
    expanded = jax.nn.gelu(jnp.dot(expand, normed, preferred_element_type=jnp.float32), approximate=False).astype(jnp.bfloat16)
    return (features.astype(jnp.float32) + jnp.dot(shrink, expanded, preferred_element_type=jnp.float32)).astype(jnp.bfloat16)

def coarsen(features, tile_side):
    coarse_side = tile_side // 2
    grouped = features.astype(jnp.float32).reshape(features.shape[0], -1, coarse_side, 2, coarse_side, 2)
    return lax.optimization_barrier(jnp.mean(grouped, (3, 5))).reshape(features.shape[0], -1).astype(jnp.bfloat16)

def upsample(values, coarse_side):
    grouped = values.reshape(values.shape[0], -1, coarse_side, 1, coarse_side, 1)
    grouped = jnp.broadcast_to(grouped, grouped.shape[:3] + (2, coarse_side, 2))
    return grouped.reshape(values.shape[0], -1)

def recurrent_update(coarse, state_now, gate_weights):
    joined = jnp.concatenate([coarse, state_now.astype(jnp.bfloat16)], 0)
    update = jax.nn.sigmoid(jnp.dot(gate_weights[0], joined, preferred_element_type=jnp.float32))
    forget = jax.nn.sigmoid(jnp.dot(gate_weights[1], joined, preferred_element_type=jnp.float32))
    gated_state = (forget * state_now).astype(jnp.bfloat16)
    candidate = jnp.tanh(jnp.dot(gate_weights[2], jnp.concatenate([coarse, gated_state], 0), preferred_element_type=jnp.float32))
    return (1.0 - update) * state_now + update * candidate

def reference(states, gru_state, neighbours, orient, embed_weight, enc_fine_depth, enc_fine_expand, enc_fine_shrink, down_weight, encoder_rough_spatial_kernel, enc_coarse_expand, enc_coarse_shrink, gru_weight, dec_coarse_depth, dec_coarse_expand, dec_coarse_shrink, up_weight, combine_weight, dec_fine_depth, dec_fine_expand, dec_fine_shrink, head_weight):

    def convnext_block(features, tile_side, depth, expand, shrink):
        halo = pick_halo(edge_rims(tile_view(features, tile_side)), neighbours, orient)
        return convnext_finish(features, tile_side, halo, depth, expand, shrink)
    predicted_trajectory = []
    final_emitted_results = []
    for ensemble_realization in range(MEMBERS):
        weather = states[ensemble_realization]
        carried = gru_state[ensemble_realization]
        per_advance_results = []
        for step_number in range(STEPS):
            fine = jnp.dot(embed_weight, weather.astype(jnp.bfloat16), preferred_element_type=jnp.float32).astype(jnp.bfloat16)
            skip = convnext_block(fine, SIDE0, enc_fine_depth, enc_fine_expand, enc_fine_shrink)
            coarse = jnp.dot(down_weight, coarsen(skip, SIDE0), preferred_element_type=jnp.float32).astype(jnp.bfloat16)
            coarse = convnext_block(coarse, SIDE1, encoder_rough_spatial_kernel, enc_coarse_expand, enc_coarse_shrink)
            carried = recurrent_update(coarse, carried, gru_weight)
            unpacked_result = convnext_block(carried.astype(jnp.bfloat16), SIDE1, dec_coarse_depth, dec_coarse_expand, dec_coarse_shrink)
            lifted = jnp.dot(up_weight, unpacked_result, preferred_element_type=jnp.float32).astype(jnp.bfloat16)
            joined = jnp.concatenate([upsample(lifted, SIDE1), skip], 0)
            merged = jnp.dot(combine_weight, joined, preferred_element_type=jnp.float32).astype(jnp.bfloat16)
            merged = convnext_block(merged, SIDE0, dec_fine_depth, dec_fine_expand, dec_fine_shrink)
            weather = weather + jnp.dot(head_weight, merged, preferred_element_type=jnp.float32)
            per_advance_results.append(weather)
        predicted_trajectory.append(jnp.stack(per_advance_results, 0))
        final_emitted_results.append(carried)
    return (jnp.stack(predicted_trajectory, 1), jnp.stack(final_emitted_results, 0))
```

```python
import jax
import jax.numpy as jnp
from jax import lax
from jax.experimental import pallas as pl
from jax.experimental.pallas import tpu as pltpu
from jax.sharding import PartitionSpec as P

FIELDS = 9
C0 = 90
C1 = 180
SIDE0 = 16
SIDE1 = 8
TILES = 2
STEPS = 2
CELLS0 = TILES * SIDE0 * SIDE0
CELLS1 = TILES * SIDE1 * SIDE1
RIM0 = TILES * 3 * SIDE0
RIM1 = TILES * 3 * SIDE1
ROWS = 16
F32, BF16 = jnp.float32, jnp.bfloat16
NORTH, EAST, SOUTH, WEST = range(4)


def dot_nt(a, b):
    return lax.dot_general(a, b, (((1,), (1,)), ((), ())), preferred_element_type=F32)


def dot_nn(a, b):
    return jnp.dot(a, b, preferred_element_type=F32)


def one_hot(index, cells, axis):
    shape = (index.shape[0], cells) if axis == 1 else (cells, index.shape[1])
    hit = lax.broadcasted_iota(jnp.int32, shape, axis) == index
    return jnp.where(hit, 1.0, 0.0)


def rim_line(nbr, orient, tile, side, p):
    o = orient[tile, p]
    from_side = lax.shift_right_logical(o, 1)
    per_depth = jnp.where(
        from_side == 0, side, jnp.where(from_side == 1, -1, jnp.where(from_side == 2, -side, 1))
    )
    base = jnp.where(from_side == 1, side - 1, jnp.where(from_side == 2, side * (side - 1), 0))
    per_step = jnp.where((from_side & 1) == 0, 1, side)
    turned = (o & 1) == 1
    base = base + jnp.where(turned, per_step * (side - 1), 0)
    per_step = jnp.where(turned, -per_step, per_step)
    return base + (nbr[tile, p] & 1) * side * side, per_depth, per_step


def far_index(m, nbr, orient, side, p):
    index = jnp.full(m.shape, -1, jnp.int32)
    for tile in range(TILES):
        base, per_depth, per_step = rim_line(nbr, orient, tile, side, p)
        local = m - tile * 3 * side
        row = jnp.where(local >= 2 * side, 2, jnp.where(local >= side, 1, 0))
        depth = 2 - row if p == NORTH else row
        value = base + per_depth * depth + per_step * (local - row * side)
        index = jnp.where((local >= 0) & (local < 3 * side), value, index)
    return index


def near_index(nbr, orient, side):
    parts = []
    for tile in range(TILES):
        m = lax.broadcasted_iota(jnp.int32, (side * 8, 1), 0)
        row, place = lax.shift_right_logical(m, 3), m & 7
        base_e, depth_e, step_e = rim_line(nbr, orient, tile, side, EAST)
        base_w, depth_w, step_w = rim_line(nbr, orient, tile, side, WEST)
        east = base_e + depth_e * place + step_e * row
        west = base_w + depth_w * (7 - place) + step_w * row
        parts.append(jnp.where(place < 3, east, jnp.where(place >= 5, west, -1)))
    return jnp.concatenate(parts, 0)


def taps_first(weight, channels, lanes):
    wide = jnp.concatenate(
        [weight.astype(F32), jnp.zeros((channels, 128 - 49), F32)], 1
    )
    wide = jnp.concatenate([wide, jnp.zeros((lanes - channels, 128), F32)], 0)
    turned = wide.T[:49, :channels]
    return jnp.broadcast_to(turned[:, None, :], (49, 8, channels))


def normalise(y, channels):
    centred = y - jnp.sum(y, 1, keepdims=True) * (1.0 / channels)
    var = jnp.sum(centred * centred, 1, keepdims=True) * (1.0 / channels)
    return (centred * lax.rsqrt(var + 1e-6)).astype(BF16)


def gelu(x):
    return (0.5 * x) * (1.0 + lax.erf(x * 0.7071067811865476))


def finish(y, r, expand, shrink):
    normed = normalise(y, y.shape[1])
    expanded = gelu(dot_nt(normed, expand)).astype(BF16)
    return (r + dot_nt(expanded, shrink)).astype(BF16)


def conv_tile(pad, tile, rows, first, taps):
    total = None
    for q in range(7):
        x = pad[tile, :, first + q - 3 : first + q + 5, :]
        for u in range(7):
            term = taps[7 * u + q][None] * x[u : u + rows]
            total = term if total is None else total + term
    return total


def conv_halo(halo, side, tile, first, taps, rows):
    rows = list(rows)
    for q in range(7):
        for h in range(3):
            x = halo[side, tile, h, first + q - 3 : first + q + 5, :]
            for o in range(3):
                u = h - o if side == 0 else 6 + h - o
                if 0 <= u <= 6:
                    rows[o] = rows[o] + taps[7 * u + q] * x
    return rows


def kernel(
    states, gru_state, nbr, orient, embed_w, ef_depth, ef_expand, ef_shrink, down_w,
    ec_depth, ec_expand, ec_shrink, gru_w, dc_depth, dc_expand, dc_shrink,
    up_w, combine_w, df_depth, df_expand, df_shrink, head_w,
    forecast, gru_final,
    weather, carried, embed, gru_a, gru_b, comb_a, comb_b,
    taps_ef, taps_df, taps_ec, taps_dc,
    near0, near1, own_far, send0, send1, grow, pool,
    pad0, pad1, halo0, halo1, y0, y1, skip, merged,
    info_out, info_in, w_out, w_in, f_out, f_in, c_out, c_in,
    info_send, info_recv, w_send, w_recv, f_send, f_recv, c_send, c_recv,
):
    size = lax.axis_size("face")
    me = lax.axis_index("face")
    after, before = lax.rem(me + 1, size), lax.rem(me + size - 1, size)

    def pair(out, into, send, recv, slot=None):
        copies = []
        for way, target in enumerate((after, before)):
            src = out.at[way] if slot is None else out.at[slot, way]
            dst = into.at[way] if slot is None else into.at[slot, way]
            one = (way,) if slot is None else (slot, way)
            copies.append(
                pltpu.make_async_remote_copy(
                    src_ref=src, dst_ref=dst, send_sem=send.at[one], recv_sem=recv.at[one],
                    device_id={"face": target}, device_id_type=pl.DeviceIdType.MESH,
                )
            )
        return copies

    def start(copies):
        for copy in copies:
            copy.start()

    def wait(copies):
        for copy in copies:
            copy.wait()

    def weather_copies(step):
        copies = []
        for way, target in enumerate((after, before)):
            copies.append(
                pltpu.make_async_remote_copy(
                    src_ref=w_out.at[step], dst_ref=w_in.at[step, way],
                    send_sem=w_send.at[step, way], recv_sem=w_recv.at[step, way],
                    device_id={"face": target}, device_id_type=pl.DeviceIdType.MESH,
                )
            )
        return copies

    barrier = pltpu.get_barrier_semaphore()
    for target in (after, before):
        pl.semaphore_signal(
            barrier, inc=1, device_id={"face": target}, device_id_type=pl.DeviceIdType.MESH
        )

    weather[...] = jnp.zeros_like(weather)
    weather[:FIELDS] = states[0]
    w_out[0] = weather[...].astype(BF16)
    lane = lax.broadcasted_iota(jnp.int32, (1, 128), 1)
    for way, p in ((0, SOUTH), (1, NORTH)):
        info_out[way, 0:1] = far_index(lane, nbr, orient, SIDE0, p)
        info_out[way, 1:2] = far_index(lane, nbr, orient, SIDE1, p)
        info_out[way, 2:8] = jnp.zeros((6, 128), jnp.int32)
    pl.semaphore_wait(barrier, 2)
    info_copies = pair(info_out, info_in, info_send, info_recv)
    start(weather_copies(0))
    start(info_copies)

    embed[...] = jnp.zeros_like(embed)
    embed[:, :FIELDS] = embed_w[...].astype(F32)
    near0[...] = one_hot(near_index(nbr, orient, SIDE0), CELLS0, 1).astype(BF16)
    for way, p in ((0, NORTH), (1, SOUTH)):
        m = lax.broadcasted_iota(jnp.int32, (RIM0, 1), 0)
        own_far[way] = one_hot(far_index(m, nbr, orient, SIDE0, p), CELLS0, 1).astype(BF16)
    pad0[...] = jnp.zeros_like(pad0)
    halo0[...] = jnp.zeros_like(halo0)
    taps_ef[...] = taps_first(ef_depth[...], C0, 128)

    def prepare_rest():
        pad1[...] = jnp.zeros_like(pad1)
        halo1[...] = jnp.zeros_like(halo1)
        near1[...] = one_hot(near_index(nbr, orient, SIDE1), CELLS1, 1).astype(BF16)
        taps_df[...] = taps_first(df_depth[...], C0, 128)
        taps_ec[...] = taps_first(ec_depth[...], C1, 256)
        taps_dc[...] = taps_first(dc_depth[...], C1, 256)
        for g in range(3):
            wide = gru_w[g].astype(F32)
            gru_a[g] = wide[:, :C1].astype(BF16)
            gru_b[g] = wide[:, C1:].astype(BF16)
        wide = combine_w[...].astype(F32)
        comb_a[...] = wide[:, :C0].astype(BF16)
        comb_b[...] = wide[:, C0:].astype(BF16)

        def coarse_of(cell):
            tile = lax.shift_right_logical(cell, 8)
            row = lax.shift_right_logical(cell, 5) & 7
            return tile * 64 + row * 8 + (lax.shift_right_logical(cell, 1) & 7)

        cell = lax.broadcasted_iota(jnp.int32, (CELLS0, 1), 0)
        grow[...] = one_hot(coarse_of(cell), CELLS1, 1).astype(BF16)
        cell = lax.broadcasted_iota(jnp.int32, (1, CELLS0), 1)
        pool[...] = (0.25 * one_hot(coarse_of(cell), CELLS1, 0)).astype(BF16)
        state = jnp.concatenate([gru_state[0], jnp.zeros((256 - C1, CELLS1), F32)], 0)
        carried[...] = state.T[:, :C1]

    def prepare_sends():
        for way in range(2):
            wanted = info_in[1 - way]
            send0[way] = one_hot(wanted[0:1], CELLS0, 0).T[:RIM0].astype(BF16)
            send1[way] = one_hot(wanted[1:2], CELLS1, 0).T[:RIM1].astype(BF16)

    def fill0(r):
        pad0[:, 3 : 3 + SIDE0, 8:24, :] = r.astype(F32).reshape(TILES, SIDE0, SIDE0, C0)
        sides = dot_nn(near0[...], r).reshape(TILES, SIDE0, 8, C0)
        pad0[:, 3 : 3 + SIDE0, 0:8, :] = sides
        pad0[:, 3 : 3 + SIDE0, 24:32, :] = sides

    def fill1(r):
        pad1[:, 3 : 3 + SIDE1, 8:16, :] = r.astype(F32).reshape(TILES, SIDE1, SIDE1, C1)
        sides = dot_nn(near1[...], r).reshape(TILES, SIDE1, 8, C1)
        pad1[:, 3 : 3 + SIDE1, 0:8, :] = sides
        pad1[:, 3 : 3 + SIDE1, 16:24, :] = sides

    def fine_block_inner(taps, expand, shrink, out):
        def body(tile, _):
            for half in range(2):
                part = conv_tile(pad0, tile, SIDE0, 8 + 8 * half, taps)
                y0[tile, :, 8 * half : 8 * half + 8, :] = part
            y = y0[tile, 3:13].reshape(10 * SIDE0, C0)
            r = pad0[tile, 6:16, 8:24, :].reshape(10 * SIDE0, C0)
            out[tile, 3:13] = finish(y, r, expand[...], shrink[...]).reshape(10, SIDE0, C0)
            return 0

        lax.fori_loop(0, TILES, body, 0)

    def fine_block_outer(taps, expand, shrink, out):
        def body(tile, _):
            ys, rs = [], []
            for side, top in ((0, 0), (1, 13)):
                halves = []
                for half in range(2):
                    rows = [y0[tile, top + o, 8 * half : 8 * half + 8, :] for o in range(3)]
                    halves.append(conv_halo(halo0, side, tile, 8 + 8 * half, taps, rows))
                for o in range(3):
                    ys += [halves[0][o], halves[1][o]]
                rs.append(pad0[tile, top + 3 : top + 6, 8:24, :].reshape(3 * SIDE0, C0))
            y, r = jnp.concatenate(ys, 0), jnp.concatenate(rs, 0)
            done = finish(y, r, expand[...], shrink[...]).reshape(6, SIDE0, C0)
            out[tile, 0:3] = done[:3]
            out[tile, 13:16] = done[3:]
            return 0

        lax.fori_loop(0, TILES, body, 0)

    def coarse_block(r, slot, taps, expand, shrink):
        for way in range(2):
            c_out[slot, way] = dot_nn(send1[way], r).astype(BF16)
        copies = pair(c_out, c_in, c_send, c_recv, slot)
        start(copies)
        fill1(r)

        def body(tile, _):
            y1[tile] = conv_tile(pad1, tile, SIDE1, 8, taps)
            return 0

        lax.fori_loop(0, TILES, body, 0)
        wait(copies)
        for way in range(2):
            arrived = c_in[slot, way].astype(F32).reshape(TILES, 3, SIDE1, C1)
            halo1[way, :, :, 8:16, :] = arrived

        def edge(tile, _):
            for side, top in ((0, 0), (1, 5)):
                rows = [y1[tile, top + o] for o in range(3)]
                rows = conv_halo(halo1, side, tile, 8, taps, rows)
                for o in range(3):
                    y1[tile, top + o] = rows[o]
            return 0

        lax.fori_loop(0, TILES, edge, 0)
        y = y1[...].reshape(CELLS1, C1)
        return finish(y, r.astype(F32), expand[...], shrink[...])

    def step_body(step, _):
        fields = weather[...].astype(BF16).astype(F32).T.astype(BF16)
        lift = embed[...].astype(BF16)
        fill0(dot_nt(fields, lift).astype(BF16))
        fine_block_inner(taps_ef, ef_expand, ef_shrink, skip)

        @pl.when(step == 0)
        def _():
            prepare_rest()
            wait(info_copies)
            prepare_sends()

        wait(weather_copies(step))
        for way in range(2):
            rim = dot_nt(own_far[way], w_in[step, way]).astype(BF16)
            rim = dot_nt(rim, lift).astype(BF16).astype(F32)
            halo0[way, :, :, 8:24, :] = rim.reshape(TILES, 3, SIDE0, C0)
        fine_block_outer(taps_ef, ef_expand, ef_shrink, skip)

        kept = skip[...].reshape(CELLS0, C0)
        coarse = dot_nn(pool[...], kept).astype(BF16)
        coarse = dot_nt(coarse, down_w[...]).astype(BF16)
        coarse = coarse_block(coarse, 2 * step, taps_ec, ec_expand, ec_shrink)

        old = carried[...]
        held = old.astype(BF16)
        update = jax.nn.sigmoid(dot_nt(coarse, gru_a[0]) + dot_nt(held, gru_b[0]))
        reset = jax.nn.sigmoid(dot_nt(coarse, gru_a[1]) + dot_nt(held, gru_b[1]))
        gated = (reset * old).astype(BF16)
        candidate = jnp.tanh(dot_nt(coarse, gru_a[2]) + dot_nt(gated, gru_b[2]))
        new = (1.0 - update) * old + update * candidate
        carried[...] = new

        decoded = coarse_block(new.astype(BF16), 2 * step + 1, taps_dc, dc_expand, dc_shrink)

        lifted = dot_nt(decoded, up_w[...]).astype(BF16)
        lifted = dot_nn(grow[...], lifted).astype(BF16)
        joined = dot_nt(lifted, comb_a[...]) + dot_nt(kept, comb_b[...])
        joined = joined.astype(BF16)
        for way in range(2):
            f_out[step, way] = dot_nn(send0[way], joined).astype(BF16)
        copies = pair(f_out, f_in, f_send, f_recv, step)
        start(copies)
        fill0(joined)
        fine_block_inner(taps_df, df_expand, df_shrink, merged)
        wait(copies)
        for way in range(2):
            arrived = f_in[step, way].astype(F32).reshape(TILES, 3, SIDE0, C0)
            halo0[way, :, :, 8:24, :] = arrived
        fine_block_outer(taps_df, df_expand, df_shrink, merged)

        change = dot_nt(head_w[...], merged[...].reshape(CELLS0, C0))
        now = weather[:FIELDS] + change
        weather[:FIELDS] = now
        forecast[step, 0] = now

        @pl.when(step < STEPS - 1)
        def _():
            w_out[step + 1] = weather[...].astype(BF16)
            start(weather_copies(step + 1))

        return 0

    lax.fori_loop(0, STEPS, step_body, 0)
    last = jnp.concatenate([carried[...], jnp.zeros((CELLS1, 256 - C1), F32)], 1)
    gru_final[0] = last.T[:C1]


def local(states, gru_state, neighbours, orient, *weights):
    vmem = pl.BlockSpec(memory_space=pltpu.VMEM)
    smem = pl.BlockSpec(memory_space=pltpu.SMEM)
    scratch = [
        pltpu.VMEM((ROWS, CELLS0), F32),
        pltpu.VMEM((CELLS1, C1), F32),
        pltpu.VMEM((C0, ROWS), F32),
        pltpu.VMEM((3, C1, C1), BF16),
        pltpu.VMEM((3, C1, C1), BF16),
        pltpu.VMEM((C0, C0), BF16),
        pltpu.VMEM((C0, C0), BF16),
        pltpu.VMEM((49, 8, C0), F32),
        pltpu.VMEM((49, 8, C0), F32),
        pltpu.VMEM((49, 8, C1), F32),
        pltpu.VMEM((49, 8, C1), F32),
        pltpu.VMEM((TILES * SIDE0 * 8, CELLS0), BF16),
        pltpu.VMEM((TILES * SIDE1 * 8, CELLS1), BF16),
        pltpu.VMEM((2, RIM0, CELLS0), BF16),
        pltpu.VMEM((2, RIM0, CELLS0), BF16),
        pltpu.VMEM((2, RIM1, CELLS1), BF16),
        pltpu.VMEM((CELLS0, CELLS1), BF16),
        pltpu.VMEM((CELLS1, CELLS0), BF16),
        pltpu.VMEM((TILES, SIDE0 + 6, 32, C0), F32),
        pltpu.VMEM((TILES, SIDE1 + 6, 24, C1), F32),
        pltpu.VMEM((2, TILES, 3, 32, C0), F32),
        pltpu.VMEM((2, TILES, 3, 24, C1), F32),
        pltpu.VMEM((TILES, SIDE0, SIDE0, C0), F32),
        pltpu.VMEM((TILES, SIDE1, SIDE1, C1), F32),
        pltpu.VMEM((TILES, SIDE0, SIDE0, C0), BF16),
        pltpu.VMEM((TILES, SIDE0, SIDE0, C0), BF16),
        pltpu.VMEM((2, 8, 128), jnp.int32),
        pltpu.VMEM((2, 8, 128), jnp.int32),
        pltpu.VMEM((STEPS, ROWS, CELLS0), BF16),
        pltpu.VMEM((STEPS, 2, ROWS, CELLS0), BF16),
        pltpu.VMEM((STEPS, 2, RIM0, C0), BF16),
        pltpu.VMEM((STEPS, 2, RIM0, C0), BF16),
        pltpu.VMEM((2 * STEPS, 2, RIM1, C1), BF16),
        pltpu.VMEM((2 * STEPS, 2, RIM1, C1), BF16),
        pltpu.SemaphoreType.DMA((2,)),
        pltpu.SemaphoreType.DMA((2,)),
        pltpu.SemaphoreType.DMA((STEPS, 2)),
        pltpu.SemaphoreType.DMA((STEPS, 2)),
        pltpu.SemaphoreType.DMA((STEPS, 2)),
        pltpu.SemaphoreType.DMA((STEPS, 2)),
        pltpu.SemaphoreType.DMA((2 * STEPS, 2)),
        pltpu.SemaphoreType.DMA((2 * STEPS, 2)),
    ]
    return pl.pallas_call(
        kernel,
        out_shape=(
            jax.ShapeDtypeStruct((STEPS, 1, FIELDS, CELLS0), F32),
            jax.ShapeDtypeStruct((1, C1, CELLS1), F32),
        ),
        in_specs=[vmem, vmem, smem, smem] + [vmem] * len(weights),
        out_specs=(vmem, vmem),
        scratch_shapes=scratch,
        compiler_params=pltpu.CompilerParams(
            collective_id=0, has_side_effects=True, vmem_limit_bytes=48 * 1024 * 1024
        ),
    )(states, gru_state, neighbours, orient, *weights)


def solution(mesh):
    in_specs = (
        P("segment", None, "face"),
        P("segment", None, "face"),
        P("face", None),
        P("face", None),
    ) + (P(),) * 18
    out_specs = (P(None, "segment", None, "face"), P("segment", None, "face"))
    return jax.shard_map(local, mesh=mesh, in_specs=in_specs, out_specs=out_specs, check_vma=False)
```

```python
import jax
import jax.numpy as jnp
from jax import lax
from jax.experimental import pallas as pl
from jax.experimental.pallas import tpu as pltpu
from jax.sharding import PartitionSpec as P

FIELDS = 9
C0 = 90
C1 = 180
SIDE0 = 16
SIDE1 = 8
TILES = 2
STEPS = 2
CELLS0 = TILES * SIDE0 * SIDE0
CELLS1 = TILES * SIDE1 * SIDE1
RIM0 = TILES * 3 * SIDE0
RIM1 = TILES * 3 * SIDE1
ROWS = 16
F32, BF16 = jnp.float32, jnp.bfloat16
NORTH, EAST, SOUTH, WEST = range(4)


def dot_nt(a, b):
    return lax.dot_general(a, b, (((1,), (1,)), ((), ())), preferred_element_type=F32)


def dot_nn(a, b):
    return jnp.dot(a, b, preferred_element_type=F32)


def one_hot(index, cells, axis):
    shape = (index.shape[0], cells) if axis == 1 else (cells, index.shape[1])
    hit = lax.broadcasted_iota(jnp.int32, shape, axis) == index
    return jnp.where(hit, 1.0, 0.0)


def rim_line(nbr, orient, tile, side, p):
    o = orient[tile, p]
    from_side = lax.shift_right_logical(o, 1)
    per_depth = jnp.where(
        from_side == 0, side, jnp.where(from_side == 1, -1, jnp.where(from_side == 2, -side, 1))
    )
    base = jnp.where(from_side == 1, side - 1, jnp.where(from_side == 2, side * (side - 1), 0))
    per_step = jnp.where((from_side & 1) == 0, 1, side)
    turned = (o & 1) == 1
    base = base + jnp.where(turned, per_step * (side - 1), 0)
    per_step = jnp.where(turned, -per_step, per_step)
    return base + (nbr[tile, p] & 1) * side * side, per_depth, per_step


def far_index(m, nbr, orient, side, p):
    index = jnp.full(m.shape, -1, jnp.int32)
    for tile in range(TILES):
        base, per_depth, per_step = rim_line(nbr, orient, tile, side, p)
        local = m - tile * 3 * side
        row = jnp.where(local >= 2 * side, 2, jnp.where(local >= side, 1, 0))
        depth = 2 - row if p == NORTH else row
        value = base + per_depth * depth + per_step * (local - row * side)
        index = jnp.where((local >= 0) & (local < 3 * side), value, index)
    return index


def near_index(nbr, orient, side):
    parts = []
    for tile in range(TILES):
        m = lax.broadcasted_iota(jnp.int32, (side * 8, 1), 0)
        row, place = lax.shift_right_logical(m, 3), m & 7
        base_e, depth_e, step_e = rim_line(nbr, orient, tile, side, EAST)
        base_w, depth_w, step_w = rim_line(nbr, orient, tile, side, WEST)
        east = base_e + depth_e * place + step_e * row
        west = base_w + depth_w * (7 - place) + step_w * row
        parts.append(jnp.where(place < 3, east, jnp.where(place >= 5, west, -1)))
    return jnp.concatenate(parts, 0)


def spread_taps(weight):
    return jnp.broadcast_to(weight.astype(F32)[:, None, :], (49, 8, weight.shape[1]))


def halves(x):
    high = x.astype(BF16)
    return jnp.concatenate([high, (x - high.astype(F32)).astype(BF16)], 0)


def normalise(y, channels):
    centred = y - jnp.sum(y, 1, keepdims=True) * (1.0 / channels)
    var = jnp.sum(centred * centred, 1, keepdims=True) * (1.0 / channels)
    return (centred * lax.rsqrt(var + 1e-6)).astype(BF16)


def gelu(x):
    return (0.5 * x) * (1.0 + lax.erf(x * 0.7071067811865476))


def finish(y, r, expand, shrink):
    normed = normalise(y, y.shape[1])
    expanded = gelu(dot_nn(normed, expand)).astype(BF16)
    return (r + dot_nt(expanded, shrink)).astype(BF16)


def conv_tile(pad, tile, rows, first, taps):
    total = None
    for q in range(7):
        x = pad[tile, :, first + q - 3 : first + q + 5, :]
        for u in range(7):
            term = taps[7 * u + q][None] * x[u : u + rows]
            total = term if total is None else total + term
    return total


def conv_halo(halo, side, tile, first, taps, rows):
    rows = list(rows)
    for q in range(7):
        for h in range(3):
            x = halo[side, tile, h, first + q - 3 : first + q + 5, :]
            for o in range(3):
                u = h - o if side == 0 else 6 + h - o
                if 0 <= u <= 6:
                    rows[o] = rows[o] + taps[7 * u + q] * x
    return rows


WEIGHTS = 18


def kernel(
    states, gru_state, nbr, orient, *refs,
):
    hbm_weights, refs = refs[:WEIGHTS], refs[WEIGHTS:]
    forecast, gru_final = refs[:2]
    (
        embed_w, ef_depth, ef_expand, ef_shrink, down_w, ec_depth, ec_expand, ec_shrink,
        gru_w, dc_depth, dc_expand, dc_shrink, up_w, combine_w, df_depth, df_expand,
        df_shrink, head_w,
    ) = vmem_weights = refs[2 : 2 + WEIGHTS]
    (
        states_in, gru_in,
        weather, carried, embed, gru_a, gru_b, lift_w, comb_b,
        taps_ef, taps_df, taps_ec, taps_dc,
        near0, near1, own_far, far1, far0, grow, gather, far_grow,
        pad0, pad1, halo0, halo1, y0, y1, edge_y, edge_r, skip, merged,
        part, far_part, held_gates,
        info_out, info_in, w_out, w_in, f_out, f_in, c_out, c_in,
        load,
        info_send, info_recv, w_send, w_recv, f_send, f_recv, c_send, c_recv,
    ) = refs[2 + WEIGHTS :]
    size = lax.axis_size("face")
    me = lax.axis_index("face")
    after, before = lax.rem(me + 1, size), lax.rem(me + size - 1, size)

    def remote(src, dst, send, recv, target):
        return pltpu.make_async_remote_copy(
            src_ref=src, dst_ref=dst, send_sem=send, recv_sem=recv,
            device_id={"face": target}, device_id_type=pl.DeviceIdType.MESH,
        )

    def pair(out, into, send, recv, slot):
        return [
            remote(out.at[slot, w], into.at[slot, w], send.at[slot, w], recv.at[slot, w], target)
            for w, target in enumerate((after, before))
        ]

    def info_copies():
        return [
            remote(info_out.at[w], info_in.at[w], info_send.at[w], info_recv.at[w], target)
            for w, target in enumerate((after, before))
        ]

    def weather_copies(step):
        return [
            remote(w_out.at[step], w_in.at[step, w], w_send.at[step, w], w_recv.at[step, w], target)
            for w, target in enumerate((after, before))
        ]

    def start(copies):
        for copy in copies:
            copy.start()

    def wait(copies):
        for copy in copies:
            copy.wait()

    barrier = pltpu.get_barrier_semaphore()
    for target in (after, before):
        pl.semaphore_signal(
            barrier, inc=1, device_id={"face": target}, device_id_type=pl.DeviceIdType.MESH
        )
    loads = [pltpu.make_async_copy(states, states_in, load.at[0])]
    loads += [
        pltpu.make_async_copy(src, dst, load.at[2 + n])
        for n, (src, dst) in enumerate(zip(hbm_weights, vmem_weights))
    ]
    loads.append(pltpu.make_async_copy(gru_state, gru_in, load.at[1]))
    start(loads)

    lane = lax.broadcasted_iota(jnp.int32, (1, 128), 1)
    for way, p in ((0, SOUTH), (1, NORTH)):
        info_out[way, 0:1] = far_index(lane, nbr, orient, SIDE0, p)
        info_out[way, 1:2] = far_index(lane, nbr, orient, SIDE1, p)
        info_out[way, 2:8] = jnp.zeros((6, 128), jnp.int32)
    weather[...] = jnp.zeros_like(weather)
    loads[0].wait()
    weather[:FIELDS] = states_in[:, 0, :]
    w_out[0] = weather[...].astype(BF16)
    pl.semaphore_wait(barrier, 2)
    start(weather_copies(0))
    start(info_copies())

    near0[...] = one_hot(near_index(nbr, orient, SIDE0), CELLS0, 1).astype(BF16)
    for way, p in ((0, NORTH), (1, SOUTH)):
        m = lax.broadcasted_iota(jnp.int32, (RIM0, 1), 0)
        own_far[way] = one_hot(far_index(m, nbr, orient, SIDE0, p), CELLS0, 1).astype(BF16)
    pad0[...] = jnp.zeros_like(pad0)
    halo0[...] = jnp.zeros_like(halo0)
    for copy in loads[1:]:
        copy.wait()
    embed[...] = jnp.zeros_like(embed)
    embed[:FIELDS] = embed_w[...].astype(F32)
    taps_ef[...] = spread_taps(ef_depth[...])

    def prepare_rest():
        pad1[...] = jnp.zeros_like(pad1)
        halo1[...] = jnp.zeros_like(halo1)
        near1[...] = one_hot(near_index(nbr, orient, SIDE1), CELLS1, 1).astype(BF16)
        taps_df[...] = spread_taps(df_depth[...])
        taps_ec[...] = spread_taps(ec_depth[...])
        taps_dc[...] = spread_taps(dc_depth[...])
        for g in range(3):
            wide = gru_w[g].astype(F32)
            gru_a[g] = wide[:, :C1].astype(BF16)
            gru_b[g] = wide[:, C1:].astype(BF16)
        wide = combine_w[...].astype(F32)
        comb_b[...] = wide[C0:].astype(BF16)
        lift_w[...] = dot_nn(up_w[...], wide[:C0].astype(BF16)).astype(BF16)

        def coarse_of(cell):
            tile = lax.shift_right_logical(cell, 8)
            row = lax.shift_right_logical(cell, 5) & 7
            return tile * 64 + row * 8 + (lax.shift_right_logical(cell, 1) & 7)

        cell = lax.broadcasted_iota(jnp.int32, (CELLS0, 1), 0)
        one = one_hot(coarse_of(cell), CELLS1, 1).astype(BF16)
        grow[:, :CELLS1] = one
        grow[:, CELLS1:] = one
        cell = lax.broadcasted_iota(jnp.int32, (1, CELLS0), 1)
        gather[:CELLS1] = (0.25 * one_hot(coarse_of(cell), CELLS1, 0)).astype(BF16)
        state = jnp.concatenate(
            [gru_in[...].reshape(C1, CELLS1), jnp.zeros((256 - C1, CELLS1), F32)], 0
        )
        carried[...] = state.T[:, :C1]

    def prepare_sends():
        for way in range(2):
            wanted = info_in[1 - way]
            rows = slice(way * RIM0, (way + 1) * RIM0)
            far0[rows] = one_hot(wanted[0:1], CELLS0, 0).T[:RIM0].astype(BF16)
            rows = slice(way * RIM1, (way + 1) * RIM1)
            far1[rows] = one_hot(wanted[1:2], CELLS1, 0).T[:RIM1].astype(BF16)
        gather[CELLS1:] = dot_nn(far1[...], gather[:CELLS1]).astype(BF16)
        one = dot_nn(far0[...], grow[:, :CELLS1]).astype(BF16)
        far_grow[:, :CELLS1] = one
        far_grow[:, CELLS1:] = one

    def fill0(r):
        pad0[:, 3 : 3 + SIDE0, 8:24, :] = r.astype(F32).reshape(TILES, SIDE0, SIDE0, C0)
        sides = dot_nn(near0[...], r).reshape(TILES, SIDE0, 8, C0)
        pad0[:, 3 : 3 + SIDE0, 0:8, :] = sides
        pad0[:, 3 : 3 + SIDE0, 24:32, :] = sides

    def fill1(r):
        pad1[:, 3 : 3 + SIDE1, 8:16, :] = r.astype(F32).reshape(TILES, SIDE1, SIDE1, C1)
        sides = dot_nn(near1[...], r).reshape(TILES, SIDE1, 8, C1)
        pad1[:, 3 : 3 + SIDE1, 0:8, :] = sides
        pad1[:, 3 : 3 + SIDE1, 16:24, :] = sides

    def fine_block_inner(taps, expand, shrink, out):
        def body(tile, _):
            for half in range(2):
                total = conv_tile(pad0, tile, SIDE0, 8 + 8 * half, taps)
                y0[tile, :, 8 * half : 8 * half + 8, :] = total
            y = y0[tile, 3:13].reshape(10 * SIDE0, C0)
            r = pad0[tile, 6:16, 8:24, :].reshape(10 * SIDE0, C0)
            out[tile, 3:13] = finish(y, r, expand[...], shrink[...]).reshape(10, SIDE0, C0)
            return 0

        lax.fori_loop(0, TILES, body, 0)
        for tile in range(TILES):
            for side, top in ((0, 3), (1, 16)):
                edge_r[tile, side] = pad0[tile, top : top + 3, 8:24, :]

    def fine_block_outer(taps, expand, shrink, out):
        def body(tile, _):
            for side, top in ((0, 0), (1, 13)):
                for half in range(2):
                    columns = slice(8 * half, 8 * half + 8)
                    rows = [y0[tile, top + o, columns, :] for o in range(3)]
                    rows = conv_halo(halo0, side, tile, 8 + 8 * half, taps, rows)
                    for o in range(3):
                        edge_y[tile, side, o, columns, :] = rows[o]
            return 0

        lax.fori_loop(0, TILES, body, 0)
        y = edge_y[...].reshape(2 * RIM0, C0)
        r = edge_r[...].reshape(2 * RIM0, C0)
        done = finish(y, r, expand[...], shrink[...]).reshape(TILES, 2, 3, SIDE0, C0)
        for tile in range(TILES):
            out[tile, 0:3] = done[tile, 0]
            out[tile, 13:16] = done[tile, 1]

    def coarse_block(r, slot, taps, expand, shrink, meanwhile):
        copies = pair(c_out, c_in, c_send, c_recv, slot)
        start(copies)
        fill1(r)

        def body(tile, _):
            y1[tile] = conv_tile(pad1, tile, SIDE1, 8, taps)
            return 0

        lax.fori_loop(0, TILES, body, 0)
        meanwhile()
        wait(copies)
        for way in range(2):
            arrived = c_in[slot, way].astype(F32).reshape(TILES, 3, SIDE1, C1)
            halo1[way, :, :, 8:16, :] = arrived

        def edge(tile, _):
            for side, top in ((0, 0), (1, 5)):
                rows = [y1[tile, top + o] for o in range(3)]
                rows = conv_halo(halo1, side, tile, 8, taps, rows)
                for o in range(3):
                    y1[tile, top + o] = rows[o]
            return 0

        lax.fori_loop(0, TILES, edge, 0)
        y = y1[...].reshape(CELLS1, C1)
        return finish(y, r.astype(F32), expand[...], shrink[...])

    def step_body(step, _):
        fields = weather[...].astype(BF16).astype(F32).T.astype(BF16)
        lift = embed[...].astype(BF16)
        fill0(dot_nn(fields, lift).astype(BF16))
        fine_block_inner(taps_ef, ef_expand, ef_shrink, skip)

        @pl.when(step == 0)
        def _():
            prepare_rest()
            wait(info_copies())
            prepare_sends()

        wait(weather_copies(step))
        for way in range(2):
            rim = dot_nt(own_far[way], w_in[step, way]).astype(BF16)
            rim = dot_nn(rim, lift).astype(BF16).astype(F32)
            halo0[way, :, :, 8:24, :] = rim.reshape(TILES, 3, SIDE0, C0)
        fine_block_outer(taps_ef, ef_expand, ef_shrink, skip)

        coarse = dot_nn(gather[...], skip[...].reshape(CELLS0, C0)).astype(BF16)
        coarse = dot_nt(coarse, down_w[...]).astype(BF16)
        for way in range(2):
            top = CELLS1 + way * RIM1
            c_out[2 * step, way] = coarse[top : top + RIM1]

        def after_skip():
            kept = skip[...].reshape(CELLS0, C0)
            part[...] = dot_nn(kept, comb_b[...])
            far_part[...] = dot_nn(dot_nn(far0[...], kept).astype(BF16), comb_b[...])
            held = carried[...].astype(BF16)
            for g in range(2):
                held_gates[g] = dot_nt(held, gru_b[g])

        coarse = coarse_block(
            coarse[:CELLS1], 2 * step, taps_ec, ec_expand, ec_shrink, after_skip
        )

        old = carried[...]
        update = jax.nn.sigmoid(dot_nt(coarse, gru_a[0]) + held_gates[0])
        reset = jax.nn.sigmoid(dot_nt(coarse, gru_a[1]) + held_gates[1])
        gated = (reset * old).astype(BF16)
        candidate = jnp.tanh(dot_nt(coarse, gru_a[2]) + dot_nt(gated, gru_b[2]))
        new = (1.0 - update) * old + update * candidate
        carried[...] = new

        new = new.astype(BF16)
        wanted = dot_nn(far1[...], new).astype(BF16)
        for way in range(2):
            c_out[2 * step + 1, way] = wanted[way * RIM1 : (way + 1) * RIM1]

        def after_update():
            @pl.when(step == STEPS - 1)
            def _():
                last = jnp.concatenate([carried[...], jnp.zeros((CELLS1, 256 - C1), F32)], 1)
                gru_final[0] = last.T[:C1]

        decoded = coarse_block(
            new, 2 * step + 1, taps_dc, dc_expand, dc_shrink, after_update
        )

        lifted = halves(dot_nn(decoded, lift_w[...]))
        wanted = (dot_nn(far_grow[...], lifted) + far_part[...]).astype(BF16)
        for way in range(2):
            f_out[step, way] = wanted[way * RIM0 : (way + 1) * RIM0]
        copies = pair(f_out, f_in, f_send, f_recv, step)
        start(copies)
        fill0((dot_nn(grow[...], lifted) + part[...]).astype(BF16))
        fine_block_inner(taps_df, df_expand, df_shrink, merged)
        wait(copies)
        for way in range(2):
            arrived = f_in[step, way].astype(F32).reshape(TILES, 3, SIDE0, C0)
            halo0[way, :, :, 8:24, :] = arrived
        fine_block_outer(taps_df, df_expand, df_shrink, merged)

        change = dot_nt(head_w[...], merged[...].reshape(CELLS0, C0))
        now = weather[:FIELDS] + change
        weather[:FIELDS] = now

        @pl.when(step < STEPS - 1)
        def _():
            w_out[step + 1] = weather[...].astype(BF16)
            start(weather_copies(step + 1))

        forecast[step, 0] = now
        return 0

    lax.fori_loop(0, STEPS, step_body, 0)


def local(states, gru_state, neighbours, orient, *weights):
    (
        embed_w, ef_depth, ef_expand, ef_shrink, down_w, ec_depth, ec_expand, ec_shrink,
        gru_w, dc_depth, dc_expand, dc_shrink, up_w, combine_w, df_depth, df_expand,
        df_shrink, head_w,
    ) = weights
    weights = (
        embed_w.T, ef_depth.T, ef_expand.T, ef_shrink, down_w, ec_depth.T, ec_expand.T, ec_shrink,
        gru_w, dc_depth.T, dc_expand.T, dc_shrink, up_w.T, combine_w.T, df_depth.T, df_expand.T,
        df_shrink, head_w,
    )
    hbm = pl.BlockSpec(memory_space=pltpu.HBM)
    smem = pl.BlockSpec(memory_space=pltpu.SMEM)
    scratch = [pltpu.VMEM(w.shape, w.dtype) for w in weights]
    scratch += [
        pltpu.VMEM((FIELDS, 1, CELLS0), F32),
        pltpu.VMEM((C1, 1, CELLS1), F32),
        pltpu.VMEM((ROWS, CELLS0), F32),
        pltpu.VMEM((CELLS1, C1), F32),
        pltpu.VMEM((ROWS, C0), F32),
        pltpu.VMEM((3, C1, C1), BF16),
        pltpu.VMEM((3, C1, C1), BF16),
        pltpu.VMEM((C1, C0), BF16),
        pltpu.VMEM((C0, C0), BF16),
        pltpu.VMEM((49, 8, C0), F32),
        pltpu.VMEM((49, 8, C0), F32),
        pltpu.VMEM((49, 8, C1), F32),
        pltpu.VMEM((49, 8, C1), F32),
        pltpu.VMEM((TILES * SIDE0 * 8, CELLS0), BF16),
        pltpu.VMEM((TILES * SIDE1 * 8, CELLS1), BF16),
        pltpu.VMEM((2, RIM0, CELLS0), BF16),
        pltpu.VMEM((2 * RIM1, CELLS1), BF16),
        pltpu.VMEM((2 * RIM0, CELLS0), BF16),
        pltpu.VMEM((CELLS0, 2 * CELLS1), BF16),
        pltpu.VMEM((CELLS1 + 2 * RIM1, CELLS0), BF16),
        pltpu.VMEM((2 * RIM0, 2 * CELLS1), BF16),
        pltpu.VMEM((TILES, SIDE0 + 6, 32, C0), F32),
        pltpu.VMEM((TILES, SIDE1 + 6, 24, C1), F32),
        pltpu.VMEM((2, TILES, 3, 32, C0), F32),
        pltpu.VMEM((2, TILES, 3, 24, C1), F32),
        pltpu.VMEM((TILES, SIDE0, SIDE0, C0), F32),
        pltpu.VMEM((TILES, SIDE1, SIDE1, C1), F32),
        pltpu.VMEM((TILES, 2, 3, SIDE0, C0), F32),
        pltpu.VMEM((TILES, 2, 3, SIDE0, C0), F32),
        pltpu.VMEM((TILES, SIDE0, SIDE0, C0), BF16),
        pltpu.VMEM((TILES, SIDE0, SIDE0, C0), BF16),
        pltpu.VMEM((CELLS0, C0), F32),
        pltpu.VMEM((2 * RIM0, C0), F32),
        pltpu.VMEM((2, CELLS1, C1), F32),
        pltpu.VMEM((2, 8, 128), jnp.int32),
        pltpu.VMEM((2, 8, 128), jnp.int32),
        pltpu.VMEM((STEPS, ROWS, CELLS0), BF16),
        pltpu.VMEM((STEPS, 2, ROWS, CELLS0), BF16),
        pltpu.VMEM((STEPS, 2, RIM0, C0), BF16),
        pltpu.VMEM((STEPS, 2, RIM0, C0), BF16),
        pltpu.VMEM((2 * STEPS, 2, RIM1, C1), BF16),
        pltpu.VMEM((2 * STEPS, 2, RIM1, C1), BF16),
        pltpu.SemaphoreType.DMA((2 + WEIGHTS,)),
        pltpu.SemaphoreType.DMA((2,)),
        pltpu.SemaphoreType.DMA((2,)),
        pltpu.SemaphoreType.DMA((STEPS, 2)),
        pltpu.SemaphoreType.DMA((STEPS, 2)),
        pltpu.SemaphoreType.DMA((STEPS, 2)),
        pltpu.SemaphoreType.DMA((STEPS, 2)),
        pltpu.SemaphoreType.DMA((2 * STEPS, 2)),
        pltpu.SemaphoreType.DMA((2 * STEPS, 2)),
    ]
    return pl.pallas_call(
        kernel,
        out_shape=(
            jax.ShapeDtypeStruct((STEPS, 1, FIELDS, CELLS0), F32),
            jax.ShapeDtypeStruct((1, C1, CELLS1), F32),
        ),
        in_specs=[hbm, hbm, smem, smem] + [hbm] * len(weights),
        out_specs=(pl.BlockSpec(memory_space=pltpu.VMEM),) * 2,
        scratch_shapes=scratch,
        compiler_params=pltpu.CompilerParams(
            collective_id=0, has_side_effects=True, vmem_limit_bytes=56 * 1024 * 1024
        ),
    )(states.transpose(1, 0, 2), gru_state.transpose(1, 0, 2), neighbours, orient, *weights)


def solution(mesh):
    in_specs = (
        P("segment", None, "face"),
        P("segment", None, "face"),
        P("face", None),
        P("face", None),
    ) + (P(),) * 18
    out_specs = (P(None, "segment", None, "face"), P("segment", None, "face"))
    return jax.shard_map(local, mesh=mesh, in_specs=in_specs, out_specs=out_specs, check_vma=False)
```

```python
import jax
import jax.numpy as jnp
from jax import lax
from jax.experimental import pallas as pl
from jax.experimental.pallas import tpu as pltpu
from jax.sharding import PartitionSpec as P

FIELDS = 9
C0 = 90
C1 = 180
SIDE0 = 16
SIDE1 = 8
TILES = 2
STEPS = 2
CELLS0 = TILES * SIDE0 * SIDE0
CELLS1 = TILES * SIDE1 * SIDE1
RIM0 = TILES * 3 * SIDE0
RIM1 = TILES * 3 * SIDE1
ROWS = 16
F32, BF16 = jnp.float32, jnp.bfloat16
NORTH, EAST, SOUTH, WEST = range(4)
ROW = 16


def dot_nt(a, b):
    return lax.dot_general(a, b, (((1,), (1,)), ((), ())), preferred_element_type=F32)


def dot_nn(a, b):
    return jnp.dot(a, b, preferred_element_type=F32)


def one_hot(index, cells, axis):
    shape = (index.shape[0], cells) if axis == 1 else (cells, index.shape[1])
    hit = lax.broadcasted_iota(jnp.int32, shape, axis) == index
    return jnp.where(hit, 1.0, 0.0)


def rim_line(nbr, orient, tile, side, p):
    o = orient[tile, p]
    from_side = lax.shift_right_logical(o, 1)
    per_depth = jnp.where(
        from_side == 0, side, jnp.where(from_side == 1, -1, jnp.where(from_side == 2, -side, 1))
    )
    base = jnp.where(from_side == 1, side - 1, jnp.where(from_side == 2, side * (side - 1), 0))
    per_step = jnp.where((from_side & 1) == 0, 1, side)
    turned = (o & 1) == 1
    base = base + jnp.where(turned, per_step * (side - 1), 0)
    per_step = jnp.where(turned, -per_step, per_step)
    return base + (nbr[tile, p] & 1) * side * side, per_depth, per_step


def far_index(m, nbr, orient, side, p):
    index = jnp.full(m.shape, -1, jnp.int32)
    for tile in range(TILES):
        base, per_depth, per_step = rim_line(nbr, orient, tile, side, p)
        local = m - tile * 3 * side
        row = jnp.where(local >= 2 * side, 2, jnp.where(local >= side, 1, 0))
        depth = 2 - row if p == NORTH else row
        value = base + per_depth * depth + per_step * (local - row * side)
        index = jnp.where((local >= 0) & (local < 3 * side), value, index)
    return index


def near_index(m, nbr, orient, side):
    index = jnp.full(m.shape, -1, jnp.int32)
    for tile in range(TILES):
        base_e, depth_e, step_e = rim_line(nbr, orient, tile, side, EAST)
        base_w, depth_w, step_w = rim_line(nbr, orient, tile, side, WEST)
        local = m - tile * side * 8
        row, place = lax.shift_right_arithmetic(local, 3), local & 7
        east = base_e + depth_e * place + step_e * row
        west = base_w + depth_w * (7 - place) + step_w * row
        value = jnp.where(place < 3, east, jnp.where(place >= 5, west, -1))
        index = jnp.where((local >= 0) & (local < 8 * side), value, index)
    return index


def host_of(block, size):
    last = lax.rem(block, ROW) == ROW - 1
    return jnp.where(last, lax.rem(block + ROW, size), block)


def block_of(device, size):
    last = lax.rem(device, ROW) == ROW - 1
    return jnp.where(last, lax.rem(device + size - ROW, size), device)


def spread_taps(weight):
    return jnp.broadcast_to(weight.astype(F32)[:, None, :], (49, 8, weight.shape[1]))


def halves(x):
    high = x.astype(BF16)
    return jnp.concatenate([high, (x - high.astype(F32)).astype(BF16)], 0)


def normalise(y, channels):
    centred = y - jnp.sum(y, 1, keepdims=True) * (1.0 / channels)
    var = jnp.sum(centred * centred, 1, keepdims=True) * (1.0 / channels)
    return (centred * lax.rsqrt(var + 1e-6)).astype(BF16)


def gelu(x):
    return (0.5 * x) * (1.0 + lax.erf(x * 0.7071067811865476))


def finish(y, r, expand, shrink):
    normed = normalise(y, y.shape[1])
    expanded = gelu(dot_nn(normed, expand)).astype(BF16)
    return (r + dot_nt(expanded, shrink)).astype(BF16)


def conv_tile(pad, tile, rows, first, taps):
    total = None
    for q in range(7):
        x = pad[tile, :, first + q - 3 : first + q + 5, :]
        for u in range(7):
            term = taps[7 * u + q][None] * x[u : u + rows]
            total = term if total is None else total + term
    return total


def conv_halo(halo, side, tile, first, taps, rows):
    rows = list(rows)
    for q in range(7):
        for h in range(3):
            x = halo[side, tile, h, first + q - 3 : first + q + 5, :]
            for o in range(3):
                u = h - o if side == 0 else 6 + h - o
                if 0 <= u <= 6:
                    rows[o] = rows[o] + taps[7 * u + q] * x
    return rows


WEIGHTS = 18


def kernel(
    states, gru_state, nbr, orient, *refs,
):
    hbm_weights, refs = refs[:WEIGHTS], refs[WEIGHTS:]
    forecast, gru_final = refs[:2]
    (
        embed_w, ef_depth, ef_expand, ef_shrink, down_w, ec_depth, ec_expand, ec_shrink,
        gru_w, dc_depth, dc_expand, dc_shrink, up_w, combine_w, df_depth, df_expand,
        df_shrink, head_w,
    ) = vmem_weights = refs[2 : 2 + WEIGHTS]
    (
        states_in, gru_in, states_moved, gru_moved, info_moved,
        result_out, result_in, gru_out, gru_back,
        weather, carried, embed, gru_a, gru_b, lift_w, comb_b,
        taps_ef, taps_df, taps_ec, taps_dc,
        near0, near1, own_far, far1, far0, grow, gather, far_grow,
        pad0, pad1, halo0, halo1, y0, y1, edge_y, edge_r, skip, merged,
        part, far_part, held_gates,
        info_out, info_in, w_out, w_in, f_out, f_in, c_out, c_in,
        load,
        m_send, m_recv, r_send, r_recv, info_send, info_recv, w_send, w_recv, f_send, f_recv, c_send, c_recv,
    ) = refs[2 + WEIGHTS :]
    size = lax.axis_size("face")
    me = lax.axis_index("face")
    mine, away = block_of(me, size), host_of(me, size)
    moved = away != me
    own_after, own_before = (lax.rem(me + k, size) for k in (1, size - 1))
    home_after, home_before = (lax.rem(mine + k, size) for k in (1, size - 1))
    after, before = host_of(home_after, size), host_of(home_before, size)
    first_targets = host_of(own_after, size), host_of(own_before, size)

    def remote(src, dst, send, recv, target):
        return pltpu.make_async_remote_copy(
            src_ref=src, dst_ref=dst, send_sem=send, recv_sem=recv,
            device_id={"face": target}, device_id_type=pl.DeviceIdType.MESH,
        )

    def pair(out, into, send, recv, slot):
        return [
            remote(out.at[slot, w], into.at[slot, w], send.at[slot, w], recv.at[slot, w], target)
            for w, target in enumerate((after, before))
        ]

    def info_copies():
        return [
            remote(info_out, info_in.at[w], info_send.at[w], info_recv.at[w], target)
            for w, target in enumerate(first_targets)
        ]

    def weather_copies(step, targets):
        return [
            remote(w_out.at[step], w_in.at[step, w], w_send.at[step, w], w_recv.at[step, w], target)
            for w, target in enumerate(targets)
        ]

    def state_copy():
        return remote(states_in, states_moved, m_send.at[0], m_recv.at[0], away)

    def own_info_copy():
        return remote(info_out, info_moved, m_send.at[1], m_recv.at[1], away)

    def gru_copy():
        return remote(gru_in, gru_moved, m_send.at[2], m_recv.at[2], away)

    def result_copy(step):
        return remote(
            result_out.at[step], result_in.at[step], r_send.at[step], r_recv.at[step], mine
        )

    def gru_result_copy():
        return remote(gru_out, gru_back, m_send.at[3], m_recv.at[3], mine)

    def start(copies):
        for copy in copies:
            copy.start()

    def wait(copies):
        for copy in copies:
            copy.wait()

    barrier = pltpu.get_barrier_semaphore()
    for target in (home_after, home_before, after, before):
        pl.semaphore_signal(
            barrier, inc=1, device_id={"face": target}, device_id_type=pl.DeviceIdType.MESH
        )

    @pl.when(moved)
    def _():
        for target in (mine, away):
            pl.semaphore_signal(
                barrier, inc=1, device_id={"face": target}, device_id_type=pl.DeviceIdType.MESH
            )
    loads = [pltpu.make_async_copy(states, states_in, load.at[0])]
    loads += [
        pltpu.make_async_copy(src, dst, load.at[2 + n])
        for n, (src, dst) in enumerate(zip(hbm_weights, vmem_weights))
    ]
    loads.append(pltpu.make_async_copy(gru_state, gru_in, load.at[1]))
    start(loads)

    lane = lax.broadcasted_iota(jnp.int32, (1, 256), 1)
    for row, p in ((0, NORTH), (2, SOUTH)):
        info_out[row : row + 1] = far_index(lane, nbr, orient, SIDE0, p)
        info_out[row + 1 : row + 2] = far_index(lane, nbr, orient, SIDE1, p)
    info_out[4:5] = near_index(lane, nbr, orient, SIDE0)
    info_out[5:6] = near_index(lane, nbr, orient, SIDE1)
    info_out[6:8] = jnp.zeros((2, 256), jnp.int32)
    weather[...] = jnp.zeros_like(weather)
    loads[0].wait()
    weather[:FIELDS] = states_in[:, 0, :]
    w_out[0] = weather[...].astype(BF16)
    pl.semaphore_wait(barrier, jnp.where(moved, 6, 4))

    @pl.when(moved)
    def _():
        state_copy().start()
        own_info_copy().start()

    start(weather_copies(0, first_targets))
    start(info_copies())

    pad0[...] = jnp.zeros_like(pad0)
    halo0[...] = jnp.zeros_like(halo0)
    for copy in loads[1:]:
        copy.wait()
    embed[...] = jnp.zeros_like(embed)
    embed[:FIELDS] = embed_w[...].astype(F32)
    taps_ef[...] = spread_taps(ef_depth[...])

    @pl.when(moved)
    def _():
        gru_copy().start()
        state_copy().wait()
        own_info_copy().wait()
        weather[:FIELDS] = states_moved[:, 0, :]

    @pl.when(jnp.logical_not(moved))
    def _():
        info_moved[...] = info_out[...]

    near0[...] = one_hot(info_moved[4:5], CELLS0, 0).T.astype(BF16)
    for way in range(2):
        wanted = info_moved[2 * way : 2 * way + 1, :128]
        own_far[way] = one_hot(wanted, CELLS0, 0).T[:RIM0].astype(BF16)

    def prepare_rest():
        pad1[...] = jnp.zeros_like(pad1)
        halo1[...] = jnp.zeros_like(halo1)
        near1[...] = one_hot(info_moved[5:6, :128], CELLS1, 0).T.astype(BF16)
        taps_df[...] = spread_taps(df_depth[...])
        taps_ec[...] = spread_taps(ec_depth[...])
        taps_dc[...] = spread_taps(dc_depth[...])
        for g in range(3):
            wide = gru_w[g].astype(F32)
            gru_a[g] = wide[:, :C1].astype(BF16)
            gru_b[g] = wide[:, C1:].astype(BF16)
        wide = combine_w[...].astype(F32)
        comb_b[...] = wide[C0:].astype(BF16)
        lift_w[...] = dot_nn(up_w[...], wide[:C0].astype(BF16)).astype(BF16)

        def coarse_of(cell):
            tile = lax.shift_right_logical(cell, 8)
            row = lax.shift_right_logical(cell, 5) & 7
            return tile * 64 + row * 8 + (lax.shift_right_logical(cell, 1) & 7)

        cell = lax.broadcasted_iota(jnp.int32, (CELLS0, 1), 0)
        one = one_hot(coarse_of(cell), CELLS1, 1).astype(BF16)
        grow[:, :CELLS1] = one
        grow[:, CELLS1:] = one
        cell = lax.broadcasted_iota(jnp.int32, (1, CELLS0), 1)
        gather[:CELLS1] = (0.25 * one_hot(coarse_of(cell), CELLS1, 0)).astype(BF16)

        @pl.when(moved)
        def _():
            gru_copy().wait()
            gru_in[...] = gru_moved[...]

        state = jnp.concatenate(
            [gru_in[...].reshape(C1, CELLS1), jnp.zeros((256 - C1, CELLS1), F32)], 0
        )
        carried[...] = state.T[:, :C1]

    def prepare_sends():
        for way in range(2):
            wanted = info_in[1 - way, 2 * way : 2 * way + 2, :128]
            rows = slice(way * RIM0, (way + 1) * RIM0)
            far0[rows] = one_hot(wanted[0:1], CELLS0, 0).T[:RIM0].astype(BF16)
            rows = slice(way * RIM1, (way + 1) * RIM1)
            far1[rows] = one_hot(wanted[1:2], CELLS1, 0).T[:RIM1].astype(BF16)
        gather[CELLS1:] = dot_nn(far1[...], gather[:CELLS1]).astype(BF16)
        one = dot_nn(far0[...], grow[:, :CELLS1]).astype(BF16)
        far_grow[:, :CELLS1] = one
        far_grow[:, CELLS1:] = one

    def fill0(r):
        pad0[:, 3 : 3 + SIDE0, 8:24, :] = r.astype(F32).reshape(TILES, SIDE0, SIDE0, C0)
        sides = dot_nn(near0[...], r).reshape(TILES, SIDE0, 8, C0)
        pad0[:, 3 : 3 + SIDE0, 0:8, :] = sides
        pad0[:, 3 : 3 + SIDE0, 24:32, :] = sides

    def fill1(r):
        pad1[:, 3 : 3 + SIDE1, 8:16, :] = r.astype(F32).reshape(TILES, SIDE1, SIDE1, C1)
        sides = dot_nn(near1[...], r).reshape(TILES, SIDE1, 8, C1)
        pad1[:, 3 : 3 + SIDE1, 0:8, :] = sides
        pad1[:, 3 : 3 + SIDE1, 16:24, :] = sides

    def fine_block_inner(taps, expand, shrink, out):
        def body(tile, _):
            for half in range(2):
                total = conv_tile(pad0, tile, SIDE0, 8 + 8 * half, taps)
                y0[tile, :, 8 * half : 8 * half + 8, :] = total
            y = y0[tile, 3:13].reshape(10 * SIDE0, C0)
            r = pad0[tile, 6:16, 8:24, :].reshape(10 * SIDE0, C0)
            out[tile, 3:13] = finish(y, r, expand[...], shrink[...]).reshape(10, SIDE0, C0)
            return 0

        lax.fori_loop(0, TILES, body, 0)
        for tile in range(TILES):
            for side, top in ((0, 3), (1, 16)):
                edge_r[tile, side] = pad0[tile, top : top + 3, 8:24, :]

    def fine_block_outer(taps, expand, shrink, out):
        def body(tile, _):
            for side, top in ((0, 0), (1, 13)):
                for half in range(2):
                    columns = slice(8 * half, 8 * half + 8)
                    rows = [y0[tile, top + o, columns, :] for o in range(3)]
                    rows = conv_halo(halo0, side, tile, 8 + 8 * half, taps, rows)
                    for o in range(3):
                        edge_y[tile, side, o, columns, :] = rows[o]
            return 0

        lax.fori_loop(0, TILES, body, 0)
        y = edge_y[...].reshape(2 * RIM0, C0)
        r = edge_r[...].reshape(2 * RIM0, C0)
        done = finish(y, r, expand[...], shrink[...]).reshape(TILES, 2, 3, SIDE0, C0)
        for tile in range(TILES):
            out[tile, 0:3] = done[tile, 0]
            out[tile, 13:16] = done[tile, 1]

    def coarse_block(r, slot, taps, expand, shrink, meanwhile):
        copies = pair(c_out, c_in, c_send, c_recv, slot)
        start(copies)
        fill1(r)

        def body(tile, _):
            y1[tile] = conv_tile(pad1, tile, SIDE1, 8, taps)
            return 0

        lax.fori_loop(0, TILES, body, 0)
        meanwhile()
        wait(copies)
        for way in range(2):
            arrived = c_in[slot, way].astype(F32).reshape(TILES, 3, SIDE1, C1)
            halo1[way, :, :, 8:16, :] = arrived

        def edge(tile, _):
            for side, top in ((0, 0), (1, 5)):
                rows = [y1[tile, top + o] for o in range(3)]
                rows = conv_halo(halo1, side, tile, 8, taps, rows)
                for o in range(3):
                    y1[tile, top + o] = rows[o]
            return 0

        lax.fori_loop(0, TILES, edge, 0)
        y = y1[...].reshape(CELLS1, C1)
        return finish(y, r.astype(F32), expand[...], shrink[...])

    def step_body(step, _):
        fields = weather[...].astype(BF16).astype(F32).T.astype(BF16)
        lift = embed[...].astype(BF16)
        fill0(dot_nn(fields, lift).astype(BF16))
        fine_block_inner(taps_ef, ef_expand, ef_shrink, skip)

        @pl.when(step == 0)
        def _():
            prepare_rest()
            wait(info_copies())
            prepare_sends()

        wait(weather_copies(step, (after, before)))
        for way in range(2):
            rim = dot_nt(own_far[way], w_in[step, way]).astype(BF16)
            rim = dot_nn(rim, lift).astype(BF16).astype(F32)
            halo0[way, :, :, 8:24, :] = rim.reshape(TILES, 3, SIDE0, C0)
        fine_block_outer(taps_ef, ef_expand, ef_shrink, skip)

        coarse = dot_nn(gather[...], skip[...].reshape(CELLS0, C0)).astype(BF16)
        coarse = dot_nt(coarse, down_w[...]).astype(BF16)
        for way in range(2):
            top = CELLS1 + way * RIM1
            c_out[2 * step, way] = coarse[top : top + RIM1]

        def after_skip():
            kept = skip[...].reshape(CELLS0, C0)
            part[...] = dot_nn(kept, comb_b[...])
            far_part[...] = dot_nn(dot_nn(far0[...], kept).astype(BF16), comb_b[...])
            held = carried[...].astype(BF16)
            for g in range(2):
                held_gates[g] = dot_nt(held, gru_b[g])

        coarse = coarse_block(
            coarse[:CELLS1], 2 * step, taps_ec, ec_expand, ec_shrink, after_skip
        )

        old = carried[...]
        update = jax.nn.sigmoid(dot_nt(coarse, gru_a[0]) + held_gates[0])
        reset = jax.nn.sigmoid(dot_nt(coarse, gru_a[1]) + held_gates[1])
        gated = (reset * old).astype(BF16)
        candidate = jnp.tanh(dot_nt(coarse, gru_a[2]) + dot_nt(gated, gru_b[2]))
        new = (1.0 - update) * old + update * candidate
        carried[...] = new

        new = new.astype(BF16)
        wanted = dot_nn(far1[...], new).astype(BF16)
        for way in range(2):
            c_out[2 * step + 1, way] = wanted[way * RIM1 : (way + 1) * RIM1]

        def after_update():
            @pl.when(step == STEPS - 1)
            def _():
                last = jnp.concatenate([carried[...], jnp.zeros((CELLS1, 256 - C1), F32)], 1)
                last = last.T[:C1]

                @pl.when(moved)
                def _():
                    gru_out[...] = last
                    gru_result_copy().start()

                @pl.when(jnp.logical_not(moved))
                def _():
                    gru_final[0] = last

        decoded = coarse_block(
            new, 2 * step + 1, taps_dc, dc_expand, dc_shrink, after_update
        )

        lifted = halves(dot_nn(decoded, lift_w[...]))
        wanted = (dot_nn(far_grow[...], lifted) + far_part[...]).astype(BF16)
        for way in range(2):
            f_out[step, way] = wanted[way * RIM0 : (way + 1) * RIM0]
        copies = pair(f_out, f_in, f_send, f_recv, step)
        start(copies)
        fill0((dot_nn(grow[...], lifted) + part[...]).astype(BF16))
        fine_block_inner(taps_df, df_expand, df_shrink, merged)
        wait(copies)
        for way in range(2):
            arrived = f_in[step, way].astype(F32).reshape(TILES, 3, SIDE0, C0)
            halo0[way, :, :, 8:24, :] = arrived
        fine_block_outer(taps_df, df_expand, df_shrink, merged)

        change = dot_nt(head_w[...], merged[...].reshape(CELLS0, C0))
        now = weather[:FIELDS] + change
        weather[:FIELDS] = now

        @pl.when(step < STEPS - 1)
        def _():
            w_out[step + 1] = weather[...].astype(BF16)
            start(weather_copies(step + 1, (after, before)))

        @pl.when(moved)
        def _():
            result_out[step] = weather[...]
            result_copy(step).start()

        @pl.when(jnp.logical_not(moved))
        def _():
            forecast[step, 0] = now

        return 0

    lax.fori_loop(0, STEPS, step_body, 0)

    @pl.when(moved)
    def _():
        gru_result_copy().wait()
        gru_final[0] = gru_back[...]
        for step in range(STEPS):
            result_copy(step).wait()
            forecast[step, 0] = result_in[step, :FIELDS]


def local(states, gru_state, neighbours, orient, *weights):
    (
        embed_w, ef_depth, ef_expand, ef_shrink, down_w, ec_depth, ec_expand, ec_shrink,
        gru_w, dc_depth, dc_expand, dc_shrink, up_w, combine_w, df_depth, df_expand,
        df_shrink, head_w,
    ) = weights
    weights = (
        embed_w.T, ef_depth.T, ef_expand.T, ef_shrink, down_w, ec_depth.T, ec_expand.T, ec_shrink,
        gru_w, dc_depth.T, dc_expand.T, dc_shrink, up_w.T, combine_w.T, df_depth.T, df_expand.T,
        df_shrink, head_w,
    )
    hbm = pl.BlockSpec(memory_space=pltpu.HBM)
    smem = pl.BlockSpec(memory_space=pltpu.SMEM)
    scratch = [pltpu.VMEM(w.shape, w.dtype) for w in weights]
    scratch += [
        pltpu.VMEM((FIELDS, 1, CELLS0), F32),
        pltpu.VMEM((C1, 1, CELLS1), F32),
        pltpu.VMEM((FIELDS, 1, CELLS0), F32),
        pltpu.VMEM((C1, 1, CELLS1), F32),
        pltpu.VMEM((8, 256), jnp.int32),
        pltpu.VMEM((STEPS, ROWS, CELLS0), F32),
        pltpu.VMEM((STEPS, ROWS, CELLS0), F32),
        pltpu.VMEM((C1, CELLS1), F32),
        pltpu.VMEM((C1, CELLS1), F32),
        pltpu.VMEM((ROWS, CELLS0), F32),
        pltpu.VMEM((CELLS1, C1), F32),
        pltpu.VMEM((ROWS, C0), F32),
        pltpu.VMEM((3, C1, C1), BF16),
        pltpu.VMEM((3, C1, C1), BF16),
        pltpu.VMEM((C1, C0), BF16),
        pltpu.VMEM((C0, C0), BF16),
        pltpu.VMEM((49, 8, C0), F32),
        pltpu.VMEM((49, 8, C0), F32),
        pltpu.VMEM((49, 8, C1), F32),
        pltpu.VMEM((49, 8, C1), F32),
        pltpu.VMEM((TILES * SIDE0 * 8, CELLS0), BF16),
        pltpu.VMEM((TILES * SIDE1 * 8, CELLS1), BF16),
        pltpu.VMEM((2, RIM0, CELLS0), BF16),
        pltpu.VMEM((2 * RIM1, CELLS1), BF16),
        pltpu.VMEM((2 * RIM0, CELLS0), BF16),
        pltpu.VMEM((CELLS0, 2 * CELLS1), BF16),
        pltpu.VMEM((CELLS1 + 2 * RIM1, CELLS0), BF16),
        pltpu.VMEM((2 * RIM0, 2 * CELLS1), BF16),
        pltpu.VMEM((TILES, SIDE0 + 6, 32, C0), F32),
        pltpu.VMEM((TILES, SIDE1 + 6, 24, C1), F32),
        pltpu.VMEM((2, TILES, 3, 32, C0), F32),
        pltpu.VMEM((2, TILES, 3, 24, C1), F32),
        pltpu.VMEM((TILES, SIDE0, SIDE0, C0), F32),
        pltpu.VMEM((TILES, SIDE1, SIDE1, C1), F32),
        pltpu.VMEM((TILES, 2, 3, SIDE0, C0), F32),
        pltpu.VMEM((TILES, 2, 3, SIDE0, C0), F32),
        pltpu.VMEM((TILES, SIDE0, SIDE0, C0), BF16),
        pltpu.VMEM((TILES, SIDE0, SIDE0, C0), BF16),
        pltpu.VMEM((CELLS0, C0), F32),
        pltpu.VMEM((2 * RIM0, C0), F32),
        pltpu.VMEM((2, CELLS1, C1), F32),
        pltpu.VMEM((8, 256), jnp.int32),
        pltpu.VMEM((2, 8, 256), jnp.int32),
        pltpu.VMEM((STEPS, ROWS, CELLS0), BF16),
        pltpu.VMEM((STEPS, 2, ROWS, CELLS0), BF16),
        pltpu.VMEM((STEPS, 2, RIM0, C0), BF16),
        pltpu.VMEM((STEPS, 2, RIM0, C0), BF16),
        pltpu.VMEM((2 * STEPS, 2, RIM1, C1), BF16),
        pltpu.VMEM((2 * STEPS, 2, RIM1, C1), BF16),
        pltpu.SemaphoreType.DMA((2 + WEIGHTS,)),
        pltpu.SemaphoreType.DMA((4,)),
        pltpu.SemaphoreType.DMA((4,)),
        pltpu.SemaphoreType.DMA((STEPS,)),
        pltpu.SemaphoreType.DMA((STEPS,)),
        pltpu.SemaphoreType.DMA((2,)),
        pltpu.SemaphoreType.DMA((2,)),
        pltpu.SemaphoreType.DMA((STEPS, 2)),
        pltpu.SemaphoreType.DMA((STEPS, 2)),
        pltpu.SemaphoreType.DMA((STEPS, 2)),
        pltpu.SemaphoreType.DMA((STEPS, 2)),
        pltpu.SemaphoreType.DMA((2 * STEPS, 2)),
        pltpu.SemaphoreType.DMA((2 * STEPS, 2)),
    ]
    return pl.pallas_call(
        kernel,
        out_shape=(
            jax.ShapeDtypeStruct((STEPS, 1, FIELDS, CELLS0), F32),
            jax.ShapeDtypeStruct((1, C1, CELLS1), F32),
        ),
        in_specs=[hbm, hbm, smem, smem] + [hbm] * len(weights),
        out_specs=(pl.BlockSpec(memory_space=pltpu.VMEM),) * 2,
        scratch_shapes=scratch,
        compiler_params=pltpu.CompilerParams(
            collective_id=0, has_side_effects=True, vmem_limit_bytes=56 * 1024 * 1024
        ),
    )(states.transpose(1, 0, 2), gru_state.transpose(1, 0, 2), neighbours, orient, *weights)


def solution(mesh):
    in_specs = (
        P("segment", None, "face"),
        P("segment", None, "face"),
        P("face", None),
        P("face", None),
    ) + (P(),) * 18
    out_specs = (P(None, "segment", None, "face"), P("segment", None, "face"))
    return jax.shard_map(local, mesh=mesh, in_specs=in_specs, out_specs=out_specs, check_vma=False)
```

```python
import jax
import jax.numpy as jnp
from jax import lax
from jax.experimental import pallas as pl
from jax.experimental.pallas import tpu as pltpu
from jax.sharding import PartitionSpec as P

FIELDS = 9
C0 = 90
C1 = 180
SIDE0 = 16
SIDE1 = 8
TILES = 2
STEPS = 2
CELLS0 = TILES * SIDE0 * SIDE0
CELLS1 = TILES * SIDE1 * SIDE1
RIM0 = TILES * 3 * SIDE0
RIM1 = TILES * 3 * SIDE1
ROWS = 16
F32, BF16 = jnp.float32, jnp.bfloat16
NORTH, EAST, SOUTH, WEST = range(4)
ROW = 16


def dot_nt(a, b):
    return lax.dot_general(a, b, (((1,), (1,)), ((), ())), preferred_element_type=F32)


def dot_nn(a, b):
    return jnp.dot(a, b, preferred_element_type=F32)


def one_hot(index, cells, axis):
    shape = (index.shape[0], cells) if axis == 1 else (cells, index.shape[1])
    hit = lax.broadcasted_iota(jnp.int32, shape, axis) == index
    return jnp.where(hit, 1.0, 0.0)


def rim_line(nbr, orient, tile, side, p):
    o = orient[tile, p]
    from_side = lax.shift_right_logical(o, 1)
    per_depth = jnp.where(
        from_side == 0, side, jnp.where(from_side == 1, -1, jnp.where(from_side == 2, -side, 1))
    )
    base = jnp.where(from_side == 1, side - 1, jnp.where(from_side == 2, side * (side - 1), 0))
    per_step = jnp.where((from_side & 1) == 0, 1, side)
    turned = (o & 1) == 1
    base = base + jnp.where(turned, per_step * (side - 1), 0)
    per_step = jnp.where(turned, -per_step, per_step)
    return base + (nbr[tile, p] & 1) * side * side, per_depth, per_step


def far_index(m, nbr, orient, side, p):
    index = jnp.full(m.shape, -1, jnp.int32)
    for tile in range(TILES):
        base, per_depth, per_step = rim_line(nbr, orient, tile, side, p)
        local = m - tile * 3 * side
        row = jnp.where(local >= 2 * side, 2, jnp.where(local >= side, 1, 0))
        depth = 2 - row if p == NORTH else row
        value = base + per_depth * depth + per_step * (local - row * side)
        index = jnp.where((local >= 0) & (local < 3 * side), value, index)
    return index


def near_index(m, nbr, orient, side):
    index = jnp.full(m.shape, -1, jnp.int32)
    for tile in range(TILES):
        base_e, depth_e, step_e = rim_line(nbr, orient, tile, side, EAST)
        base_w, depth_w, step_w = rim_line(nbr, orient, tile, side, WEST)
        local = m - tile * side * 8
        row, place = lax.shift_right_arithmetic(local, 3), local & 7
        east = base_e + depth_e * place + step_e * row
        west = base_w + depth_w * (7 - place) + step_w * row
        value = jnp.where(place < 3, east, jnp.where(place >= 5, west, -1))
        index = jnp.where((local >= 0) & (local < 8 * side), value, index)
    return index


def host_of(segment, block, size):
    core, odd = segment & 1, block & 1
    face = block - odd + core
    last = lax.rem(block, ROW) == ROW - 1
    return segment - core + odd, jnp.where(last, lax.rem(face + ROW, size), face)


def block_of(segment, face, size):
    core, odd = segment & 1, face & 1
    block = face - odd + core
    last = lax.rem(block, ROW) == ROW - 1
    return segment - core + odd, jnp.where(last, lax.rem(block + size - ROW, size), block)


def spread_taps(weight):
    return jnp.broadcast_to(weight.astype(F32)[:, None, :], (49, 8, weight.shape[1]))


def halves(x):
    high = x.astype(BF16)
    return jnp.concatenate([high, (x - high.astype(F32)).astype(BF16)], 0)


def normalise(y, channels):
    centred = y - jnp.sum(y, 1, keepdims=True) * (1.0 / channels)
    var = jnp.sum(centred * centred, 1, keepdims=True) * (1.0 / channels)
    return (centred * lax.rsqrt(var + 1e-6)).astype(BF16)


def gelu(x):
    return (0.5 * x) * (1.0 + lax.erf(x * 0.7071067811865476))


def finish(y, r, expand, shrink):
    normed = normalise(y, y.shape[1])
    expanded = gelu(dot_nn(normed, expand)).astype(BF16)
    return (r + dot_nt(expanded, shrink)).astype(BF16)


def conv_tile(pad, tile, rows, first, taps):
    total = None
    for q in range(7):
        x = pad[tile, :, first + q - 3 : first + q + 5, :]
        for u in range(7):
            term = taps[7 * u + q][None] * x[u : u + rows]
            total = term if total is None else total + term
    return total


def conv_halo(halo, side, tile, first, taps, rows):
    rows = list(rows)
    for q in range(7):
        for h in range(3):
            x = halo[side, tile, h, first + q - 3 : first + q + 5, :]
            for o in range(3):
                u = h - o if side == 0 else 6 + h - o
                if 0 <= u <= 6:
                    rows[o] = rows[o] + taps[7 * u + q] * x
    return rows


WEIGHTS = 18


def kernel(
    states, gru_state, nbr, orient, *refs,
):
    hbm_weights, refs = refs[:WEIGHTS], refs[WEIGHTS:]
    forecast, gru_final = refs[:2]
    (
        embed_w, ef_depth, ef_expand, ef_shrink, down_w, ec_depth, ec_expand, ec_shrink,
        gru_w, dc_depth, dc_expand, dc_shrink, up_w, combine_w, df_depth, df_expand,
        df_shrink, head_w,
    ) = vmem_weights = refs[2 : 2 + WEIGHTS]
    (
        states_in, gru_in, states_moved, gru_moved, info_moved,
        result_out, result_in, gru_out, gru_back,
        weather, carried, embed, gru_a, gru_b, lift_w, comb_b,
        taps_ef, taps_df, taps_ec, taps_dc,
        near0, near1, own_far, far1, far0, grow, gather, far_grow,
        pad0, pad1, halo0, halo1, y0, y1, edge_y, edge_r, skip, merged,
        part, far_part, held_gates,
        info_out, info_in, w_out, w_in, f_out, f_in, c_out, c_in,
        load,
        m_send, m_recv, r_send, r_recv, info_send, info_recv, w_send, w_recv, f_send, f_recv, c_send, c_recv,
    ) = refs[2 + WEIGHTS :]
    size = lax.axis_size("face")
    here = lax.axis_index("segment"), lax.axis_index("face")
    mine = block_of(*here, size)
    away = host_of(*here, size)
    moved = (away[0] != here[0]) | (away[1] != here[1])

    def beside(place, step):
        return place[0], lax.rem(place[1] + step + size, size)

    home_after, home_before = beside(mine, 1), beside(mine, -1)
    after, before = host_of(*home_after, size), host_of(*home_before, size)
    first_targets = host_of(*beside(here, 1), size), host_of(*beside(here, -1), size)

    def greet(target):
        pl.semaphore_signal(
            barrier, inc=1, device_id={"segment": target[0], "face": target[1]},
            device_id_type=pl.DeviceIdType.MESH,
        )

    def remote(src, dst, send, recv, target):
        return pltpu.make_async_remote_copy(
            src_ref=src, dst_ref=dst, send_sem=send, recv_sem=recv,
            device_id={"segment": target[0], "face": target[1]},
            device_id_type=pl.DeviceIdType.MESH,
        )

    def pair(out, into, send, recv, slot):
        return [
            remote(out.at[slot, w], into.at[slot, w], send.at[slot, w], recv.at[slot, w], target)
            for w, target in enumerate((after, before))
        ]

    def info_copies():
        return [
            remote(info_out, info_in.at[w], info_send.at[w], info_recv.at[w], target)
            for w, target in enumerate(first_targets)
        ]

    def weather_copies(step, targets):
        return [
            remote(w_out.at[step], w_in.at[step, w], w_send.at[step, w], w_recv.at[step, w], target)
            for w, target in enumerate(targets)
        ]

    def state_copy():
        return remote(states_in, states_moved, m_send.at[0], m_recv.at[0], away)

    def own_info_copy():
        return remote(info_out, info_moved, m_send.at[1], m_recv.at[1], away)

    def gru_copy():
        return remote(gru_in, gru_moved, m_send.at[2], m_recv.at[2], away)

    def result_copy(step):
        return remote(
            result_out.at[step], result_in.at[step], r_send.at[step], r_recv.at[step], mine
        )

    def gru_result_copy():
        return remote(gru_out, gru_back, m_send.at[3], m_recv.at[3], mine)

    def start(copies):
        for copy in copies:
            copy.start()

    def wait(copies):
        for copy in copies:
            copy.wait()

    barrier = pltpu.get_barrier_semaphore()
    for target in (home_after, home_before, after, before):
        greet(target)

    @pl.when(moved)
    def _():
        greet(mine)
        greet(away)

    loads = [pltpu.make_async_copy(states, states_in, load.at[0])]
    loads += [
        pltpu.make_async_copy(src, dst, load.at[2 + n])
        for n, (src, dst) in enumerate(zip(hbm_weights, vmem_weights))
    ]
    loads.append(pltpu.make_async_copy(gru_state, gru_in, load.at[1]))
    start(loads)

    lane = lax.broadcasted_iota(jnp.int32, (1, 256), 1)
    for row, p in ((0, NORTH), (2, SOUTH)):
        info_out[row : row + 1] = far_index(lane, nbr, orient, SIDE0, p)
        info_out[row + 1 : row + 2] = far_index(lane, nbr, orient, SIDE1, p)
    info_out[4:5] = near_index(lane, nbr, orient, SIDE0)
    info_out[5:6] = near_index(lane, nbr, orient, SIDE1)
    info_out[6:8] = jnp.zeros((2, 256), jnp.int32)
    weather[...] = jnp.zeros_like(weather)
    loads[0].wait()
    weather[:FIELDS] = states_in[:, 0, :]
    w_out[0] = weather[...].astype(BF16)
    pl.semaphore_wait(barrier, jnp.where(moved, 6, 4))

    @pl.when(moved)
    def _():
        state_copy().start()
        own_info_copy().start()

    start(weather_copies(0, first_targets))
    start(info_copies())

    pad0[...] = jnp.zeros_like(pad0)
    halo0[...] = jnp.zeros_like(halo0)
    for copy in loads[1:]:
        copy.wait()
    embed[...] = jnp.zeros_like(embed)
    embed[:FIELDS] = embed_w[...].astype(F32)
    taps_ef[...] = spread_taps(ef_depth[...])

    @pl.when(moved)
    def _():
        gru_copy().start()
        state_copy().wait()
        own_info_copy().wait()
        weather[:FIELDS] = states_moved[:, 0, :]

    @pl.when(jnp.logical_not(moved))
    def _():
        info_moved[...] = info_out[...]

    near0[...] = one_hot(info_moved[4:5], CELLS0, 0).T.astype(BF16)
    for way in range(2):
        wanted = info_moved[2 * way : 2 * way + 1, :128]
        own_far[way] = one_hot(wanted, CELLS0, 0).T[:RIM0].astype(BF16)

    def prepare_rest():
        pad1[...] = jnp.zeros_like(pad1)
        halo1[...] = jnp.zeros_like(halo1)
        near1[...] = one_hot(info_moved[5:6, :128], CELLS1, 0).T.astype(BF16)
        taps_df[...] = spread_taps(df_depth[...])
        taps_ec[...] = spread_taps(ec_depth[...])
        taps_dc[...] = spread_taps(dc_depth[...])
        for g in range(3):
            wide = gru_w[g].astype(F32)
            gru_a[g] = wide[:, :C1].astype(BF16)
            gru_b[g] = wide[:, C1:].astype(BF16)
        wide = combine_w[...].astype(F32)
        comb_b[...] = wide[C0:].astype(BF16)
        lift_w[...] = dot_nn(up_w[...], wide[:C0].astype(BF16)).astype(BF16)

        def coarse_of(cell):
            tile = lax.shift_right_logical(cell, 8)
            row = lax.shift_right_logical(cell, 5) & 7
            return tile * 64 + row * 8 + (lax.shift_right_logical(cell, 1) & 7)

        cell = lax.broadcasted_iota(jnp.int32, (CELLS0, 1), 0)
        one = one_hot(coarse_of(cell), CELLS1, 1).astype(BF16)
        grow[:, :CELLS1] = one
        grow[:, CELLS1:] = one
        cell = lax.broadcasted_iota(jnp.int32, (1, CELLS0), 1)
        gather[:CELLS1] = (0.25 * one_hot(coarse_of(cell), CELLS1, 0)).astype(BF16)

        @pl.when(moved)
        def _():
            gru_copy().wait()
            gru_in[...] = gru_moved[...]

        state = jnp.concatenate(
            [gru_in[...].reshape(C1, CELLS1), jnp.zeros((256 - C1, CELLS1), F32)], 0
        )
        carried[...] = state.T[:, :C1]

    def prepare_sends():
        for way in range(2):
            wanted = info_in[1 - way, 2 * way : 2 * way + 2, :128]
            rows = slice(way * RIM0, (way + 1) * RIM0)
            far0[rows] = one_hot(wanted[0:1], CELLS0, 0).T[:RIM0].astype(BF16)
            rows = slice(way * RIM1, (way + 1) * RIM1)
            far1[rows] = one_hot(wanted[1:2], CELLS1, 0).T[:RIM1].astype(BF16)
        gather[CELLS1:] = dot_nn(far1[...], gather[:CELLS1]).astype(BF16)
        one = dot_nn(far0[...], grow[:, :CELLS1]).astype(BF16)
        far_grow[:, :CELLS1] = one
        far_grow[:, CELLS1:] = one

    def fill0(r):
        pad0[:, 3 : 3 + SIDE0, 8:24, :] = r.astype(F32).reshape(TILES, SIDE0, SIDE0, C0)
        sides = dot_nn(near0[...], r).reshape(TILES, SIDE0, 8, C0)
        pad0[:, 3 : 3 + SIDE0, 0:8, :] = sides
        pad0[:, 3 : 3 + SIDE0, 24:32, :] = sides

    def fill1(r):
        pad1[:, 3 : 3 + SIDE1, 8:16, :] = r.astype(F32).reshape(TILES, SIDE1, SIDE1, C1)
        sides = dot_nn(near1[...], r).reshape(TILES, SIDE1, 8, C1)
        pad1[:, 3 : 3 + SIDE1, 0:8, :] = sides
        pad1[:, 3 : 3 + SIDE1, 16:24, :] = sides

    def fine_block_inner(taps, expand, shrink, out):
        def body(tile, _):
            for half in range(2):
                total = conv_tile(pad0, tile, SIDE0, 8 + 8 * half, taps)
                y0[tile, :, 8 * half : 8 * half + 8, :] = total
            y = y0[tile, 3:13].reshape(10 * SIDE0, C0)
            r = pad0[tile, 6:16, 8:24, :].reshape(10 * SIDE0, C0)
            out[tile, 3:13] = finish(y, r, expand[...], shrink[...]).reshape(10, SIDE0, C0)
            return 0

        lax.fori_loop(0, TILES, body, 0)
        for tile in range(TILES):
            for side, top in ((0, 3), (1, 16)):
                edge_r[tile, side] = pad0[tile, top : top + 3, 8:24, :]

    def fine_block_outer(taps, expand, shrink, out):
        def body(tile, _):
            for side, top in ((0, 0), (1, 13)):
                for half in range(2):
                    columns = slice(8 * half, 8 * half + 8)
                    rows = [y0[tile, top + o, columns, :] for o in range(3)]
                    rows = conv_halo(halo0, side, tile, 8 + 8 * half, taps, rows)
                    for o in range(3):
                        edge_y[tile, side, o, columns, :] = rows[o]
            return 0

        lax.fori_loop(0, TILES, body, 0)
        y = edge_y[...].reshape(2 * RIM0, C0)
        r = edge_r[...].reshape(2 * RIM0, C0)
        done = finish(y, r, expand[...], shrink[...]).reshape(TILES, 2, 3, SIDE0, C0)
        for tile in range(TILES):
            out[tile, 0:3] = done[tile, 0]
            out[tile, 13:16] = done[tile, 1]

    def coarse_block(r, slot, taps, expand, shrink, meanwhile):
        copies = pair(c_out, c_in, c_send, c_recv, slot)
        start(copies)
        fill1(r)

        def body(tile, _):
            y1[tile] = conv_tile(pad1, tile, SIDE1, 8, taps)
            return 0

        lax.fori_loop(0, TILES, body, 0)
        meanwhile()
        wait(copies)
        for way in range(2):
            arrived = c_in[slot, way].astype(F32).reshape(TILES, 3, SIDE1, C1)
            halo1[way, :, :, 8:16, :] = arrived

        def edge(tile, _):
            for side, top in ((0, 0), (1, 5)):
                rows = [y1[tile, top + o] for o in range(3)]
                rows = conv_halo(halo1, side, tile, 8, taps, rows)
                for o in range(3):
                    y1[tile, top + o] = rows[o]
            return 0

        lax.fori_loop(0, TILES, edge, 0)
        y = y1[...].reshape(CELLS1, C1)
        return finish(y, r.astype(F32), expand[...], shrink[...])

    def step_body(step, _):
        fields = weather[...].astype(BF16).astype(F32).T.astype(BF16)
        lift = embed[...].astype(BF16)
        fill0(dot_nn(fields, lift).astype(BF16))
        fine_block_inner(taps_ef, ef_expand, ef_shrink, skip)

        @pl.when(step == 0)
        def _():
            prepare_rest()
            wait(info_copies())
            prepare_sends()

        wait(weather_copies(step, (after, before)))
        for way in range(2):
            rim = dot_nt(own_far[way], w_in[step, way]).astype(BF16)
            rim = dot_nn(rim, lift).astype(BF16).astype(F32)
            halo0[way, :, :, 8:24, :] = rim.reshape(TILES, 3, SIDE0, C0)
        fine_block_outer(taps_ef, ef_expand, ef_shrink, skip)

        coarse = dot_nn(gather[...], skip[...].reshape(CELLS0, C0)).astype(BF16)
        coarse = dot_nt(coarse, down_w[...]).astype(BF16)
        for way in range(2):
            top = CELLS1 + way * RIM1
            c_out[2 * step, way] = coarse[top : top + RIM1]

        def after_skip():
            kept = skip[...].reshape(CELLS0, C0)
            part[...] = dot_nn(kept, comb_b[...])
            far_part[...] = dot_nn(dot_nn(far0[...], kept).astype(BF16), comb_b[...])
            held = carried[...].astype(BF16)
            for g in range(2):
                held_gates[g] = dot_nt(held, gru_b[g])

        coarse = coarse_block(
            coarse[:CELLS1], 2 * step, taps_ec, ec_expand, ec_shrink, after_skip
        )

        old = carried[...]
        update = jax.nn.sigmoid(dot_nt(coarse, gru_a[0]) + held_gates[0])
        reset = jax.nn.sigmoid(dot_nt(coarse, gru_a[1]) + held_gates[1])
        gated = (reset * old).astype(BF16)
        candidate = jnp.tanh(dot_nt(coarse, gru_a[2]) + dot_nt(gated, gru_b[2]))
        new = (1.0 - update) * old + update * candidate
        carried[...] = new

        new = new.astype(BF16)
        wanted = dot_nn(far1[...], new).astype(BF16)
        for way in range(2):
            c_out[2 * step + 1, way] = wanted[way * RIM1 : (way + 1) * RIM1]

        def after_update():
            @pl.when(step == STEPS - 1)
            def _():
                last = jnp.concatenate([carried[...], jnp.zeros((CELLS1, 256 - C1), F32)], 1)
                last = last.T[:C1]

                @pl.when(moved)
                def _():
                    gru_out[...] = last
                    gru_result_copy().start()

                @pl.when(jnp.logical_not(moved))
                def _():
                    gru_final[0] = last

        decoded = coarse_block(
            new, 2 * step + 1, taps_dc, dc_expand, dc_shrink, after_update
        )

        lifted = halves(dot_nn(decoded, lift_w[...]))
        wanted = (dot_nn(far_grow[...], lifted) + far_part[...]).astype(BF16)
        for way in range(2):
            f_out[step, way] = wanted[way * RIM0 : (way + 1) * RIM0]
        copies = pair(f_out, f_in, f_send, f_recv, step)
        start(copies)
        fill0((dot_nn(grow[...], lifted) + part[...]).astype(BF16))
        fine_block_inner(taps_df, df_expand, df_shrink, merged)
        wait(copies)
        for way in range(2):
            arrived = f_in[step, way].astype(F32).reshape(TILES, 3, SIDE0, C0)
            halo0[way, :, :, 8:24, :] = arrived
        fine_block_outer(taps_df, df_expand, df_shrink, merged)

        change = dot_nt(head_w[...], merged[...].reshape(CELLS0, C0))
        now = weather[:FIELDS] + change
        weather[:FIELDS] = now

        @pl.when(step < STEPS - 1)
        def _():
            w_out[step + 1] = weather[...].astype(BF16)
            start(weather_copies(step + 1, (after, before)))

        @pl.when(moved)
        def _():
            result_out[step] = weather[...]
            result_copy(step).start()

        @pl.when(jnp.logical_not(moved))
        def _():
            forecast[step, 0] = now

        return 0

    lax.fori_loop(0, STEPS, step_body, 0)

    @pl.when(moved)
    def _():
        gru_result_copy().wait()
        gru_final[0] = gru_back[...]
        for step in range(STEPS):
            result_copy(step).wait()
            forecast[step, 0] = result_in[step, :FIELDS]


def local(states, gru_state, neighbours, orient, *weights):
    (
        embed_w, ef_depth, ef_expand, ef_shrink, down_w, ec_depth, ec_expand, ec_shrink,
        gru_w, dc_depth, dc_expand, dc_shrink, up_w, combine_w, df_depth, df_expand,
        df_shrink, head_w,
    ) = weights
    weights = (
        embed_w.T, ef_depth.T, ef_expand.T, ef_shrink, down_w, ec_depth.T, ec_expand.T, ec_shrink,
        gru_w, dc_depth.T, dc_expand.T, dc_shrink, up_w.T, combine_w.T, df_depth.T, df_expand.T,
        df_shrink, head_w,
    )
    hbm = pl.BlockSpec(memory_space=pltpu.HBM)
    smem = pl.BlockSpec(memory_space=pltpu.SMEM)
    scratch = [pltpu.VMEM(w.shape, w.dtype) for w in weights]
    scratch += [
        pltpu.VMEM((FIELDS, 1, CELLS0), F32),
        pltpu.VMEM((C1, 1, CELLS1), F32),
        pltpu.VMEM((FIELDS, 1, CELLS0), F32),
        pltpu.VMEM((C1, 1, CELLS1), F32),
        pltpu.VMEM((8, 256), jnp.int32),
        pltpu.VMEM((STEPS, ROWS, CELLS0), F32),
        pltpu.VMEM((STEPS, ROWS, CELLS0), F32),
        pltpu.VMEM((C1, CELLS1), F32),
        pltpu.VMEM((C1, CELLS1), F32),
        pltpu.VMEM((ROWS, CELLS0), F32),
        pltpu.VMEM((CELLS1, C1), F32),
        pltpu.VMEM((ROWS, C0), F32),
        pltpu.VMEM((3, C1, C1), BF16),
        pltpu.VMEM((3, C1, C1), BF16),
        pltpu.VMEM((C1, C0), BF16),
        pltpu.VMEM((C0, C0), BF16),
        pltpu.VMEM((49, 8, C0), F32),
        pltpu.VMEM((49, 8, C0), F32),
        pltpu.VMEM((49, 8, C1), F32),
        pltpu.VMEM((49, 8, C1), F32),
        pltpu.VMEM((TILES * SIDE0 * 8, CELLS0), BF16),
        pltpu.VMEM((TILES * SIDE1 * 8, CELLS1), BF16),
        pltpu.VMEM((2, RIM0, CELLS0), BF16),
        pltpu.VMEM((2 * RIM1, CELLS1), BF16),
        pltpu.VMEM((2 * RIM0, CELLS0), BF16),
        pltpu.VMEM((CELLS0, 2 * CELLS1), BF16),
        pltpu.VMEM((CELLS1 + 2 * RIM1, CELLS0), BF16),
        pltpu.VMEM((2 * RIM0, 2 * CELLS1), BF16),
        pltpu.VMEM((TILES, SIDE0 + 6, 32, C0), F32),
        pltpu.VMEM((TILES, SIDE1 + 6, 24, C1), F32),
        pltpu.VMEM((2, TILES, 3, 32, C0), F32),
        pltpu.VMEM((2, TILES, 3, 24, C1), F32),
        pltpu.VMEM((TILES, SIDE0, SIDE0, C0), F32),
        pltpu.VMEM((TILES, SIDE1, SIDE1, C1), F32),
        pltpu.VMEM((TILES, 2, 3, SIDE0, C0), F32),
        pltpu.VMEM((TILES, 2, 3, SIDE0, C0), F32),
        pltpu.VMEM((TILES, SIDE0, SIDE0, C0), BF16),
        pltpu.VMEM((TILES, SIDE0, SIDE0, C0), BF16),
        pltpu.VMEM((CELLS0, C0), F32),
        pltpu.VMEM((2 * RIM0, C0), F32),
        pltpu.VMEM((2, CELLS1, C1), F32),
        pltpu.VMEM((8, 256), jnp.int32),
        pltpu.VMEM((2, 8, 256), jnp.int32),
        pltpu.VMEM((STEPS, ROWS, CELLS0), BF16),
        pltpu.VMEM((STEPS, 2, ROWS, CELLS0), BF16),
        pltpu.VMEM((STEPS, 2, RIM0, C0), BF16),
        pltpu.VMEM((STEPS, 2, RIM0, C0), BF16),
        pltpu.VMEM((2 * STEPS, 2, RIM1, C1), BF16),
        pltpu.VMEM((2 * STEPS, 2, RIM1, C1), BF16),
        pltpu.SemaphoreType.DMA((2 + WEIGHTS,)),
        pltpu.SemaphoreType.DMA((4,)),
        pltpu.SemaphoreType.DMA((4,)),
        pltpu.SemaphoreType.DMA((STEPS,)),
        pltpu.SemaphoreType.DMA((STEPS,)),
        pltpu.SemaphoreType.DMA((2,)),
        pltpu.SemaphoreType.DMA((2,)),
        pltpu.SemaphoreType.DMA((STEPS, 2)),
        pltpu.SemaphoreType.DMA((STEPS, 2)),
        pltpu.SemaphoreType.DMA((STEPS, 2)),
        pltpu.SemaphoreType.DMA((STEPS, 2)),
        pltpu.SemaphoreType.DMA((2 * STEPS, 2)),
        pltpu.SemaphoreType.DMA((2 * STEPS, 2)),
    ]
    return pl.pallas_call(
        kernel,
        out_shape=(
            jax.ShapeDtypeStruct((STEPS, 1, FIELDS, CELLS0), F32),
            jax.ShapeDtypeStruct((1, C1, CELLS1), F32),
        ),
        in_specs=[hbm, hbm, smem, smem] + [hbm] * len(weights),
        out_specs=(pl.BlockSpec(memory_space=pltpu.VMEM),) * 2,
        scratch_shapes=scratch,
        compiler_params=pltpu.CompilerParams(
            collective_id=0, has_side_effects=True, vmem_limit_bytes=56 * 1024 * 1024
        ),
    )(states.transpose(1, 0, 2), gru_state.transpose(1, 0, 2), neighbours, orient, *weights)


def solution(mesh):
    in_specs = (
        P("segment", None, "face"),
        P("segment", None, "face"),
        P("face", None),
        P("face", None),
    ) + (P(),) * 18
    out_specs = (P(None, "segment", None, "face"), P("segment", None, "face"))
    return jax.shard_map(local, mesh=mesh, in_specs=in_specs, out_specs=out_specs, check_vma=False)
```

```python
import jax
import jax.numpy as jnp
from jax import lax
from jax.experimental import pallas as pl
from jax.experimental.pallas import tpu as pltpu
from jax.sharding import PartitionSpec as P

FIELDS = 9
C0 = 90
C1 = 180
SIDE0 = 16
SIDE1 = 8
TILES = 2
STEPS = 2
CELLS0 = TILES * SIDE0 * SIDE0
CELLS1 = TILES * SIDE1 * SIDE1
RIM0 = TILES * 3 * SIDE0
RIM1 = TILES * 3 * SIDE1
ROWS = 16
F32, BF16 = jnp.float32, jnp.bfloat16
NORTH, EAST, SOUTH, WEST = range(4)
ROW = 16


def dot_nt(a, b):
    return lax.dot_general(a, b, (((1,), (1,)), ((), ())), preferred_element_type=F32)


def dot_nn(a, b):
    return jnp.dot(a, b, preferred_element_type=F32)


def one_hot(index, cells, axis):
    shape = (index.shape[0], cells) if axis == 1 else (cells, index.shape[1])
    hit = lax.broadcasted_iota(jnp.int32, shape, axis) == index
    return jnp.where(hit, 1.0, 0.0)


def rim_line(nbr, orient, tile, side, p):
    o = orient[tile, p]
    from_side = lax.shift_right_logical(o, 1)
    per_depth = jnp.where(
        from_side == 0, side, jnp.where(from_side == 1, -1, jnp.where(from_side == 2, -side, 1))
    )
    base = jnp.where(from_side == 1, side - 1, jnp.where(from_side == 2, side * (side - 1), 0))
    per_step = jnp.where((from_side & 1) == 0, 1, side)
    turned = (o & 1) == 1
    base = base + jnp.where(turned, per_step * (side - 1), 0)
    per_step = jnp.where(turned, -per_step, per_step)
    return base + (nbr[tile, p] & 1) * side * side, per_depth, per_step


def far_index(m, nbr, orient, side, p):
    index = jnp.full(m.shape, -1, jnp.int32)
    for tile in range(TILES):
        base, per_depth, per_step = rim_line(nbr, orient, tile, side, p)
        local = m - tile * 3 * side
        row = jnp.where(local >= 2 * side, 2, jnp.where(local >= side, 1, 0))
        depth = 2 - row if p == NORTH else row
        value = base + per_depth * depth + per_step * (local - row * side)
        index = jnp.where((local >= 0) & (local < 3 * side), value, index)
    return index


def near_index(m, nbr, orient, side):
    index = jnp.full(m.shape, -1, jnp.int32)
    for tile in range(TILES):
        base_e, depth_e, step_e = rim_line(nbr, orient, tile, side, EAST)
        base_w, depth_w, step_w = rim_line(nbr, orient, tile, side, WEST)
        local = m - tile * side * 8
        row, place = lax.shift_right_arithmetic(local, 3), local & 7
        east = base_e + depth_e * place + step_e * row
        west = base_w + depth_w * (7 - place) + step_w * row
        value = jnp.where(place < 3, east, jnp.where(place >= 5, west, -1))
        index = jnp.where((local >= 0) & (local < 8 * side), value, index)
    return index


def host_of(segment, block, size):
    core, odd = segment & 1, block & 1
    face = block - odd + (1 - core)
    last = lax.rem(block, ROW) == ROW - 1
    return segment - core + (1 - odd), jnp.where(last, lax.rem(face + ROW, size), face)


def block_of(segment, face, size):
    core, odd = segment & 1, face & 1
    block = face - odd + (1 - core)
    last = lax.rem(block, ROW) == ROW - 1
    return segment - core + (1 - odd), jnp.where(last, lax.rem(block + size - ROW, size), block)


def spread_taps(weight):
    return jnp.broadcast_to(weight.astype(F32)[:, None, :], (49, 8, weight.shape[1]))


def halves(x):
    high = x.astype(BF16)
    return jnp.concatenate([high, (x - high.astype(F32)).astype(BF16)], 0)


def normalise(y, channels):
    centred = y - jnp.sum(y, 1, keepdims=True) * (1.0 / channels)
    var = jnp.sum(centred * centred, 1, keepdims=True) * (1.0 / channels)
    return (centred * lax.rsqrt(var + 1e-6)).astype(BF16)


def gelu(x):
    return (0.5 * x) * (1.0 + lax.erf(x * 0.7071067811865476))


def finish(y, r, expand, shrink):
    normed = normalise(y, y.shape[1])
    expanded = gelu(dot_nn(normed, expand)).astype(BF16)
    return (r + dot_nt(expanded, shrink)).astype(BF16)


def conv_tile(pad, tile, rows, first, taps):
    total = None
    for q in range(7):
        x = pad[tile, :, first + q - 3 : first + q + 5, :]
        for u in range(7):
            term = taps[7 * u + q][None] * x[u : u + rows]
            total = term if total is None else total + term
    return total


def conv_halo(halo, side, tile, first, taps, rows):
    rows = list(rows)
    for q in range(7):
        for h in range(3):
            x = halo[side, tile, h, first + q - 3 : first + q + 5, :]
            for o in range(3):
                u = h - o if side == 0 else 6 + h - o
                if 0 <= u <= 6:
                    rows[o] = rows[o] + taps[7 * u + q] * x
    return rows


WEIGHTS = 18


def kernel(
    states, gru_state, nbr, orient, *refs,
):
    hbm_weights, refs = refs[:WEIGHTS], refs[WEIGHTS:]
    forecast, gru_final = refs[:2]
    (
        embed_w, ef_depth, ef_expand, ef_shrink, down_w, ec_depth, ec_expand, ec_shrink,
        gru_w, dc_depth, dc_expand, dc_shrink, up_w, combine_w, df_depth, df_expand,
        df_shrink, head_w,
    ) = vmem_weights = refs[2 : 2 + WEIGHTS]
    (
        states_in, gru_in, states_moved, gru_moved, info_moved,
        result_out, result_in, gru_out, gru_back,
        weather, carried, embed, gru_a, gru_b, lift_w, comb_b,
        taps_ef, taps_df, taps_ec, taps_dc,
        near0, near1, own_far, far1, far0, grow, gather, far_grow,
        pad0, pad1, halo0, halo1, y0, y1, edge_y, edge_r, skip, merged,
        part, far_part, held_gates,
        info_out, info_in, w_out, w_in, f_out, f_in, c_out, c_in,
        load,
        m_send, m_recv, r_send, r_recv, info_send, info_recv, w_send, w_recv, f_send, f_recv, c_send, c_recv,
    ) = refs[2 + WEIGHTS :]
    size = lax.axis_size("face")
    here = lax.axis_index("segment"), lax.axis_index("face")
    mine = block_of(*here, size)
    away = host_of(*here, size)
    moved = (away[0] != here[0]) | (away[1] != here[1])

    def beside(place, step):
        return place[0], lax.rem(place[1] + step + size, size)

    home_after, home_before = beside(mine, 1), beside(mine, -1)
    after, before = host_of(*home_after, size), host_of(*home_before, size)
    first_targets = host_of(*beside(here, 1), size), host_of(*beside(here, -1), size)

    def greet(target):
        pl.semaphore_signal(
            barrier, inc=1, device_id={"segment": target[0], "face": target[1]},
            device_id_type=pl.DeviceIdType.MESH,
        )

    def remote(src, dst, send, recv, target):
        return pltpu.make_async_remote_copy(
            src_ref=src, dst_ref=dst, send_sem=send, recv_sem=recv,
            device_id={"segment": target[0], "face": target[1]},
            device_id_type=pl.DeviceIdType.MESH,
        )

    def pair(out, into, send, recv, slot):
        return [
            remote(out.at[slot, w], into.at[slot, w], send.at[slot, w], recv.at[slot, w], target)
            for w, target in enumerate((after, before))
        ]

    def info_copies():
        return [
            remote(info_out, info_in.at[w], info_send.at[w], info_recv.at[w], target)
            for w, target in enumerate(first_targets)
        ]

    def weather_copies(step, targets):
        return [
            remote(w_out.at[step], w_in.at[step, w], w_send.at[step, w], w_recv.at[step, w], target)
            for w, target in enumerate(targets)
        ]

    def state_copy():
        return remote(states_in, states_moved, m_send.at[0], m_recv.at[0], away)

    def own_info_copy():
        return remote(info_out, info_moved, m_send.at[1], m_recv.at[1], away)

    def gru_copy():
        return remote(gru_in, gru_moved, m_send.at[2], m_recv.at[2], away)

    def result_copy(step):
        return remote(
            result_out.at[step], result_in.at[step], r_send.at[step], r_recv.at[step], mine
        )

    def gru_result_copy():
        return remote(gru_out, gru_back, m_send.at[3], m_recv.at[3], mine)

    def start(copies):
        for copy in copies:
            copy.start()

    def wait(copies):
        for copy in copies:
            copy.wait()

    barrier = pltpu.get_barrier_semaphore()
    for target in (home_after, home_before, after, before):
        greet(target)

    @pl.when(moved)
    def _():
        greet(mine)
        greet(away)

    loads = [pltpu.make_async_copy(states, states_in, load.at[0])]
    loads += [
        pltpu.make_async_copy(src, dst, load.at[2 + n])
        for n, (src, dst) in enumerate(zip(hbm_weights, vmem_weights))
    ]
    loads.append(pltpu.make_async_copy(gru_state, gru_in, load.at[1]))
    start(loads)

    lane = lax.broadcasted_iota(jnp.int32, (1, 256), 1)
    for row, p in ((0, NORTH), (2, SOUTH)):
        info_out[row : row + 1] = far_index(lane, nbr, orient, SIDE0, p)
        info_out[row + 1 : row + 2] = far_index(lane, nbr, orient, SIDE1, p)
    info_out[4:5] = near_index(lane, nbr, orient, SIDE0)
    info_out[5:6] = near_index(lane, nbr, orient, SIDE1)
    info_out[6:8] = jnp.zeros((2, 256), jnp.int32)
    weather[...] = jnp.zeros_like(weather)
    loads[0].wait()
    weather[:FIELDS] = states_in[:, 0, :]
    w_out[0] = weather[...].astype(BF16)
    pl.semaphore_wait(barrier, jnp.where(moved, 6, 4))

    @pl.when(moved)
    def _():
        own_info_copy().start()
        state_copy().start()

    start(weather_copies(0, first_targets))
    start(info_copies())

    def coarse_of(cell):
        tile = lax.shift_right_logical(cell, 8)
        row = lax.shift_right_logical(cell, 5) & 7
        return tile * 64 + row * 8 + (lax.shift_right_logical(cell, 1) & 7)

    pad0[...] = jnp.zeros_like(pad0)
    halo0[...] = jnp.zeros_like(halo0)
    pad1[...] = jnp.zeros_like(pad1)
    halo1[...] = jnp.zeros_like(halo1)
    cell = lax.broadcasted_iota(jnp.int32, (CELLS0, 1), 0)
    one = one_hot(coarse_of(cell), CELLS1, 1).astype(BF16)
    grow[:, :CELLS1] = one
    grow[:, CELLS1:] = one
    cell = lax.broadcasted_iota(jnp.int32, (1, CELLS0), 1)
    gather[:CELLS1] = (0.25 * one_hot(coarse_of(cell), CELLS1, 0)).astype(BF16)
    for copy in loads[1:]:
        copy.wait()

    @pl.when(moved)
    def _():
        gru_copy().start()

    embed[...] = jnp.zeros_like(embed)
    embed[:FIELDS] = embed_w[...].astype(F32)
    taps_ef[...] = spread_taps(ef_depth[...])
    taps_df[...] = spread_taps(df_depth[...])
    taps_ec[...] = spread_taps(ec_depth[...])
    taps_dc[...] = spread_taps(dc_depth[...])
    for g in range(3):
        wide = gru_w[g].astype(F32)
        gru_a[g] = wide[:, :C1].astype(BF16)
        gru_b[g] = wide[:, C1:].astype(BF16)
    wide = combine_w[...].astype(F32)
    comb_b[...] = wide[C0:].astype(BF16)
    lift_w[...] = dot_nn(up_w[...], wide[:C0].astype(BF16)).astype(BF16)

    @pl.when(moved)
    def _():
        own_info_copy().wait()

    @pl.when(jnp.logical_not(moved))
    def _():
        info_moved[...] = info_out[...]

    near0[...] = one_hot(info_moved[4:5], CELLS0, 0).T.astype(BF16)
    for way in range(2):
        wanted = info_moved[2 * way : 2 * way + 1, :128]
        own_far[way] = one_hot(wanted, CELLS0, 0).T[:RIM0].astype(BF16)

    @pl.when(moved)
    def _():
        state_copy().wait()
        weather[:FIELDS] = states_moved[:, 0, :]

    def prepare_gather():
        for way in range(2):
            wanted = info_in[1 - way, 2 * way + 1 : 2 * way + 2, :128]
            rows = slice(way * RIM1, (way + 1) * RIM1)
            far1[rows] = one_hot(wanted, CELLS1, 0).T[:RIM1].astype(BF16)
        gather[CELLS1:] = dot_nn(far1[...], gather[:CELLS1]).astype(BF16)

    def prepare_rest():
        for way in range(2):
            wanted = info_in[1 - way, 2 * way : 2 * way + 1, :128]
            rows = slice(way * RIM0, (way + 1) * RIM0)
            far0[rows] = one_hot(wanted, CELLS0, 0).T[:RIM0].astype(BF16)
        one = dot_nn(far0[...], grow[:, :CELLS1]).astype(BF16)
        far_grow[:, :CELLS1] = one
        far_grow[:, CELLS1:] = one

        @pl.when(moved)
        def _():
            gru_copy().wait()
            gru_in[...] = gru_moved[...]

        state = jnp.concatenate(
            [gru_in[...].reshape(C1, CELLS1), jnp.zeros((256 - C1, CELLS1), F32)], 0
        )
        carried[...] = state.T[:, :C1]

    def fill0(r):
        pad0[:, 3 : 3 + SIDE0, 8:24, :] = r.astype(F32).reshape(TILES, SIDE0, SIDE0, C0)
        sides = dot_nn(near0[...], r).reshape(TILES, SIDE0, 8, C0)
        pad0[:, 3 : 3 + SIDE0, 0:8, :] = sides
        pad0[:, 3 : 3 + SIDE0, 24:32, :] = sides

    def fill1(r):
        pad1[:, 3 : 3 + SIDE1, 8:16, :] = r.astype(F32).reshape(TILES, SIDE1, SIDE1, C1)
        sides = dot_nn(near1[...], r).reshape(TILES, SIDE1, 8, C1)
        pad1[:, 3 : 3 + SIDE1, 0:8, :] = sides
        pad1[:, 3 : 3 + SIDE1, 16:24, :] = sides

    def fine_block_inner(taps, expand, shrink, out):
        def body(tile, _):
            for half in range(2):
                total = conv_tile(pad0, tile, SIDE0, 8 + 8 * half, taps)
                y0[tile, :, 8 * half : 8 * half + 8, :] = total
            y = y0[tile, 3:13].reshape(10 * SIDE0, C0)
            r = pad0[tile, 6:16, 8:24, :].reshape(10 * SIDE0, C0)
            out[tile, 3:13] = finish(y, r, expand[...], shrink[...]).reshape(10, SIDE0, C0)
            return 0

        lax.fori_loop(0, TILES, body, 0)
        for tile in range(TILES):
            for side, top in ((0, 3), (1, 16)):
                edge_r[tile, side] = pad0[tile, top : top + 3, 8:24, :]

    def fine_block_outer(taps, expand, shrink, out):
        def body(tile, _):
            for side, top in ((0, 0), (1, 13)):
                for half in range(2):
                    columns = slice(8 * half, 8 * half + 8)
                    rows = [y0[tile, top + o, columns, :] for o in range(3)]
                    rows = conv_halo(halo0, side, tile, 8 + 8 * half, taps, rows)
                    for o in range(3):
                        edge_y[tile, side, o, columns, :] = rows[o]
            return 0

        lax.fori_loop(0, TILES, body, 0)
        y = edge_y[...].reshape(2 * RIM0, C0)
        r = edge_r[...].reshape(2 * RIM0, C0)
        done = finish(y, r, expand[...], shrink[...]).reshape(TILES, 2, 3, SIDE0, C0)
        for tile in range(TILES):
            out[tile, 0:3] = done[tile, 0]
            out[tile, 13:16] = done[tile, 1]

    def coarse_block(r, slot, taps, expand, shrink, meanwhile):
        copies = pair(c_out, c_in, c_send, c_recv, slot)
        start(copies)
        fill1(r)

        def body(tile, _):
            y1[tile] = conv_tile(pad1, tile, SIDE1, 8, taps)
            return 0

        lax.fori_loop(0, TILES, body, 0)
        meanwhile()
        wait(copies)
        for way in range(2):
            arrived = c_in[slot, way].astype(F32).reshape(TILES, 3, SIDE1, C1)
            halo1[way, :, :, 8:16, :] = arrived

        def edge(tile, _):
            for side, top in ((0, 0), (1, 5)):
                rows = [y1[tile, top + o] for o in range(3)]
                rows = conv_halo(halo1, side, tile, 8, taps, rows)
                for o in range(3):
                    y1[tile, top + o] = rows[o]
            return 0

        lax.fori_loop(0, TILES, edge, 0)
        y = y1[...].reshape(CELLS1, C1)
        return finish(y, r.astype(F32), expand[...], shrink[...])

    def step_body(step, _):
        fields = weather[...].astype(BF16).astype(F32).T.astype(BF16)
        lift = embed[...].astype(BF16)
        fill0(dot_nn(fields, lift).astype(BF16))
        fine_block_inner(taps_ef, ef_expand, ef_shrink, skip)

        @pl.when(step == 0)
        def _():
            near1[...] = one_hot(info_moved[5:6, :128], CELLS1, 0).T.astype(BF16)
            wait(info_copies())
            prepare_gather()

        wait(weather_copies(step, (after, before)))
        for way in range(2):
            rim = dot_nt(own_far[way], w_in[step, way]).astype(BF16)
            rim = dot_nn(rim, lift).astype(BF16).astype(F32)
            halo0[way, :, :, 8:24, :] = rim.reshape(TILES, 3, SIDE0, C0)
        fine_block_outer(taps_ef, ef_expand, ef_shrink, skip)

        coarse = dot_nn(gather[...], skip[...].reshape(CELLS0, C0)).astype(BF16)
        coarse = dot_nt(coarse, down_w[...]).astype(BF16)
        for way in range(2):
            top = CELLS1 + way * RIM1
            c_out[2 * step, way] = coarse[top : top + RIM1]

        def after_skip():
            @pl.when(step == 0)
            def _():
                prepare_rest()

            kept = skip[...].reshape(CELLS0, C0)
            part[...] = dot_nn(kept, comb_b[...])
            far_part[...] = dot_nn(dot_nn(far0[...], kept).astype(BF16), comb_b[...])
            held = carried[...].astype(BF16)
            for g in range(2):
                held_gates[g] = dot_nt(held, gru_b[g])

        coarse = coarse_block(
            coarse[:CELLS1], 2 * step, taps_ec, ec_expand, ec_shrink, after_skip
        )

        old = carried[...]
        update = jax.nn.sigmoid(dot_nt(coarse, gru_a[0]) + held_gates[0])
        reset = jax.nn.sigmoid(dot_nt(coarse, gru_a[1]) + held_gates[1])
        gated = (reset * old).astype(BF16)
        candidate = jnp.tanh(dot_nt(coarse, gru_a[2]) + dot_nt(gated, gru_b[2]))
        new = (1.0 - update) * old + update * candidate
        carried[...] = new

        new = new.astype(BF16)
        wanted = dot_nn(far1[...], new).astype(BF16)
        for way in range(2):
            c_out[2 * step + 1, way] = wanted[way * RIM1 : (way + 1) * RIM1]

        def after_update():
            @pl.when(step == STEPS - 1)
            def _():
                last = jnp.concatenate([carried[...], jnp.zeros((CELLS1, 256 - C1), F32)], 1)
                last = last.T[:C1]

                @pl.when(moved)
                def _():
                    gru_out[...] = last
                    gru_result_copy().start()

                @pl.when(jnp.logical_not(moved))
                def _():
                    gru_final[0] = last

        decoded = coarse_block(
            new, 2 * step + 1, taps_dc, dc_expand, dc_shrink, after_update
        )

        lifted = halves(dot_nn(decoded, lift_w[...]))
        wanted = (dot_nn(far_grow[...], lifted) + far_part[...]).astype(BF16)
        for way in range(2):
            f_out[step, way] = wanted[way * RIM0 : (way + 1) * RIM0]
        copies = pair(f_out, f_in, f_send, f_recv, step)
        start(copies)
        fill0((dot_nn(grow[...], lifted) + part[...]).astype(BF16))
        fine_block_inner(taps_df, df_expand, df_shrink, merged)
        wait(copies)
        for way in range(2):
            arrived = f_in[step, way].astype(F32).reshape(TILES, 3, SIDE0, C0)
            halo0[way, :, :, 8:24, :] = arrived
        fine_block_outer(taps_df, df_expand, df_shrink, merged)

        change = dot_nt(head_w[...], merged[...].reshape(CELLS0, C0))
        now = weather[:FIELDS] + change
        weather[:FIELDS] = now

        @pl.when(step < STEPS - 1)
        def _():
            w_out[step + 1] = weather[...].astype(BF16)
            start(weather_copies(step + 1, (after, before)))

        @pl.when(moved)
        def _():
            result_out[step] = weather[...]
            result_copy(step).start()

        @pl.when(jnp.logical_not(moved))
        def _():
            forecast[step, 0] = now

        return 0

    lax.fori_loop(0, STEPS, step_body, 0)

    @pl.when(moved)
    def _():
        gru_result_copy().wait()
        gru_final[0] = gru_back[...]
        for step in range(STEPS):
            result_copy(step).wait()
            forecast[step, 0] = result_in[step, :FIELDS]


def local(states, gru_state, neighbours, orient, *weights):
    (
        embed_w, ef_depth, ef_expand, ef_shrink, down_w, ec_depth, ec_expand, ec_shrink,
        gru_w, dc_depth, dc_expand, dc_shrink, up_w, combine_w, df_depth, df_expand,
        df_shrink, head_w,
    ) = weights
    weights = (
        embed_w.T, ef_depth.T, ef_expand.T, ef_shrink, down_w, ec_depth.T, ec_expand.T, ec_shrink,
        gru_w, dc_depth.T, dc_expand.T, dc_shrink, up_w.T, combine_w.T, df_depth.T, df_expand.T,
        df_shrink, head_w,
    )
    hbm = pl.BlockSpec(memory_space=pltpu.HBM)
    smem = pl.BlockSpec(memory_space=pltpu.SMEM)
    scratch = [pltpu.VMEM(w.shape, w.dtype) for w in weights]
    scratch += [
        pltpu.VMEM((FIELDS, 1, CELLS0), F32),
        pltpu.VMEM((C1, 1, CELLS1), F32),
        pltpu.VMEM((FIELDS, 1, CELLS0), F32),
        pltpu.VMEM((C1, 1, CELLS1), F32),
        pltpu.VMEM((8, 256), jnp.int32),
        pltpu.VMEM((STEPS, ROWS, CELLS0), F32),
        pltpu.VMEM((STEPS, ROWS, CELLS0), F32),
        pltpu.VMEM((C1, CELLS1), F32),
        pltpu.VMEM((C1, CELLS1), F32),
        pltpu.VMEM((ROWS, CELLS0), F32),
        pltpu.VMEM((CELLS1, C1), F32),
        pltpu.VMEM((ROWS, C0), F32),
        pltpu.VMEM((3, C1, C1), BF16),
        pltpu.VMEM((3, C1, C1), BF16),
        pltpu.VMEM((C1, C0), BF16),
        pltpu.VMEM((C0, C0), BF16),
        pltpu.VMEM((49, 8, C0), F32),
        pltpu.VMEM((49, 8, C0), F32),
        pltpu.VMEM((49, 8, C1), F32),
        pltpu.VMEM((49, 8, C1), F32),
        pltpu.VMEM((TILES * SIDE0 * 8, CELLS0), BF16),
        pltpu.VMEM((TILES * SIDE1 * 8, CELLS1), BF16),
        pltpu.VMEM((2, RIM0, CELLS0), BF16),
        pltpu.VMEM((2 * RIM1, CELLS1), BF16),
        pltpu.VMEM((2 * RIM0, CELLS0), BF16),
        pltpu.VMEM((CELLS0, 2 * CELLS1), BF16),
        pltpu.VMEM((CELLS1 + 2 * RIM1, CELLS0), BF16),
        pltpu.VMEM((2 * RIM0, 2 * CELLS1), BF16),
        pltpu.VMEM((TILES, SIDE0 + 6, 32, C0), F32),
        pltpu.VMEM((TILES, SIDE1 + 6, 24, C1), F32),
        pltpu.VMEM((2, TILES, 3, 32, C0), F32),
        pltpu.VMEM((2, TILES, 3, 24, C1), F32),
        pltpu.VMEM((TILES, SIDE0, SIDE0, C0), F32),
        pltpu.VMEM((TILES, SIDE1, SIDE1, C1), F32),
        pltpu.VMEM((TILES, 2, 3, SIDE0, C0), F32),
        pltpu.VMEM((TILES, 2, 3, SIDE0, C0), F32),
        pltpu.VMEM((TILES, SIDE0, SIDE0, C0), BF16),
        pltpu.VMEM((TILES, SIDE0, SIDE0, C0), BF16),
        pltpu.VMEM((CELLS0, C0), F32),
        pltpu.VMEM((2 * RIM0, C0), F32),
        pltpu.VMEM((2, CELLS1, C1), F32),
        pltpu.VMEM((8, 256), jnp.int32),
        pltpu.VMEM((2, 8, 256), jnp.int32),
        pltpu.VMEM((STEPS, ROWS, CELLS0), BF16),
        pltpu.VMEM((STEPS, 2, ROWS, CELLS0), BF16),
        pltpu.VMEM((STEPS, 2, RIM0, C0), BF16),
        pltpu.VMEM((STEPS, 2, RIM0, C0), BF16),
        pltpu.VMEM((2 * STEPS, 2, RIM1, C1), BF16),
        pltpu.VMEM((2 * STEPS, 2, RIM1, C1), BF16),
        pltpu.SemaphoreType.DMA((2 + WEIGHTS,)),
        pltpu.SemaphoreType.DMA((4,)),
        pltpu.SemaphoreType.DMA((4,)),
        pltpu.SemaphoreType.DMA((STEPS,)),
        pltpu.SemaphoreType.DMA((STEPS,)),
        pltpu.SemaphoreType.DMA((2,)),
        pltpu.SemaphoreType.DMA((2,)),
        pltpu.SemaphoreType.DMA((STEPS, 2)),
        pltpu.SemaphoreType.DMA((STEPS, 2)),
        pltpu.SemaphoreType.DMA((STEPS, 2)),
        pltpu.SemaphoreType.DMA((STEPS, 2)),
        pltpu.SemaphoreType.DMA((2 * STEPS, 2)),
        pltpu.SemaphoreType.DMA((2 * STEPS, 2)),
    ]
    return pl.pallas_call(
        kernel,
        out_shape=(
            jax.ShapeDtypeStruct((STEPS, 1, FIELDS, CELLS0), F32),
            jax.ShapeDtypeStruct((1, C1, CELLS1), F32),
        ),
        in_specs=[hbm, hbm, smem, smem] + [hbm] * len(weights),
        out_specs=(pl.BlockSpec(memory_space=pltpu.VMEM),) * 2,
        scratch_shapes=scratch,
        compiler_params=pltpu.CompilerParams(
            collective_id=0, has_side_effects=True, vmem_limit_bytes=56 * 1024 * 1024
        ),
    )(states.transpose(1, 0, 2), gru_state.transpose(1, 0, 2), neighbours, orient, *weights)


def solution(mesh):
    in_specs = (
        P("segment", None, "face"),
        P("segment", None, "face"),
        P("face", None),
        P("face", None),
    ) + (P(),) * 18
    out_specs = (P(None, "segment", None, "face"), P("segment", None, "face"))
    return jax.shard_map(local, mesh=mesh, in_specs=in_specs, out_specs=out_specs, check_vma=False)
```

```python
import jax
import jax.numpy as jnp
from jax import lax
from jax.experimental import pallas as pl
from jax.experimental.pallas import tpu as pltpu
from jax.sharding import PartitionSpec as P

FIELDS = 9
C0 = 90
C1 = 180
SIDE0 = 16
SIDE1 = 8
TILES = 2
STEPS = 2
CELLS0 = TILES * SIDE0 * SIDE0
CELLS1 = TILES * SIDE1 * SIDE1
RIM0 = TILES * 3 * SIDE0
RIM1 = TILES * 3 * SIDE1
ROWS = 16
F32, BF16 = jnp.float32, jnp.bfloat16
NORTH, EAST, SOUTH, WEST = range(4)
ROW = 16


def dot_nt(a, b):
    return lax.dot_general(a, b, (((1,), (1,)), ((), ())), preferred_element_type=F32)


def dot_nn(a, b):
    return jnp.dot(a, b, preferred_element_type=F32)


def one_hot(index, cells, axis):
    shape = (index.shape[0], cells) if axis == 1 else (cells, index.shape[1])
    hit = lax.broadcasted_iota(jnp.int32, shape, axis) == index
    return jnp.where(hit, 1.0, 0.0)


def rim_line(nbr, orient, tile, side, p):
    o = orient[tile, p]
    from_side = lax.shift_right_logical(o, 1)
    per_depth = jnp.where(
        from_side == 0, side, jnp.where(from_side == 1, -1, jnp.where(from_side == 2, -side, 1))
    )
    base = jnp.where(from_side == 1, side - 1, jnp.where(from_side == 2, side * (side - 1), 0))
    per_step = jnp.where((from_side & 1) == 0, 1, side)
    turned = (o & 1) == 1
    base = base + jnp.where(turned, per_step * (side - 1), 0)
    per_step = jnp.where(turned, -per_step, per_step)
    return base + (nbr[tile, p] & 1) * side * side, per_depth, per_step


def far_index(m, nbr, orient, side, p):
    index = jnp.full(m.shape, -1, jnp.int32)
    for tile in range(TILES):
        base, per_depth, per_step = rim_line(nbr, orient, tile, side, p)
        local = m - tile * 3 * side
        row = jnp.where(local >= 2 * side, 2, jnp.where(local >= side, 1, 0))
        depth = 2 - row if p == NORTH else row
        value = base + per_depth * depth + per_step * (local - row * side)
        index = jnp.where((local >= 0) & (local < 3 * side), value, index)
    return index


def near_index(m, nbr, orient, side):
    index = jnp.full(m.shape, -1, jnp.int32)
    for tile in range(TILES):
        base_e, depth_e, step_e = rim_line(nbr, orient, tile, side, EAST)
        base_w, depth_w, step_w = rim_line(nbr, orient, tile, side, WEST)
        local = m - tile * side * 8
        row, place = lax.shift_right_arithmetic(local, 3), local & 7
        east = base_e + depth_e * place + step_e * row
        west = base_w + depth_w * (7 - place) + step_w * row
        value = jnp.where(place < 3, east, jnp.where(place >= 5, west, -1))
        index = jnp.where((local >= 0) & (local < 8 * side), value, index)
    return index


def host_of(segment, block, size):
    core, odd = segment & 1, block & 1
    face = block - odd + (1 - core)
    last = lax.rem(block, ROW) == ROW - 1
    return segment - core + (1 - odd), jnp.where(last, lax.rem(face + ROW, size), face)


def block_of(segment, face, size):
    core, odd = segment & 1, face & 1
    block = face - odd + (1 - core)
    last = lax.rem(block, ROW) == ROW - 1
    return segment - core + (1 - odd), jnp.where(last, lax.rem(block + size - ROW, size), block)


def spread_taps(weight):
    return jnp.broadcast_to(weight.astype(F32)[:, None, :], (49, 8, weight.shape[1]))


def halves(x):
    high = x.astype(BF16)
    return jnp.concatenate([high, (x - high.astype(F32)).astype(BF16)], 0)


def normalise(y, channels):
    centred = y - jnp.sum(y, 1, keepdims=True) * (1.0 / channels)
    var = jnp.sum(centred * centred, 1, keepdims=True) * (1.0 / channels)
    return (centred * lax.rsqrt(var + 1e-6)).astype(BF16)


def gelu(x):
    return (0.5 * x) * (1.0 + lax.erf(x * 0.7071067811865476))


def finish(y, r, expand, shrink):
    normed = normalise(y, y.shape[1])
    expanded = gelu(dot_nn(normed, expand)).astype(BF16)
    return (r + dot_nt(expanded, shrink)).astype(BF16)


def conv_tile(pad, tile, rows, first, taps):
    total = None
    for q in range(7):
        x = pad[tile, :, first + q - 3 : first + q + 5, :]
        for u in range(7):
            term = taps[7 * u + q][None] * x[u : u + rows]
            total = term if total is None else total + term
    return total


def conv_halo(halo, side, tile, first, taps, rows):
    rows = list(rows)
    for q in range(7):
        for h in range(3):
            x = halo[side, tile, h, first + q - 3 : first + q + 5, :]
            for o in range(3):
                u = h - o if side == 0 else 6 + h - o
                if 0 <= u <= 6:
                    rows[o] = rows[o] + taps[7 * u + q] * x
    return rows


WEIGHTS = 18


def kernel(
    states, gru_state, nbr, orient, *refs,
):
    hbm_weights, refs = refs[:WEIGHTS], refs[WEIGHTS:]
    forecast, gru_final = refs[:2]
    (
        embed_w, ef_depth, ef_expand, ef_shrink, down_w, ec_depth, ec_expand, ec_shrink,
        gru_w, dc_depth, dc_expand, dc_shrink, up_w, combine_w, df_depth, df_expand,
        df_shrink, head_w,
    ) = vmem_weights = refs[2 : 2 + WEIGHTS]
    (
        states_in, gru_in, states_moved, gru_moved, info_moved,
        result_out, result_in, gru_out, gru_back,
        weather, carried, embed, gru_a, gru_b, lift_w, comb_b,
        taps_ef, taps_df, taps_ec, taps_dc,
        near0, near1, own_far, far1, far0, grow, gather, far_grow,
        pad0, pad1, halo0, halo1, y0, y1, edge_y, edge_r, skip, merged,
        part, far_part, held_gates,
        info_out, info_in, w_out, w_in, f_out, f_in, c_out, c_in,
        load,
        m_send, m_recv, r_send, r_recv, info_send, info_recv, w_send, w_recv, f_send, f_recv, c_send, c_recv,
    ) = refs[2 + WEIGHTS :]
    size = lax.axis_size("face")
    here = lax.axis_index("segment"), lax.axis_index("face")
    mine = block_of(*here, size)
    away = host_of(*here, size)
    moved = (away[0] != here[0]) | (away[1] != here[1])

    def beside(place, step):
        return place[0], lax.rem(place[1] + step + size, size)

    home_after, home_before = beside(mine, 1), beside(mine, -1)
    after, before = host_of(*home_after, size), host_of(*home_before, size)
    first_targets = host_of(*beside(here, 1), size), host_of(*beside(here, -1), size)

    def greet(target):
        pl.semaphore_signal(
            barrier, inc=1, device_id={"segment": target[0], "face": target[1]},
            device_id_type=pl.DeviceIdType.MESH,
        )

    def remote(src, dst, send, recv, target):
        return pltpu.make_async_remote_copy(
            src_ref=src, dst_ref=dst, send_sem=send, recv_sem=recv,
            device_id={"segment": target[0], "face": target[1]},
            device_id_type=pl.DeviceIdType.MESH,
        )

    def pair(out, into, send, recv, slot):
        return [
            remote(out.at[slot, w], into.at[slot, w], send.at[slot, w], recv.at[slot, w], target)
            for w, target in enumerate((after, before))
        ]

    def info_copies():
        return [
            remote(info_out, info_in.at[w], info_send.at[w], info_recv.at[w], target)
            for w, target in enumerate(first_targets)
        ]

    def weather_copies(step, targets):
        return [
            remote(w_out.at[step], w_in.at[step, w], w_send.at[step, w], w_recv.at[step, w], target)
            for w, target in enumerate(targets)
        ]

    def state_copy():
        return remote(states_in, states_moved, m_send.at[0], m_recv.at[0], away)

    def own_info_copy():
        return remote(info_out, info_moved, m_send.at[1], m_recv.at[1], away)

    def gru_copy():
        return remote(gru_in, gru_moved, m_send.at[2], m_recv.at[2], away)

    def result_copy(step):
        return remote(
            result_out.at[step], result_in.at[step], r_send.at[step], r_recv.at[step], mine
        )

    def gru_result_copy():
        return remote(gru_out, gru_back, m_send.at[3], m_recv.at[3], mine)

    def start(copies):
        for copy in copies:
            copy.start()

    def wait(copies):
        for copy in copies:
            copy.wait()

    barrier = pltpu.get_barrier_semaphore()
    for target in (home_after, home_before, after, before):
        greet(target)

    @pl.when(moved)
    def _():
        greet(mine)
        greet(away)

    loads = [pltpu.make_async_copy(states, states_in, load.at[0])]
    loads += [
        pltpu.make_async_copy(src, dst, load.at[2 + n])
        for n, (src, dst) in enumerate(zip(hbm_weights, vmem_weights))
    ]
    loads.append(pltpu.make_async_copy(gru_state, gru_in, load.at[1]))
    start(loads)

    lane = lax.broadcasted_iota(jnp.int32, (1, 256), 1)
    for row, p in ((0, NORTH), (2, SOUTH)):
        info_out[row : row + 1] = far_index(lane, nbr, orient, SIDE0, p)
        info_out[row + 1 : row + 2] = far_index(lane, nbr, orient, SIDE1, p)
    info_out[4:5] = near_index(lane, nbr, orient, SIDE0)
    info_out[5:6] = near_index(lane, nbr, orient, SIDE1)
    info_out[6:8] = jnp.zeros((2, 256), jnp.int32)
    weather[...] = jnp.zeros_like(weather)
    loads[0].wait()
    weather[:FIELDS] = states_in[:, 0, :]
    w_out[0] = weather[...].astype(BF16)
    pl.semaphore_wait(barrier, jnp.where(moved, 6, 4))

    @pl.when(moved)
    def _():
        own_info_copy().start()
        state_copy().start()

    start(weather_copies(0, first_targets))
    start(info_copies())

    def coarse_of(cell):
        tile = lax.shift_right_logical(cell, 8)
        row = lax.shift_right_logical(cell, 5) & 7
        return tile * 64 + row * 8 + (lax.shift_right_logical(cell, 1) & 7)

    pad0[...] = jnp.zeros_like(pad0)
    halo0[...] = jnp.zeros_like(halo0)
    pad1[...] = jnp.zeros_like(pad1)
    halo1[...] = jnp.zeros_like(halo1)
    cell = lax.broadcasted_iota(jnp.int32, (CELLS0, 1), 0)
    one = one_hot(coarse_of(cell), CELLS1, 1).astype(BF16)
    grow[:, :CELLS1] = one
    grow[:, CELLS1:] = one
    cell = lax.broadcasted_iota(jnp.int32, (1, CELLS0), 1)
    gather[:CELLS1] = (0.25 * one_hot(coarse_of(cell), CELLS1, 0)).astype(BF16)
    for copy in loads[1:]:
        copy.wait()

    @pl.when(moved)
    def _():
        gru_copy().start()

    embed[...] = jnp.zeros_like(embed)
    embed[:FIELDS] = embed_w[...].astype(F32)
    taps_ef[...] = spread_taps(ef_depth[...])
    taps_df[...] = spread_taps(df_depth[...])
    taps_ec[...] = spread_taps(ec_depth[...])
    taps_dc[...] = spread_taps(dc_depth[...])
    for g in range(3):
        wide = gru_w[g].astype(F32)
        gru_a[g] = wide[:, :C1].astype(BF16)
        gru_b[g] = wide[:, C1:].astype(BF16)
    wide = combine_w[...].astype(F32)
    comb_b[...] = wide[C0:].astype(BF16)
    lift_w[...] = dot_nn(up_w[...], wide[:C0].astype(BF16)).astype(BF16)

    @pl.when(moved)
    def _():
        own_info_copy().wait()

    @pl.when(jnp.logical_not(moved))
    def _():
        info_moved[...] = info_out[...]

    near0[...] = one_hot(info_moved[4:5], CELLS0, 0).T.astype(BF16)
    for way in range(2):
        wanted = info_moved[2 * way : 2 * way + 1, :128]
        own_far[way] = one_hot(wanted, CELLS0, 0).T[:RIM0].astype(BF16)

    @pl.when(moved)
    def _():
        state_copy().wait()
        weather[:FIELDS] = states_moved[:, 0, :]

    def prepare_gather():
        for way in range(2):
            wanted = info_in[1 - way, 2 * way + 1 : 2 * way + 2, :128]
            rows = slice(way * RIM1, (way + 1) * RIM1)
            far1[rows] = one_hot(wanted, CELLS1, 0).T[:RIM1].astype(BF16)
        gather[CELLS1:] = dot_nn(far1[...], gather[:CELLS1]).astype(BF16)

    def prepare_rest():
        for way in range(2):
            wanted = info_in[1 - way, 2 * way : 2 * way + 1, :128]
            rows = slice(way * RIM0, (way + 1) * RIM0)
            far0[rows] = one_hot(wanted, CELLS0, 0).T[:RIM0].astype(BF16)
        one = dot_nn(far0[...], grow[:, :CELLS1]).astype(BF16)
        far_grow[:, :CELLS1] = one
        far_grow[:, CELLS1:] = one

        @pl.when(moved)
        def _():
            gru_copy().wait()
            gru_in[...] = gru_moved[...]

        state = jnp.concatenate(
            [gru_in[...].reshape(C1, CELLS1), jnp.zeros((256 - C1, CELLS1), F32)], 0
        )
        carried[...] = state.T[:, :C1]

    def fill0(r):
        pad0[:, 3 : 3 + SIDE0, 8:24, :] = r.astype(F32).reshape(TILES, SIDE0, SIDE0, C0)
        sides = dot_nn(near0[...], r).reshape(TILES, SIDE0, 8, C0)
        pad0[:, 3 : 3 + SIDE0, 0:8, :] = sides
        pad0[:, 3 : 3 + SIDE0, 24:32, :] = sides

    def fill1(r):
        pad1[:, 3 : 3 + SIDE1, 8:16, :] = r.astype(F32).reshape(TILES, SIDE1, SIDE1, C1)
        sides = dot_nn(near1[...], r).reshape(TILES, SIDE1, 8, C1)
        pad1[:, 3 : 3 + SIDE1, 0:8, :] = sides
        pad1[:, 3 : 3 + SIDE1, 16:24, :] = sides

    def fine_block_inner(taps, expand, shrink, out):
        def body(tile, _):
            for half in range(2):
                total = conv_tile(pad0, tile, SIDE0, 8 + 8 * half, taps)
                y0[tile, :, 8 * half : 8 * half + 8, :] = total
            y = y0[tile, 3:13].reshape(10 * SIDE0, C0)
            r = pad0[tile, 6:16, 8:24, :].reshape(10 * SIDE0, C0)
            out[tile, 3:13] = finish(y, r, expand[...], shrink[...]).reshape(10, SIDE0, C0)
            return 0

        lax.fori_loop(0, TILES, body, 0, unroll=True)
        for tile in range(TILES):
            for side, top in ((0, 3), (1, 16)):
                edge_r[tile, side] = pad0[tile, top : top + 3, 8:24, :]

    def fine_block_outer(taps, expand, shrink, out):
        def body(tile, _):
            for side, top in ((0, 0), (1, 13)):
                for half in range(2):
                    columns = slice(8 * half, 8 * half + 8)
                    rows = [y0[tile, top + o, columns, :] for o in range(3)]
                    rows = conv_halo(halo0, side, tile, 8 + 8 * half, taps, rows)
                    for o in range(3):
                        edge_y[tile, side, o, columns, :] = rows[o]
            return 0

        lax.fori_loop(0, TILES, body, 0, unroll=True)
        y = edge_y[...].reshape(2 * RIM0, C0)
        r = edge_r[...].reshape(2 * RIM0, C0)
        done = finish(y, r, expand[...], shrink[...]).reshape(TILES, 2, 3, SIDE0, C0)
        for tile in range(TILES):
            out[tile, 0:3] = done[tile, 0]
            out[tile, 13:16] = done[tile, 1]

    def coarse_block(r, slot, taps, expand, shrink, meanwhile):
        copies = pair(c_out, c_in, c_send, c_recv, slot)
        start(copies)
        fill1(r)

        def body(tile, _):
            y1[tile] = conv_tile(pad1, tile, SIDE1, 8, taps)
            return 0

        lax.fori_loop(0, TILES, body, 0, unroll=True)
        meanwhile()
        wait(copies)
        for way in range(2):
            arrived = c_in[slot, way].astype(F32).reshape(TILES, 3, SIDE1, C1)
            halo1[way, :, :, 8:16, :] = arrived

        def edge(tile, _):
            for side, top in ((0, 0), (1, 5)):
                rows = [y1[tile, top + o] for o in range(3)]
                rows = conv_halo(halo1, side, tile, 8, taps, rows)
                for o in range(3):
                    y1[tile, top + o] = rows[o]
            return 0

        lax.fori_loop(0, TILES, edge, 0, unroll=True)
        y = y1[...].reshape(CELLS1, C1)
        return finish(y, r.astype(F32), expand[...], shrink[...])

    def step_body(step, _):
        fields = weather[...].astype(BF16).astype(F32).T.astype(BF16)
        lift = embed[...].astype(BF16)
        fill0(dot_nn(fields, lift).astype(BF16))
        fine_block_inner(taps_ef, ef_expand, ef_shrink, skip)

        @pl.when(step == 0)
        def _():
            near1[...] = one_hot(info_moved[5:6, :128], CELLS1, 0).T.astype(BF16)
            wait(info_copies())
            prepare_gather()

        wait(weather_copies(step, (after, before)))
        for way in range(2):
            rim = dot_nt(own_far[way], w_in[step, way]).astype(BF16)
            rim = dot_nn(rim, lift).astype(BF16).astype(F32)
            halo0[way, :, :, 8:24, :] = rim.reshape(TILES, 3, SIDE0, C0)
        fine_block_outer(taps_ef, ef_expand, ef_shrink, skip)

        coarse = dot_nn(gather[...], skip[...].reshape(CELLS0, C0)).astype(BF16)
        coarse = dot_nt(coarse, down_w[...]).astype(BF16)
        for way in range(2):
            top = CELLS1 + way * RIM1
            c_out[2 * step, way] = coarse[top : top + RIM1]

        def after_skip():
            @pl.when(step == 0)
            def _():
                prepare_rest()

            kept = skip[...].reshape(CELLS0, C0)
            part[...] = dot_nn(kept, comb_b[...])
            far_part[...] = dot_nn(dot_nn(far0[...], kept).astype(BF16), comb_b[...])
            held = carried[...].astype(BF16)
            for g in range(2):
                held_gates[g] = dot_nt(held, gru_b[g])

        coarse = coarse_block(
            coarse[:CELLS1], 2 * step, taps_ec, ec_expand, ec_shrink, after_skip
        )

        old = carried[...]
        update = jax.nn.sigmoid(dot_nt(coarse, gru_a[0]) + held_gates[0])
        reset = jax.nn.sigmoid(dot_nt(coarse, gru_a[1]) + held_gates[1])
        gated = (reset * old).astype(BF16)
        candidate = jnp.tanh(dot_nt(coarse, gru_a[2]) + dot_nt(gated, gru_b[2]))
        new = (1.0 - update) * old + update * candidate
        carried[...] = new

        new = new.astype(BF16)
        wanted = dot_nn(far1[...], new).astype(BF16)
        for way in range(2):
            c_out[2 * step + 1, way] = wanted[way * RIM1 : (way + 1) * RIM1]

        def after_update():
            @pl.when(step == STEPS - 1)
            def _():
                last = jnp.concatenate([carried[...], jnp.zeros((CELLS1, 256 - C1), F32)], 1)
                last = last.T[:C1]

                @pl.when(moved)
                def _():
                    gru_out[...] = last
                    gru_result_copy().start()

                @pl.when(jnp.logical_not(moved))
                def _():
                    gru_final[0] = last

        decoded = coarse_block(
            new, 2 * step + 1, taps_dc, dc_expand, dc_shrink, after_update
        )

        lifted = halves(dot_nn(decoded, lift_w[...]))
        wanted = (dot_nn(far_grow[...], lifted) + far_part[...]).astype(BF16)
        for way in range(2):
            f_out[step, way] = wanted[way * RIM0 : (way + 1) * RIM0]
        copies = pair(f_out, f_in, f_send, f_recv, step)
        start(copies)
        fill0((dot_nn(grow[...], lifted) + part[...]).astype(BF16))
        fine_block_inner(taps_df, df_expand, df_shrink, merged)
        wait(copies)
        for way in range(2):
            arrived = f_in[step, way].astype(F32).reshape(TILES, 3, SIDE0, C0)
            halo0[way, :, :, 8:24, :] = arrived
        fine_block_outer(taps_df, df_expand, df_shrink, merged)

        change = dot_nt(head_w[...], merged[...].reshape(CELLS0, C0))
        now = weather[:FIELDS] + change
        weather[:FIELDS] = now

        @pl.when(step < STEPS - 1)
        def _():
            w_out[step + 1] = weather[...].astype(BF16)
            start(weather_copies(step + 1, (after, before)))

        @pl.when(moved)
        def _():
            result_out[step] = weather[...]
            result_copy(step).start()

        @pl.when(jnp.logical_not(moved))
        def _():
            forecast[step, 0] = now

        return 0

    lax.fori_loop(0, STEPS, step_body, 0)

    @pl.when(moved)
    def _():
        gru_result_copy().wait()
        gru_final[0] = gru_back[...]
        for step in range(STEPS):
            result_copy(step).wait()
            forecast[step, 0] = result_in[step, :FIELDS]


def local(states, gru_state, neighbours, orient, *weights):
    (
        embed_w, ef_depth, ef_expand, ef_shrink, down_w, ec_depth, ec_expand, ec_shrink,
        gru_w, dc_depth, dc_expand, dc_shrink, up_w, combine_w, df_depth, df_expand,
        df_shrink, head_w,
    ) = weights
    weights = (
        embed_w.T, ef_depth.T, ef_expand.T, ef_shrink, down_w, ec_depth.T, ec_expand.T, ec_shrink,
        gru_w, dc_depth.T, dc_expand.T, dc_shrink, up_w.T, combine_w.T, df_depth.T, df_expand.T,
        df_shrink, head_w,
    )
    hbm = pl.BlockSpec(memory_space=pltpu.HBM)
    smem = pl.BlockSpec(memory_space=pltpu.SMEM)
    scratch = [pltpu.VMEM(w.shape, w.dtype) for w in weights]
    scratch += [
        pltpu.VMEM((FIELDS, 1, CELLS0), F32),
        pltpu.VMEM((C1, 1, CELLS1), F32),
        pltpu.VMEM((FIELDS, 1, CELLS0), F32),
        pltpu.VMEM((C1, 1, CELLS1), F32),
        pltpu.VMEM((8, 256), jnp.int32),
        pltpu.VMEM((STEPS, ROWS, CELLS0), F32),
        pltpu.VMEM((STEPS, ROWS, CELLS0), F32),
        pltpu.VMEM((C1, CELLS1), F32),
        pltpu.VMEM((C1, CELLS1), F32),
        pltpu.VMEM((ROWS, CELLS0), F32),
        pltpu.VMEM((CELLS1, C1), F32),
        pltpu.VMEM((ROWS, C0), F32),
        pltpu.VMEM((3, C1, C1), BF16),
        pltpu.VMEM((3, C1, C1), BF16),
        pltpu.VMEM((C1, C0), BF16),
        pltpu.VMEM((C0, C0), BF16),
        pltpu.VMEM((49, 8, C0), F32),
        pltpu.VMEM((49, 8, C0), F32),
        pltpu.VMEM((49, 8, C1), F32),
        pltpu.VMEM((49, 8, C1), F32),
        pltpu.VMEM((TILES * SIDE0 * 8, CELLS0), BF16),
        pltpu.VMEM((TILES * SIDE1 * 8, CELLS1), BF16),
        pltpu.VMEM((2, RIM0, CELLS0), BF16),
        pltpu.VMEM((2 * RIM1, CELLS1), BF16),
        pltpu.VMEM((2 * RIM0, CELLS0), BF16),
        pltpu.VMEM((CELLS0, 2 * CELLS1), BF16),
        pltpu.VMEM((CELLS1 + 2 * RIM1, CELLS0), BF16),
        pltpu.VMEM((2 * RIM0, 2 * CELLS1), BF16),
        pltpu.VMEM((TILES, SIDE0 + 6, 32, C0), F32),
        pltpu.VMEM((TILES, SIDE1 + 6, 24, C1), F32),
        pltpu.VMEM((2, TILES, 3, 32, C0), F32),
        pltpu.VMEM((2, TILES, 3, 24, C1), F32),
        pltpu.VMEM((TILES, SIDE0, SIDE0, C0), F32),
        pltpu.VMEM((TILES, SIDE1, SIDE1, C1), F32),
        pltpu.VMEM((TILES, 2, 3, SIDE0, C0), F32),
        pltpu.VMEM((TILES, 2, 3, SIDE0, C0), F32),
        pltpu.VMEM((TILES, SIDE0, SIDE0, C0), BF16),
        pltpu.VMEM((TILES, SIDE0, SIDE0, C0), BF16),
        pltpu.VMEM((CELLS0, C0), F32),
        pltpu.VMEM((2 * RIM0, C0), F32),
        pltpu.VMEM((2, CELLS1, C1), F32),
        pltpu.VMEM((8, 256), jnp.int32),
        pltpu.VMEM((2, 8, 256), jnp.int32),
        pltpu.VMEM((STEPS, ROWS, CELLS0), BF16),
        pltpu.VMEM((STEPS, 2, ROWS, CELLS0), BF16),
        pltpu.VMEM((STEPS, 2, RIM0, C0), BF16),
        pltpu.VMEM((STEPS, 2, RIM0, C0), BF16),
        pltpu.VMEM((2 * STEPS, 2, RIM1, C1), BF16),
        pltpu.VMEM((2 * STEPS, 2, RIM1, C1), BF16),
        pltpu.SemaphoreType.DMA((2 + WEIGHTS,)),
        pltpu.SemaphoreType.DMA((4,)),
        pltpu.SemaphoreType.DMA((4,)),
        pltpu.SemaphoreType.DMA((STEPS,)),
        pltpu.SemaphoreType.DMA((STEPS,)),
        pltpu.SemaphoreType.DMA((2,)),
        pltpu.SemaphoreType.DMA((2,)),
        pltpu.SemaphoreType.DMA((STEPS, 2)),
        pltpu.SemaphoreType.DMA((STEPS, 2)),
        pltpu.SemaphoreType.DMA((STEPS, 2)),
        pltpu.SemaphoreType.DMA((STEPS, 2)),
        pltpu.SemaphoreType.DMA((2 * STEPS, 2)),
        pltpu.SemaphoreType.DMA((2 * STEPS, 2)),
    ]
    return pl.pallas_call(
        kernel,
        out_shape=(
            jax.ShapeDtypeStruct((STEPS, 1, FIELDS, CELLS0), F32),
            jax.ShapeDtypeStruct((1, C1, CELLS1), F32),
        ),
        in_specs=[hbm, hbm, smem, smem] + [hbm] * len(weights),
        out_specs=(pl.BlockSpec(memory_space=pltpu.VMEM),) * 2,
        scratch_shapes=scratch,
        compiler_params=pltpu.CompilerParams(
            collective_id=0, has_side_effects=True, vmem_limit_bytes=56 * 1024 * 1024
        ),
    )(states.transpose(1, 0, 2), gru_state.transpose(1, 0, 2), neighbours, orient, *weights)


def solution(mesh):
    in_specs = (
        P("segment", None, "face"),
        P("segment", None, "face"),
        P("face", None),
        P("face", None),
    ) + (P(),) * 18
    out_specs = (P(None, "segment", None, "face"), P("segment", None, "face"))
    return jax.shard_map(local, mesh=mesh, in_specs=in_specs, out_specs=out_specs, check_vma=False)
```

```python
import jax
import jax.numpy as jnp
from jax import lax
from jax.experimental import pallas as pl
from jax.experimental.pallas import tpu as pltpu
from jax.sharding import PartitionSpec as P

FIELDS = 9
C0 = 90
C1 = 180
SIDE0 = 16
SIDE1 = 8
TILES = 2
STEPS = 2
CELLS0 = TILES * SIDE0 * SIDE0
CELLS1 = TILES * SIDE1 * SIDE1
RIM0 = TILES * 3 * SIDE0
RIM1 = TILES * 3 * SIDE1
ROWS = 16
F32, BF16 = jnp.float32, jnp.bfloat16
NORTH, EAST, SOUTH, WEST = range(4)
ROW = 16


def dot_nt(a, b):
    return lax.dot_general(a, b, (((1,), (1,)), ((), ())), preferred_element_type=F32)


def dot_nn(a, b):
    return jnp.dot(a, b, preferred_element_type=F32)


def one_hot(index, cells, axis):
    shape = (index.shape[0], cells) if axis == 1 else (cells, index.shape[1])
    hit = lax.broadcasted_iota(jnp.int32, shape, axis) == index
    return jnp.where(hit, 1.0, 0.0)


def rim_line(nbr, orient, tile, side, p):
    o = orient[tile, p]
    from_side = lax.shift_right_logical(o, 1)
    per_depth = jnp.where(
        from_side == 0, side, jnp.where(from_side == 1, -1, jnp.where(from_side == 2, -side, 1))
    )
    base = jnp.where(from_side == 1, side - 1, jnp.where(from_side == 2, side * (side - 1), 0))
    per_step = jnp.where((from_side & 1) == 0, 1, side)
    turned = (o & 1) == 1
    base = base + jnp.where(turned, per_step * (side - 1), 0)
    per_step = jnp.where(turned, -per_step, per_step)
    return base + (nbr[tile, p] & 1) * side * side, per_depth, per_step


def far_index(m, nbr, orient, side, p):
    index = jnp.full(m.shape, -1, jnp.int32)
    for tile in range(TILES):
        base, per_depth, per_step = rim_line(nbr, orient, tile, side, p)
        local = m - tile * 3 * side
        row = jnp.where(local >= 2 * side, 2, jnp.where(local >= side, 1, 0))
        depth = 2 - row if p == NORTH else row
        value = base + per_depth * depth + per_step * (local - row * side)
        index = jnp.where((local >= 0) & (local < 3 * side), value, index)
    return index


def near_index(m, nbr, orient, side):
    index = jnp.full(m.shape, -1, jnp.int32)
    for tile in range(TILES):
        base_e, depth_e, step_e = rim_line(nbr, orient, tile, side, EAST)
        base_w, depth_w, step_w = rim_line(nbr, orient, tile, side, WEST)
        local = m - tile * side * 8
        row, place = lax.shift_right_arithmetic(local, 3), local & 7
        east = base_e + depth_e * place + step_e * row
        west = base_w + depth_w * (7 - place) + step_w * row
        value = jnp.where(place < 3, east, jnp.where(place >= 5, west, -1))
        index = jnp.where((local >= 0) & (local < 8 * side), value, index)
    return index


def host_of(segment, block, size):
    core, odd = segment & 1, block & 1
    face = block - odd + (1 - core)
    last = lax.rem(block, ROW) == ROW - 1
    return segment - core + (1 - odd), jnp.where(last, lax.rem(face + ROW, size), face)


def block_of(segment, face, size):
    core, odd = segment & 1, face & 1
    block = face - odd + (1 - core)
    last = lax.rem(block, ROW) == ROW - 1
    return segment - core + (1 - odd), jnp.where(last, lax.rem(block + size - ROW, size), block)


def spread_taps(weight):
    return jnp.broadcast_to(weight.astype(F32)[:, None, :], (49, 8, weight.shape[1]))


def halves(x):
    high = x.astype(BF16)
    return jnp.concatenate([high, (x - high.astype(F32)).astype(BF16)], 0)


def normalise(y, channels):
    centred = y - jnp.sum(y, 1, keepdims=True) * (1.0 / channels)
    var = jnp.sum(centred * centred, 1, keepdims=True) * (1.0 / channels)
    return (centred * lax.rsqrt(var + 1e-6)).astype(BF16)


def gelu(x):
    return (0.5 * x) * (1.0 + lax.erf(x * 0.7071067811865476))


def finish(y, r, expand, shrink):
    normed = normalise(y, y.shape[1])
    expanded = gelu(dot_nn(normed, expand)).astype(BF16)
    return (r + dot_nt(expanded, shrink)).astype(BF16)


def conv_tile(pad, tile, rows, first, taps):
    total = None
    for q in range(7):
        x = pad[tile, :, first + q - 3 : first + q + 5, :]
        for u in range(7):
            term = taps[7 * u + q][None] * x[u : u + rows]
            total = term if total is None else total + term
    return total


def conv_halo(halo, side, tile, first, taps, rows):
    rows = list(rows)
    for q in range(7):
        for h in range(3):
            x = halo[side, tile, h, first + q - 3 : first + q + 5, :]
            for o in range(3):
                u = h - o if side == 0 else 6 + h - o
                if 0 <= u <= 6:
                    rows[o] = rows[o] + taps[7 * u + q] * x
    return rows


WEIGHTS = 18


def kernel(
    states, gru_state, nbr_hbm, orient_hbm, *refs,
):
    hbm_weights, refs = refs[:WEIGHTS], refs[WEIGHTS:]
    forecast, gru_final = refs[:2]
    (
        embed_w, ef_depth, ef_expand, ef_shrink, down_w, ec_depth, ec_expand, ec_shrink,
        gru_w, dc_depth, dc_expand, dc_shrink, up_w, combine_w, df_depth, df_expand,
        df_shrink, head_w,
    ) = vmem_weights = refs[2 : 2 + WEIGHTS]
    (
        nbr, orient, states_in, gru_in, states_moved, gru_moved, info_moved,
        result_out, gru_out,
        weather, carried, embed, gru_a, gru_b, lift_w, comb_b,
        taps_ef, taps_df, taps_ec, taps_dc,
        near0, near1, own_far, far1, far0, grow, pool, far_pool, far_grow,
        pad0, pad1, halo0, halo1, y0, y1, edge_y, edge_r, skip, merged,
        part, far_part, held_gates,
        info_out, info_in, w_out, w_in, f_out, f_in, c_out, c_in,
        load, store,
        m_send, m_recv, r_send, r_recv, info_send, info_recv, w_send, w_recv, f_send, f_recv, c_send, c_recv,
    ) = refs[2 + WEIGHTS :]
    size = lax.axis_size("face")
    here = lax.axis_index("segment"), lax.axis_index("face")
    mine = block_of(*here, size)
    away = host_of(*here, size)
    moved = (away[0] != here[0]) | (away[1] != here[1])

    def beside(place, step):
        return place[0], lax.rem(place[1] + step + size, size)

    home_after, home_before = beside(mine, 1), beside(mine, -1)
    after, before = host_of(*home_after, size), host_of(*home_before, size)
    odd = (mine[1] & 1) == 1
    far = jnp.where(odd, 0, 1)
    ways = (
        (far, tuple(jnp.where(odd, a, b) for a, b in zip(after, before))),
        (1 - far, tuple(jnp.where(odd, b, a) for a, b in zip(after, before))),
    )
    first_targets = host_of(*beside(here, 1), size), host_of(*beside(here, -1), size)

    def greet(target):
        pl.semaphore_signal(
            barrier, inc=1, device_id={"segment": target[0], "face": target[1]},
            device_id_type=pl.DeviceIdType.MESH,
        )

    def remote(src, dst, send, recv, target):
        return pltpu.make_async_remote_copy(
            src_ref=src, dst_ref=dst, send_sem=send, recv_sem=recv,
            device_id={"segment": target[0], "face": target[1]},
            device_id_type=pl.DeviceIdType.MESH,
        )

    def pair(out, into, send, recv, slot):
        return [
            remote(out.at[slot, w], into.at[slot, w], send.at[slot, w], recv.at[slot, w], target)
            for w, target in ways
        ]

    def info_copies():
        return [
            remote(info_out, info_in.at[w], info_send.at[w], info_recv.at[w], target)
            for w, target in enumerate(first_targets)
        ]

    def weather_copies(step, ways):
        return [
            remote(w_out.at[step], w_in.at[step, w], w_send.at[step, w], w_recv.at[step, w], target)
            for w, target in ways
        ]

    def state_copy():
        return remote(states_in, states_moved, m_send.at[0], m_recv.at[0], away)

    def own_info_copy():
        return remote(info_out, info_moved, m_send.at[1], m_recv.at[1], away)

    def gru_copy():
        return remote(gru_in, gru_moved, m_send.at[2], m_recv.at[2], away)

    def result_copy(step):
        return remote(
            result_out.at[step], forecast.at[step, 0], r_send.at[step], r_recv.at[step], mine
        )

    def gru_result_copy():
        return remote(gru_out, gru_final.at[0], m_send.at[3], m_recv.at[3], mine)

    def result_store(step):
        return pltpu.make_async_copy(result_out.at[step], forecast.at[step, 0], store.at[step])

    def gru_result_store():
        return pltpu.make_async_copy(gru_out, gru_final.at[0], store.at[STEPS])

    def start(copies):
        for copy in copies:
            copy.start()

    def wait(copies):
        for copy in copies:
            copy.wait()

    barrier = pltpu.get_barrier_semaphore()
    for target in (home_after, home_before, after, before):
        greet(target)

    @pl.when(moved)
    def _():
        greet(mine)
        greet(away)

    loads = [
        pltpu.make_async_copy(nbr_hbm, nbr, load.at[2 + WEIGHTS]),
        pltpu.make_async_copy(orient_hbm, orient, load.at[3 + WEIGHTS]),
        pltpu.make_async_copy(states, states_in, load.at[0]),
    ]
    loads += [
        pltpu.make_async_copy(src, dst, load.at[2 + n])
        for n, (src, dst) in enumerate(zip(hbm_weights, vmem_weights))
    ]
    loads.append(pltpu.make_async_copy(gru_state, gru_in, load.at[1]))
    start(loads)

    loads[0].wait()
    loads[1].wait()
    lane = lax.broadcasted_iota(jnp.int32, (1, 256), 1)
    for row, p in ((0, NORTH), (2, SOUTH)):
        info_out[row : row + 1] = far_index(lane, nbr, orient, SIDE0, p)
        info_out[row + 1 : row + 2] = far_index(lane, nbr, orient, SIDE1, p)
    info_out[4:5] = near_index(lane, nbr, orient, SIDE0)
    info_out[5:6] = near_index(lane, nbr, orient, SIDE1)
    info_out[6:8] = jnp.zeros((2, 256), jnp.int32)
    weather[...] = jnp.zeros_like(weather)
    loads[2].wait()
    weather[:FIELDS] = states_in[:, 0, :]
    w_out[0] = weather[...].astype(BF16)
    pl.semaphore_wait(barrier, jnp.where(moved, 6, 4))

    @pl.when(moved)
    def _():
        own_info_copy().start()
        state_copy().start()

    start(weather_copies(0, tuple(enumerate(first_targets))))
    start(info_copies())

    def coarse_of(cell):
        tile = lax.shift_right_logical(cell, 8)
        row = lax.shift_right_logical(cell, 5) & 7
        return tile * 64 + row * 8 + (lax.shift_right_logical(cell, 1) & 7)

    pad0[...] = jnp.zeros_like(pad0)
    halo0[...] = jnp.zeros_like(halo0)
    pad1[...] = jnp.zeros_like(pad1)
    halo1[...] = jnp.zeros_like(halo1)
    cell = lax.broadcasted_iota(jnp.int32, (CELLS0, 1), 0)
    one = one_hot(coarse_of(cell), CELLS1, 1).astype(BF16)
    grow[:, :CELLS1] = one
    grow[:, CELLS1:] = one
    cell = lax.broadcasted_iota(jnp.int32, (1, CELLS0), 1)
    pool[...] = (0.25 * one_hot(coarse_of(cell), CELLS1, 0)).astype(BF16)
    for copy in loads[3:]:
        copy.wait()

    @pl.when(moved)
    def _():
        gru_copy().start()

    embed[...] = jnp.zeros_like(embed)
    embed[:FIELDS] = embed_w[...].astype(F32)
    taps_ef[...] = spread_taps(ef_depth[...])
    taps_df[...] = spread_taps(df_depth[...])
    taps_ec[...] = spread_taps(ec_depth[...])
    taps_dc[...] = spread_taps(dc_depth[...])
    for g in range(3):
        wide = gru_w[g].astype(F32)
        gru_a[g] = wide[:, :C1].astype(BF16)
        gru_b[g] = wide[:, C1:].astype(BF16)
    wide = combine_w[...].astype(F32)
    comb_b[...] = wide[C0:].astype(BF16)
    lift_w[...] = dot_nn(up_w[...], wide[:C0].astype(BF16)).astype(BF16)

    @pl.when(moved)
    def _():
        own_info_copy().wait()

    @pl.when(jnp.logical_not(moved))
    def _():
        info_moved[...] = info_out[...]

    near0[...] = one_hot(info_moved[4:5], CELLS0, 0).T.astype(BF16)
    for way in range(2):
        wanted = info_moved[2 * way : 2 * way + 1, :128]
        own_far[way] = one_hot(wanted, CELLS0, 0).T[:RIM0].astype(BF16)

    @pl.when(moved)
    def _():
        state_copy().wait()
        weather[:FIELDS] = states_moved[:, 0, :]

    def prepare_gather():
        for way in range(2):
            wanted = info_in[1 - way, 2 * way + 1 : 2 * way + 2, :128]
            far1[way] = one_hot(wanted, CELLS1, 0).T[:RIM1].astype(BF16)
            far_pool[way] = dot_nn(far1[way], pool[...]).astype(BF16)

    def prepare_rest():
        for way in range(2):
            wanted = info_in[1 - way, 2 * way : 2 * way + 1, :128]
            far0[way] = one_hot(wanted, CELLS0, 0).T[:RIM0].astype(BF16)
            one = dot_nn(far0[way], grow[:, :CELLS1]).astype(BF16)
            far_grow[way, :, :CELLS1] = one
            far_grow[way, :, CELLS1:] = one

        @pl.when(moved)
        def _():
            gru_copy().wait()
            gru_in[...] = gru_moved[...]

        state = jnp.concatenate(
            [gru_in[...].reshape(C1, CELLS1), jnp.zeros((256 - C1, CELLS1), F32)], 0
        )
        carried[...] = state.T[:, :C1]

    def fill0(r):
        pad0[:, 3 : 3 + SIDE0, 8:24, :] = r.astype(F32).reshape(TILES, SIDE0, SIDE0, C0)
        sides = dot_nn(near0[...], r).reshape(TILES, SIDE0, 8, C0)
        pad0[:, 3 : 3 + SIDE0, 0:8, :] = sides
        pad0[:, 3 : 3 + SIDE0, 24:32, :] = sides

    def fill1(r):
        pad1[:, 3 : 3 + SIDE1, 8:16, :] = r.astype(F32).reshape(TILES, SIDE1, SIDE1, C1)
        sides = dot_nn(near1[...], r).reshape(TILES, SIDE1, 8, C1)
        pad1[:, 3 : 3 + SIDE1, 0:8, :] = sides
        pad1[:, 3 : 3 + SIDE1, 16:24, :] = sides

    def fine_block_inner(taps, expand, shrink, out):
        def body(tile, _):
            for half in range(2):
                total = conv_tile(pad0, tile, SIDE0, 8 + 8 * half, taps)
                y0[tile, :, 8 * half : 8 * half + 8, :] = total
            y = y0[tile, 3:13].reshape(10 * SIDE0, C0)
            r = pad0[tile, 6:16, 8:24, :].reshape(10 * SIDE0, C0)
            out[tile, 3:13] = finish(y, r, expand[...], shrink[...]).reshape(10, SIDE0, C0)
            return 0

        lax.fori_loop(0, TILES, body, 0, unroll=True)
        for tile in range(TILES):
            for side, top in ((0, 3), (1, 16)):
                edge_r[tile, side] = pad0[tile, top : top + 3, 8:24, :]

    def fine_block_outer(taps, expand, shrink, out):
        def body(tile, _):
            for side, top in ((0, 0), (1, 13)):
                for half in range(2):
                    columns = slice(8 * half, 8 * half + 8)
                    rows = [y0[tile, top + o, columns, :] for o in range(3)]
                    rows = conv_halo(halo0, side, tile, 8 + 8 * half, taps, rows)
                    for o in range(3):
                        edge_y[tile, side, o, columns, :] = rows[o]
            return 0

        lax.fori_loop(0, TILES, body, 0, unroll=True)
        y = edge_y[...].reshape(2 * RIM0, C0)
        r = edge_r[...].reshape(2 * RIM0, C0)
        done = finish(y, r, expand[...], shrink[...]).reshape(TILES, 2, 3, SIDE0, C0)
        for tile in range(TILES):
            out[tile, 0:3] = done[tile, 0]
            out[tile, 13:16] = done[tile, 1]

    def coarse_block(r, slot, copies, taps, expand, shrink, meanwhile):
        fill1(r)

        def body(tile, _):
            y1[tile] = conv_tile(pad1, tile, SIDE1, 8, taps)
            return 0

        lax.fori_loop(0, TILES, body, 0, unroll=True)
        meanwhile()
        wait(copies)
        for way in range(2):
            arrived = c_in[slot, way].astype(F32).reshape(TILES, 3, SIDE1, C1)
            halo1[way, :, :, 8:16, :] = arrived

        def edge(tile, _):
            for side, top in ((0, 0), (1, 5)):
                rows = [y1[tile, top + o] for o in range(3)]
                rows = conv_halo(halo1, side, tile, 8, taps, rows)
                for o in range(3):
                    y1[tile, top + o] = rows[o]
            return 0

        lax.fori_loop(0, TILES, edge, 0, unroll=True)
        y = y1[...].reshape(CELLS1, C1)
        return finish(y, r.astype(F32), expand[...], shrink[...])

    def step_body(step, _):
        fields = weather[...].astype(BF16).astype(F32).T.astype(BF16)
        lift = embed[...].astype(BF16)
        fill0(dot_nn(fields, lift).astype(BF16))
        fine_block_inner(taps_ef, ef_expand, ef_shrink, skip)

        @pl.when(step == 0)
        def _():
            near1[...] = one_hot(info_moved[5:6, :128], CELLS1, 0).T.astype(BF16)
            wait(info_copies())
            prepare_gather()

        wait(weather_copies(step, ways))
        for way in range(2):
            rim = dot_nt(own_far[way], w_in[step, way]).astype(BF16)
            rim = dot_nn(rim, lift).astype(BF16).astype(F32)
            halo0[way, :, :, 8:24, :] = rim.reshape(TILES, 3, SIDE0, C0)
        fine_block_outer(taps_ef, ef_expand, ef_shrink, skip)

        kept = skip[...].reshape(CELLS0, C0)
        copies = pair(c_out, c_in, c_send, c_recv, 2 * step)
        for (way, _), copy in zip(ways, copies):
            wanted = dot_nn(far_pool[way], kept).astype(BF16)
            c_out[2 * step, way] = dot_nt(wanted, down_w[...]).astype(BF16)
            copy.start()
        coarse = dot_nn(pool[...], kept).astype(BF16)
        coarse = dot_nt(coarse, down_w[...]).astype(BF16)

        def after_skip():
            @pl.when(step == 0)
            def _():
                prepare_rest()

            kept = skip[...].reshape(CELLS0, C0)
            part[...] = dot_nn(kept, comb_b[...])
            for way in range(2):
                far_part[way] = dot_nn(dot_nn(far0[way], kept).astype(BF16), comb_b[...])
            held = carried[...].astype(BF16)
            for g in range(2):
                held_gates[g] = dot_nt(held, gru_b[g])

        coarse = coarse_block(
            coarse, 2 * step, copies, taps_ec, ec_expand, ec_shrink, after_skip
        )

        old = carried[...]
        update = jax.nn.sigmoid(dot_nt(coarse, gru_a[0]) + held_gates[0])
        reset = jax.nn.sigmoid(dot_nt(coarse, gru_a[1]) + held_gates[1])
        gated = (reset * old).astype(BF16)
        candidate = jnp.tanh(dot_nt(coarse, gru_a[2]) + dot_nt(gated, gru_b[2]))
        new = (1.0 - update) * old + update * candidate
        carried[...] = new

        new = new.astype(BF16)
        copies = pair(c_out, c_in, c_send, c_recv, 2 * step + 1)
        for (way, _), copy in zip(ways, copies):
            c_out[2 * step + 1, way] = dot_nn(far1[way], new).astype(BF16)
            copy.start()

        def after_update():
            @pl.when(step == STEPS - 1)
            def _():
                last = jnp.concatenate([carried[...], jnp.zeros((CELLS1, 256 - C1), F32)], 1)
                gru_out[...] = last.T[:C1]

                @pl.when(moved)
                def _():
                    gru_result_copy().start()

                @pl.when(jnp.logical_not(moved))
                def _():
                    gru_result_store().start()

        decoded = coarse_block(
            new, 2 * step + 1, copies, taps_dc, dc_expand, dc_shrink, after_update
        )

        lifted = halves(dot_nn(decoded, lift_w[...]))
        copies = pair(f_out, f_in, f_send, f_recv, step)
        for (way, _), copy in zip(ways, copies):
            f_out[step, way] = (dot_nn(far_grow[way], lifted) + far_part[way]).astype(BF16)
            copy.start()
        fill0((dot_nn(grow[...], lifted) + part[...]).astype(BF16))
        fine_block_inner(taps_df, df_expand, df_shrink, merged)
        wait(copies)
        for way in range(2):
            arrived = f_in[step, way].astype(F32).reshape(TILES, 3, SIDE0, C0)
            halo0[way, :, :, 8:24, :] = arrived
        fine_block_outer(taps_df, df_expand, df_shrink, merged)

        change = dot_nt(head_w[...], merged[...].reshape(CELLS0, C0))
        now = weather[:FIELDS] + change
        weather[:FIELDS] = now

        @pl.when(step < STEPS - 1)
        def _():
            w_out[step + 1] = weather[...].astype(BF16)
            start(weather_copies(step + 1, ways))

        result_out[step] = now

        @pl.when(moved)
        def _():
            result_copy(step).start()

        @pl.when(jnp.logical_not(moved))
        def _():
            result_store(step).start()

        return 0

    lax.fori_loop(0, STEPS, step_body, 0)

    @pl.when(moved)
    def _():
        gru_result_copy().wait()
        for step in range(STEPS):
            result_copy(step).wait()

    @pl.when(jnp.logical_not(moved))
    def _():
        gru_result_store().wait()
        for step in range(STEPS):
            result_store(step).wait()


def local(states, gru_state, neighbours, orient, *weights):
    (
        embed_w, ef_depth, ef_expand, ef_shrink, down_w, ec_depth, ec_expand, ec_shrink,
        gru_w, dc_depth, dc_expand, dc_shrink, up_w, combine_w, df_depth, df_expand,
        df_shrink, head_w,
    ) = weights
    weights = (
        embed_w.T, ef_depth.T, ef_expand.T, ef_shrink, down_w, ec_depth.T, ec_expand.T, ec_shrink,
        gru_w, dc_depth.T, dc_expand.T, dc_shrink, up_w.T, combine_w.T, df_depth.T, df_expand.T,
        df_shrink, head_w,
    )
    hbm = pl.BlockSpec(memory_space=pltpu.HBM)
    scratch = [pltpu.VMEM(w.shape, w.dtype) for w in weights]
    scratch += [
        pltpu.SMEM((TILES, 4), jnp.int32),
        pltpu.SMEM((TILES, 4), jnp.int32),
        pltpu.VMEM((FIELDS, 1, CELLS0), F32),
        pltpu.VMEM((C1, 1, CELLS1), F32),
        pltpu.VMEM((FIELDS, 1, CELLS0), F32),
        pltpu.VMEM((C1, 1, CELLS1), F32),
        pltpu.VMEM((8, 256), jnp.int32),
        pltpu.VMEM((STEPS, FIELDS, CELLS0), F32),
        pltpu.VMEM((C1, CELLS1), F32),
        pltpu.VMEM((ROWS, CELLS0), F32),
        pltpu.VMEM((CELLS1, C1), F32),
        pltpu.VMEM((ROWS, C0), F32),
        pltpu.VMEM((3, C1, C1), BF16),
        pltpu.VMEM((3, C1, C1), BF16),
        pltpu.VMEM((C1, C0), BF16),
        pltpu.VMEM((C0, C0), BF16),
        pltpu.VMEM((49, 8, C0), F32),
        pltpu.VMEM((49, 8, C0), F32),
        pltpu.VMEM((49, 8, C1), F32),
        pltpu.VMEM((49, 8, C1), F32),
        pltpu.VMEM((TILES * SIDE0 * 8, CELLS0), BF16),
        pltpu.VMEM((TILES * SIDE1 * 8, CELLS1), BF16),
        pltpu.VMEM((2, RIM0, CELLS0), BF16),
        pltpu.VMEM((2, RIM1, CELLS1), BF16),
        pltpu.VMEM((2, RIM0, CELLS0), BF16),
        pltpu.VMEM((CELLS0, 2 * CELLS1), BF16),
        pltpu.VMEM((CELLS1, CELLS0), BF16),
        pltpu.VMEM((2, RIM1, CELLS0), BF16),
        pltpu.VMEM((2, RIM0, 2 * CELLS1), BF16),
        pltpu.VMEM((TILES, SIDE0 + 6, 32, C0), F32),
        pltpu.VMEM((TILES, SIDE1 + 6, 24, C1), F32),
        pltpu.VMEM((2, TILES, 3, 32, C0), F32),
        pltpu.VMEM((2, TILES, 3, 24, C1), F32),
        pltpu.VMEM((TILES, SIDE0, SIDE0, C0), F32),
        pltpu.VMEM((TILES, SIDE1, SIDE1, C1), F32),
        pltpu.VMEM((TILES, 2, 3, SIDE0, C0), F32),
        pltpu.VMEM((TILES, 2, 3, SIDE0, C0), F32),
        pltpu.VMEM((TILES, SIDE0, SIDE0, C0), BF16),
        pltpu.VMEM((TILES, SIDE0, SIDE0, C0), BF16),
        pltpu.VMEM((CELLS0, C0), F32),
        pltpu.VMEM((2, RIM0, C0), F32),
        pltpu.VMEM((2, CELLS1, C1), F32),
        pltpu.VMEM((8, 256), jnp.int32),
        pltpu.VMEM((2, 8, 256), jnp.int32),
        pltpu.VMEM((STEPS, ROWS, CELLS0), BF16),
        pltpu.VMEM((STEPS, 2, ROWS, CELLS0), BF16),
        pltpu.VMEM((STEPS, 2, RIM0, C0), BF16),
        pltpu.VMEM((STEPS, 2, RIM0, C0), BF16),
        pltpu.VMEM((2 * STEPS, 2, RIM1, C1), BF16),
        pltpu.VMEM((2 * STEPS, 2, RIM1, C1), BF16),
        pltpu.SemaphoreType.DMA((4 + WEIGHTS,)),
        pltpu.SemaphoreType.DMA((STEPS + 1,)),
        pltpu.SemaphoreType.DMA((4,)),
        pltpu.SemaphoreType.DMA((4,)),
        pltpu.SemaphoreType.DMA((STEPS,)),
        pltpu.SemaphoreType.DMA((STEPS,)),
        pltpu.SemaphoreType.DMA((2,)),
        pltpu.SemaphoreType.DMA((2,)),
        pltpu.SemaphoreType.DMA((STEPS, 2)),
        pltpu.SemaphoreType.DMA((STEPS, 2)),
        pltpu.SemaphoreType.DMA((STEPS, 2)),
        pltpu.SemaphoreType.DMA((STEPS, 2)),
        pltpu.SemaphoreType.DMA((2 * STEPS, 2)),
        pltpu.SemaphoreType.DMA((2 * STEPS, 2)),
    ]
    return pl.pallas_call(
        kernel,
        out_shape=(
            jax.ShapeDtypeStruct((STEPS, 1, FIELDS, CELLS0), F32),
            jax.ShapeDtypeStruct((1, C1, CELLS1), F32),
        ),
        in_specs=[hbm] * (4 + len(weights)),
        out_specs=(hbm, hbm),
        scratch_shapes=scratch,
        compiler_params=pltpu.CompilerParams(
            collective_id=0, has_side_effects=True, vmem_limit_bytes=56 * 1024 * 1024
        ),
    )(states.transpose(1, 0, 2), gru_state.transpose(1, 0, 2), neighbours, orient, *weights)


def solution(mesh):
    in_specs = (
        P("segment", None, "face"),
        P("segment", None, "face"),
        P("face", None),
        P("face", None),
    ) + (P(),) * 18
    out_specs = (P(None, "segment", None, "face"), P("segment", None, "face"))
    return jax.shard_map(local, mesh=mesh, in_specs=in_specs, out_specs=out_specs, check_vma=False)
```

```python
import jax
import jax.numpy as jnp
from jax import lax
from jax.experimental import pallas as pl
from jax.experimental.pallas import tpu as pltpu
from jax.sharding import PartitionSpec as P

FIELDS = 9
C0 = 90
C1 = 180
SIDE0 = 16
SIDE1 = 8
TILES = 2
STEPS = 2
CELLS0 = TILES * SIDE0 * SIDE0
CELLS1 = TILES * SIDE1 * SIDE1
RIM0 = TILES * 3 * SIDE0
RIM1 = TILES * 3 * SIDE1
ROWS = 16
F32, BF16 = jnp.float32, jnp.bfloat16
NORTH, EAST, SOUTH, WEST = range(4)
ROW = 16


def dot_nt(a, b):
    return lax.dot_general(a, b, (((1,), (1,)), ((), ())), preferred_element_type=F32)


def dot_nn(a, b):
    return jnp.dot(a, b, preferred_element_type=F32)


def one_hot(index, cells, axis):
    shape = (index.shape[0], cells) if axis == 1 else (cells, index.shape[1])
    hit = lax.broadcasted_iota(jnp.int32, shape, axis) == index
    return jnp.where(hit, 1.0, 0.0)


def rim_line(nbr, orient, tile, side, p):
    o = orient[tile, p]
    from_side = lax.shift_right_logical(o, 1)
    per_depth = jnp.where(
        from_side == 0, side, jnp.where(from_side == 1, -1, jnp.where(from_side == 2, -side, 1))
    )
    base = jnp.where(from_side == 1, side - 1, jnp.where(from_side == 2, side * (side - 1), 0))
    per_step = jnp.where((from_side & 1) == 0, 1, side)
    turned = (o & 1) == 1
    base = base + jnp.where(turned, per_step * (side - 1), 0)
    per_step = jnp.where(turned, -per_step, per_step)
    return base + (nbr[tile, p] & 1) * side * side, per_depth, per_step


def far_index(m, nbr, orient, side, p):
    index = jnp.full(m.shape, -1, jnp.int32)
    for tile in range(TILES):
        base, per_depth, per_step = rim_line(nbr, orient, tile, side, p)
        local = m - tile * 3 * side
        row = jnp.where(local >= 2 * side, 2, jnp.where(local >= side, 1, 0))
        depth = 2 - row if p == NORTH else row
        value = base + per_depth * depth + per_step * (local - row * side)
        index = jnp.where((local >= 0) & (local < 3 * side), value, index)
    return index


def near_index(m, nbr, orient, side):
    index = jnp.full(m.shape, -1, jnp.int32)
    for tile in range(TILES):
        base_e, depth_e, step_e = rim_line(nbr, orient, tile, side, EAST)
        base_w, depth_w, step_w = rim_line(nbr, orient, tile, side, WEST)
        local = m - tile * side * 8
        row, place = lax.shift_right_arithmetic(local, 3), local & 7
        east = base_e + depth_e * place + step_e * row
        west = base_w + depth_w * (7 - place) + step_w * row
        value = jnp.where(place < 3, east, jnp.where(place >= 5, west, -1))
        index = jnp.where((local >= 0) & (local < 8 * side), value, index)
    return index


def host_of(segment, block, size):
    core, odd = segment & 1, block & 1
    face = block - odd + (1 - core)
    last = lax.rem(block, ROW) == ROW - 1
    return segment - core + (1 - odd), jnp.where(last, lax.rem(face + ROW, size), face)


def block_of(segment, face, size):
    core, odd = segment & 1, face & 1
    block = face - odd + (1 - core)
    last = lax.rem(block, ROW) == ROW - 1
    return segment - core + (1 - odd), jnp.where(last, lax.rem(block + size - ROW, size), block)


def spread_taps(weight):
    return jnp.broadcast_to(weight.astype(F32)[:, None, :], (49, 8, weight.shape[1]))


def halves(x):
    high = x.astype(BF16)
    return jnp.concatenate([high, (x - high.astype(F32)).astype(BF16)], 0)


def normalise(y, channels):
    centred = y - jnp.sum(y, 1, keepdims=True) * (1.0 / channels)
    var = jnp.sum(centred * centred, 1, keepdims=True) * (1.0 / channels)
    return (centred * lax.rsqrt(var + 1e-6)).astype(BF16)


def gelu(x):
    return (0.5 * x) * (1.0 + lax.erf(x * 0.7071067811865476))


def finish(y, r, expand, shrink):
    normed = normalise(y, y.shape[1])
    expanded = gelu(dot_nn(normed, expand)).astype(BF16)
    return (r + dot_nt(expanded, shrink)).astype(BF16)


def conv_tile(pad, tile, rows, first, taps):
    total = [None] * rows
    for q in range(7):
        x = pad[tile, 3 : 3 + rows, first + q - 3 : first + q + 5, :]
        for u in range(7):
            low, high = max(0, 3 - u), min(rows, rows + 3 - u)
            term = taps[7 * u + q][None] * x[low + u - 3 : high + u - 3]
            for o in range(low, high):
                one = term[o - low]
                total[o] = one if total[o] is None else total[o] + one
    return jnp.stack(total, 0)


def conv_halo(halo, side, tile, first, taps, rows):
    rows = list(rows)
    for q in range(7):
        for h in range(3):
            x = halo[side, tile, h, first + q - 3 : first + q + 5, :]
            for o in range(3):
                u = h - o if side == 0 else 6 + h - o
                if 0 <= u <= 6:
                    rows[o] = rows[o] + taps[7 * u + q] * x
    return rows


WEIGHTS = 18


def kernel(
    states, gru_state, nbr_hbm, orient_hbm, *refs,
):
    hbm_weights, refs = refs[:WEIGHTS], refs[WEIGHTS:]
    forecast, gru_final = refs[:2]
    (
        embed_w, ef_depth, ef_expand, ef_shrink, down_w, ec_depth, ec_expand, ec_shrink,
        gru_w, dc_depth, dc_expand, dc_shrink, up_w, combine_w, df_depth, df_expand,
        df_shrink, head_w,
    ) = vmem_weights = refs[2 : 2 + WEIGHTS]
    (
        nbr, orient, states_in, gru_in, states_moved, gru_moved, info_moved,
        result_out, gru_out,
        weather, carried, embed, gru_a, gru_b, lift_w, comb_b,
        taps_ef, taps_df, taps_ec, taps_dc,
        near0, near1, own_far, far1, far0, grow, pool, far_pool, far_grow,
        pad0, pad1, halo0, halo1, y0, y1, edge_y, edge_r, skip, merged,
        part, far_part, held_gates,
        info_out, info_in, w_out, w_in, f_out, f_in, c_out, c_in,
        load, store,
        m_send, m_recv, r_send, r_recv, info_send, info_recv, w_send, w_recv, f_send, f_recv, c_send, c_recv,
    ) = refs[2 + WEIGHTS :]
    size = lax.axis_size("face")
    here = lax.axis_index("segment"), lax.axis_index("face")
    mine = block_of(*here, size)
    away = host_of(*here, size)
    moved = (away[0] != here[0]) | (away[1] != here[1])

    def beside(place, step):
        return place[0], lax.rem(place[1] + step + size, size)

    home_after, home_before = beside(mine, 1), beside(mine, -1)
    after, before = host_of(*home_after, size), host_of(*home_before, size)
    odd = (mine[1] & 1) == 1
    far = jnp.where(odd, 0, 1)
    ways = (
        (far, tuple(jnp.where(odd, a, b) for a, b in zip(after, before))),
        (1 - far, tuple(jnp.where(odd, b, a) for a, b in zip(after, before))),
    )
    first_targets = host_of(*beside(here, 1), size), host_of(*beside(here, -1), size)

    def greet(target):
        pl.semaphore_signal(
            barrier, inc=1, device_id={"segment": target[0], "face": target[1]},
            device_id_type=pl.DeviceIdType.MESH,
        )

    def remote(src, dst, send, recv, target):
        return pltpu.make_async_remote_copy(
            src_ref=src, dst_ref=dst, send_sem=send, recv_sem=recv,
            device_id={"segment": target[0], "face": target[1]},
            device_id_type=pl.DeviceIdType.MESH,
        )

    def pair(out, into, send, recv, slot):
        return [
            remote(out.at[slot, w], into.at[slot, w], send.at[slot, w], recv.at[slot, w], target)
            for w, target in ways
        ]

    def info_copies():
        return [
            remote(info_out, info_in.at[w], info_send.at[w], info_recv.at[w], target)
            for w, target in enumerate(first_targets)
        ]

    def weather_copies(step, ways):
        return [
            remote(w_out.at[step], w_in.at[step, w], w_send.at[step, w], w_recv.at[step, w], target)
            for w, target in ways
        ]

    def state_copy():
        return remote(states_in, states_moved, m_send.at[0], m_recv.at[0], away)

    def own_info_copy():
        return remote(info_out, info_moved, m_send.at[1], m_recv.at[1], away)

    def gru_copy():
        return remote(gru_in, gru_moved, m_send.at[2], m_recv.at[2], away)

    def result_copy(step):
        return remote(
            result_out.at[step], forecast.at[step, 0], r_send.at[step], r_recv.at[step], mine
        )

    def gru_result_copy():
        return remote(gru_out, gru_final.at[0], m_send.at[3], m_recv.at[3], mine)

    def result_store(step):
        return pltpu.make_async_copy(result_out.at[step], forecast.at[step, 0], store.at[step])

    def gru_result_store():
        return pltpu.make_async_copy(gru_out, gru_final.at[0], store.at[STEPS])

    def start(copies):
        for copy in copies:
            copy.start()

    def wait(copies):
        for copy in copies:
            copy.wait()

    barrier = pltpu.get_barrier_semaphore()
    for target in (home_after, home_before, after, before):
        greet(target)

    @pl.when(moved)
    def _():
        greet(mine)
        greet(away)

    loads = [
        pltpu.make_async_copy(nbr_hbm, nbr, load.at[2 + WEIGHTS]),
        pltpu.make_async_copy(orient_hbm, orient, load.at[3 + WEIGHTS]),
        pltpu.make_async_copy(states, states_in, load.at[0]),
    ]
    loads += [
        pltpu.make_async_copy(src, dst, load.at[2 + n])
        for n, (src, dst) in enumerate(zip(hbm_weights, vmem_weights))
    ]
    loads.append(pltpu.make_async_copy(gru_state, gru_in, load.at[1]))
    start(loads[:3])

    loads[0].wait()
    loads[1].wait()
    lane = lax.broadcasted_iota(jnp.int32, (1, 256), 1)
    for row, p in ((0, NORTH), (2, SOUTH)):
        info_out[row : row + 1] = far_index(lane, nbr, orient, SIDE0, p)
        info_out[row + 1 : row + 2] = far_index(lane, nbr, orient, SIDE1, p)
    info_out[4:5] = near_index(lane, nbr, orient, SIDE0)
    info_out[5:6] = near_index(lane, nbr, orient, SIDE1)
    info_out[6:8] = jnp.zeros((2, 256), jnp.int32)
    weather[...] = jnp.zeros_like(weather)
    loads[2].wait()
    weather[:FIELDS] = states_in[:, 0, :]
    w_out[0] = weather[...].astype(BF16)
    pl.semaphore_wait(barrier, jnp.where(moved, 6, 4))

    @pl.when(moved)
    def _():
        own_info_copy().start()
        state_copy().start()

    start(weather_copies(0, tuple(enumerate(first_targets))))
    start(info_copies())
    start(loads[3:])

    def coarse_of(cell):
        tile = lax.shift_right_logical(cell, 8)
        row = lax.shift_right_logical(cell, 5) & 7
        return tile * 64 + row * 8 + (lax.shift_right_logical(cell, 1) & 7)

    pad0[...] = jnp.zeros_like(pad0)
    halo0[...] = jnp.zeros_like(halo0)
    pad1[...] = jnp.zeros_like(pad1)
    halo1[...] = jnp.zeros_like(halo1)
    cell = lax.broadcasted_iota(jnp.int32, (CELLS0, 1), 0)
    one = one_hot(coarse_of(cell), CELLS1, 1).astype(BF16)
    grow[:, :CELLS1] = one
    grow[:, CELLS1:] = one
    cell = lax.broadcasted_iota(jnp.int32, (1, CELLS0), 1)
    pool[...] = (0.25 * one_hot(coarse_of(cell), CELLS1, 0)).astype(BF16)
    for copy in loads[3:]:
        copy.wait()

    @pl.when(moved)
    def _():
        gru_copy().start()

    embed[...] = jnp.zeros_like(embed)
    embed[:FIELDS] = embed_w[...].astype(F32)
    taps_ef[...] = spread_taps(ef_depth[...])
    taps_df[...] = spread_taps(df_depth[...])
    taps_ec[...] = spread_taps(ec_depth[...])
    taps_dc[...] = spread_taps(dc_depth[...])
    for g in range(3):
        wide = gru_w[g].astype(F32)
        gru_a[g] = wide[:, :C1].astype(BF16)
        gru_b[g] = wide[:, C1:].astype(BF16)
    wide = combine_w[...].astype(F32)
    comb_b[...] = wide[C0:].astype(BF16)
    lift_w[...] = dot_nn(up_w[...], wide[:C0].astype(BF16)).astype(BF16)

    @pl.when(moved)
    def _():
        own_info_copy().wait()

    @pl.when(jnp.logical_not(moved))
    def _():
        info_moved[...] = info_out[...]

    near0[...] = one_hot(info_moved[4:5], CELLS0, 0).T.astype(BF16)
    for way in range(2):
        wanted = info_moved[2 * way : 2 * way + 1, :128]
        own_far[way] = one_hot(wanted, CELLS0, 0).T[:RIM0].astype(BF16)

    @pl.when(moved)
    def _():
        state_copy().wait()
        weather[:FIELDS] = states_moved[:, 0, :]

    def prepare_gather():
        for way in range(2):
            wanted = info_in[1 - way, 2 * way + 1 : 2 * way + 2, :128]
            far1[way] = one_hot(wanted, CELLS1, 0).T[:RIM1].astype(BF16)
            far_pool[way] = dot_nn(far1[way], pool[...]).astype(BF16)

    def prepare_rest():
        for way in range(2):
            wanted = info_in[1 - way, 2 * way : 2 * way + 1, :128]
            far0[way] = one_hot(wanted, CELLS0, 0).T[:RIM0].astype(BF16)
            one = dot_nn(far0[way], grow[:, :CELLS1]).astype(BF16)
            far_grow[way, :, :CELLS1] = one
            far_grow[way, :, CELLS1:] = one

        @pl.when(moved)
        def _():
            gru_copy().wait()
            gru_in[...] = gru_moved[...]

        state = jnp.concatenate(
            [gru_in[...].reshape(C1, CELLS1), jnp.zeros((256 - C1, CELLS1), F32)], 0
        )
        carried[...] = state.T[:, :C1]

    def fill0(r):
        pad0[:, 3 : 3 + SIDE0, 8:24, :] = r.astype(F32).reshape(TILES, SIDE0, SIDE0, C0)
        sides = dot_nn(near0[...], r).reshape(TILES, SIDE0, 8, C0)
        pad0[:, 3 : 3 + SIDE0, 0:8, :] = sides
        pad0[:, 3 : 3 + SIDE0, 24:32, :] = sides

    def fill1(r):
        pad1[:, 3 : 3 + SIDE1, 8:16, :] = r.astype(F32).reshape(TILES, SIDE1, SIDE1, C1)
        sides = dot_nn(near1[...], r).reshape(TILES, SIDE1, 8, C1)
        pad1[:, 3 : 3 + SIDE1, 0:8, :] = sides
        pad1[:, 3 : 3 + SIDE1, 16:24, :] = sides

    def fine_block_inner(taps, expand, shrink, out):
        for tile in range(TILES):
            for half in range(2):
                total = conv_tile(pad0, tile, SIDE0, 8 + 8 * half, taps)
                y0[tile, :, 8 * half : 8 * half + 8, :] = total
        y = y0[:, 3:13].reshape(TILES * 10 * SIDE0, C0)
        r = pad0[:, 6:16, 8:24, :].reshape(TILES * 10 * SIDE0, C0)
        done = finish(y, r, expand[...], shrink[...])
        out[:, 3:13] = done.reshape(TILES, 10, SIDE0, C0)
        for tile in range(TILES):
            for side, top in ((0, 3), (1, 16)):
                edge_r[tile, side] = pad0[tile, top : top + 3, 8:24, :]

    def fine_block_outer(taps, expand, shrink, out):
        def body(tile, _):
            for side, top in ((0, 0), (1, 13)):
                for half in range(2):
                    columns = slice(8 * half, 8 * half + 8)
                    rows = [y0[tile, top + o, columns, :] for o in range(3)]
                    rows = conv_halo(halo0, side, tile, 8 + 8 * half, taps, rows)
                    for o in range(3):
                        edge_y[tile, side, o, columns, :] = rows[o]
            return 0

        lax.fori_loop(0, TILES, body, 0, unroll=True)
        y = edge_y[...].reshape(2 * RIM0, C0)
        r = edge_r[...].reshape(2 * RIM0, C0)
        done = finish(y, r, expand[...], shrink[...]).reshape(TILES, 2, 3, SIDE0, C0)
        for tile in range(TILES):
            out[tile, 0:3] = done[tile, 0]
            out[tile, 13:16] = done[tile, 1]

    def coarse_block(r, slot, copies, taps, expand, shrink, meanwhile):
        fill1(r)

        def body(tile, _):
            y1[tile] = conv_tile(pad1, tile, SIDE1, 8, taps)
            return 0

        lax.fori_loop(0, TILES, body, 0, unroll=True)
        meanwhile()
        wait(copies)
        for way in range(2):
            arrived = c_in[slot, way].astype(F32).reshape(TILES, 3, SIDE1, C1)
            halo1[way, :, :, 8:16, :] = arrived

        def edge(tile, _):
            for side, top in ((0, 0), (1, 5)):
                rows = [y1[tile, top + o] for o in range(3)]
                rows = conv_halo(halo1, side, tile, 8, taps, rows)
                for o in range(3):
                    y1[tile, top + o] = rows[o]
            return 0

        lax.fori_loop(0, TILES, edge, 0, unroll=True)
        y = y1[...].reshape(CELLS1, C1)
        return finish(y, r.astype(F32), expand[...], shrink[...])

    def step_body(step, _):
        fields = weather[...].astype(BF16).astype(F32).T.astype(BF16)
        lift = embed[...].astype(BF16)
        fill0(dot_nn(fields, lift).astype(BF16))
        fine_block_inner(taps_ef, ef_expand, ef_shrink, skip)

        @pl.when(step == 0)
        def _():
            near1[...] = one_hot(info_moved[5:6, :128], CELLS1, 0).T.astype(BF16)
            wait(info_copies())
            prepare_gather()

        wait(weather_copies(step, ways))
        for way in range(2):
            rim = dot_nt(own_far[way], w_in[step, way]).astype(BF16)
            rim = dot_nn(rim, lift).astype(BF16).astype(F32)
            halo0[way, :, :, 8:24, :] = rim.reshape(TILES, 3, SIDE0, C0)
        fine_block_outer(taps_ef, ef_expand, ef_shrink, skip)

        kept = skip[...].reshape(CELLS0, C0)
        copies = pair(c_out, c_in, c_send, c_recv, 2 * step)
        for (way, _), copy in zip(ways, copies):
            wanted = dot_nn(far_pool[way], kept).astype(BF16)
            c_out[2 * step, way] = dot_nt(wanted, down_w[...]).astype(BF16)
            copy.start()
        coarse = dot_nn(pool[...], kept).astype(BF16)
        coarse = dot_nt(coarse, down_w[...]).astype(BF16)

        def after_skip():
            @pl.when(step == 0)
            def _():
                prepare_rest()

            kept = skip[...].reshape(CELLS0, C0)
            part[...] = dot_nn(kept, comb_b[...])
            for way in range(2):
                far_part[way] = dot_nn(dot_nn(far0[way], kept).astype(BF16), comb_b[...])
            held = carried[...].astype(BF16)
            for g in range(2):
                held_gates[g] = dot_nt(held, gru_b[g])

        coarse = coarse_block(
            coarse, 2 * step, copies, taps_ec, ec_expand, ec_shrink, after_skip
        )

        old = carried[...]
        update = jax.nn.sigmoid(dot_nt(coarse, gru_a[0]) + held_gates[0])
        reset = jax.nn.sigmoid(dot_nt(coarse, gru_a[1]) + held_gates[1])
        gated = (reset * old).astype(BF16)
        candidate = jnp.tanh(dot_nt(coarse, gru_a[2]) + dot_nt(gated, gru_b[2]))
        new = (1.0 - update) * old + update * candidate
        carried[...] = new

        new = new.astype(BF16)
        copies = pair(c_out, c_in, c_send, c_recv, 2 * step + 1)
        for (way, _), copy in zip(ways, copies):
            c_out[2 * step + 1, way] = dot_nn(far1[way], new).astype(BF16)
            copy.start()

        def after_update():
            @pl.when(step == STEPS - 1)
            def _():
                last = jnp.concatenate([carried[...], jnp.zeros((CELLS1, 256 - C1), F32)], 1)
                gru_out[...] = last.T[:C1]

                @pl.when(moved)
                def _():
                    gru_result_copy().start()

                @pl.when(jnp.logical_not(moved))
                def _():
                    gru_result_store().start()

        decoded = coarse_block(
            new, 2 * step + 1, copies, taps_dc, dc_expand, dc_shrink, after_update
        )

        lifted = halves(dot_nn(decoded, lift_w[...]))
        copies = pair(f_out, f_in, f_send, f_recv, step)
        for (way, _), copy in zip(ways, copies):
            f_out[step, way] = (dot_nn(far_grow[way], lifted) + far_part[way]).astype(BF16)
            copy.start()
        fill0((dot_nn(grow[...], lifted) + part[...]).astype(BF16))
        fine_block_inner(taps_df, df_expand, df_shrink, merged)
        wait(copies)
        for way in range(2):
            arrived = f_in[step, way].astype(F32).reshape(TILES, 3, SIDE0, C0)
            halo0[way, :, :, 8:24, :] = arrived
        fine_block_outer(taps_df, df_expand, df_shrink, merged)

        change = dot_nt(head_w[...], merged[...].reshape(CELLS0, C0))
        now = weather[:FIELDS] + change
        weather[:FIELDS] = now

        @pl.when(step < STEPS - 1)
        def _():
            w_out[step + 1] = weather[...].astype(BF16)
            start(weather_copies(step + 1, ways))

        result_out[step] = now

        @pl.when(moved)
        def _():
            result_copy(step).start()

        @pl.when(jnp.logical_not(moved))
        def _():
            result_store(step).start()

        return 0

    lax.fori_loop(0, STEPS, step_body, 0)

    @pl.when(moved)
    def _():
        gru_result_copy().wait()
        for step in range(STEPS):
            result_copy(step).wait()

    @pl.when(jnp.logical_not(moved))
    def _():
        gru_result_store().wait()
        for step in range(STEPS):
            result_store(step).wait()


def local(states, gru_state, neighbours, orient, *weights):
    (
        embed_w, ef_depth, ef_expand, ef_shrink, down_w, ec_depth, ec_expand, ec_shrink,
        gru_w, dc_depth, dc_expand, dc_shrink, up_w, combine_w, df_depth, df_expand,
        df_shrink, head_w,
    ) = weights
    weights = (
        embed_w.T, ef_depth.T, ef_expand.T, ef_shrink, down_w, ec_depth.T, ec_expand.T, ec_shrink,
        gru_w, dc_depth.T, dc_expand.T, dc_shrink, up_w.T, combine_w.T, df_depth.T, df_expand.T,
        df_shrink, head_w,
    )
    hbm = pl.BlockSpec(memory_space=pltpu.HBM)
    scratch = [pltpu.VMEM(w.shape, w.dtype) for w in weights]
    scratch += [
        pltpu.SMEM((TILES, 4), jnp.int32),
        pltpu.SMEM((TILES, 4), jnp.int32),
        pltpu.VMEM((FIELDS, 1, CELLS0), F32),
        pltpu.VMEM((C1, 1, CELLS1), F32),
        pltpu.VMEM((FIELDS, 1, CELLS0), F32),
        pltpu.VMEM((C1, 1, CELLS1), F32),
        pltpu.VMEM((8, 256), jnp.int32),
        pltpu.VMEM((STEPS, FIELDS, CELLS0), F32),
        pltpu.VMEM((C1, CELLS1), F32),
        pltpu.VMEM((ROWS, CELLS0), F32),
        pltpu.VMEM((CELLS1, C1), F32),
        pltpu.VMEM((ROWS, C0), F32),
        pltpu.VMEM((3, C1, C1), BF16),
        pltpu.VMEM((3, C1, C1), BF16),
        pltpu.VMEM((C1, C0), BF16),
        pltpu.VMEM((C0, C0), BF16),
        pltpu.VMEM((49, 8, C0), F32),
        pltpu.VMEM((49, 8, C0), F32),
        pltpu.VMEM((49, 8, C1), F32),
        pltpu.VMEM((49, 8, C1), F32),
        pltpu.VMEM((TILES * SIDE0 * 8, CELLS0), BF16),
        pltpu.VMEM((TILES * SIDE1 * 8, CELLS1), BF16),
        pltpu.VMEM((2, RIM0, CELLS0), BF16),
        pltpu.VMEM((2, RIM1, CELLS1), BF16),
        pltpu.VMEM((2, RIM0, CELLS0), BF16),
        pltpu.VMEM((CELLS0, 2 * CELLS1), BF16),
        pltpu.VMEM((CELLS1, CELLS0), BF16),
        pltpu.VMEM((2, RIM1, CELLS0), BF16),
        pltpu.VMEM((2, RIM0, 2 * CELLS1), BF16),
        pltpu.VMEM((TILES, SIDE0 + 6, 32, C0), F32),
        pltpu.VMEM((TILES, SIDE1 + 6, 24, C1), F32),
        pltpu.VMEM((2, TILES, 3, 32, C0), F32),
        pltpu.VMEM((2, TILES, 3, 24, C1), F32),
        pltpu.VMEM((TILES, SIDE0, SIDE0, C0), F32),
        pltpu.VMEM((TILES, SIDE1, SIDE1, C1), F32),
        pltpu.VMEM((TILES, 2, 3, SIDE0, C0), F32),
        pltpu.VMEM((TILES, 2, 3, SIDE0, C0), F32),
        pltpu.VMEM((TILES, SIDE0, SIDE0, C0), BF16),
        pltpu.VMEM((TILES, SIDE0, SIDE0, C0), BF16),
        pltpu.VMEM((CELLS0, C0), F32),
        pltpu.VMEM((2, RIM0, C0), F32),
        pltpu.VMEM((2, CELLS1, C1), F32),
        pltpu.VMEM((8, 256), jnp.int32),
        pltpu.VMEM((2, 8, 256), jnp.int32),
        pltpu.VMEM((STEPS, ROWS, CELLS0), BF16),
        pltpu.VMEM((STEPS, 2, ROWS, CELLS0), BF16),
        pltpu.VMEM((STEPS, 2, RIM0, C0), BF16),
        pltpu.VMEM((STEPS, 2, RIM0, C0), BF16),
        pltpu.VMEM((2 * STEPS, 2, RIM1, C1), BF16),
        pltpu.VMEM((2 * STEPS, 2, RIM1, C1), BF16),
        pltpu.SemaphoreType.DMA((4 + WEIGHTS,)),
        pltpu.SemaphoreType.DMA((STEPS + 1,)),
        pltpu.SemaphoreType.DMA((4,)),
        pltpu.SemaphoreType.DMA((4,)),
        pltpu.SemaphoreType.DMA((STEPS,)),
        pltpu.SemaphoreType.DMA((STEPS,)),
        pltpu.SemaphoreType.DMA((2,)),
        pltpu.SemaphoreType.DMA((2,)),
        pltpu.SemaphoreType.DMA((STEPS, 2)),
        pltpu.SemaphoreType.DMA((STEPS, 2)),
        pltpu.SemaphoreType.DMA((STEPS, 2)),
        pltpu.SemaphoreType.DMA((STEPS, 2)),
        pltpu.SemaphoreType.DMA((2 * STEPS, 2)),
        pltpu.SemaphoreType.DMA((2 * STEPS, 2)),
    ]
    return pl.pallas_call(
        kernel,
        out_shape=(
            jax.ShapeDtypeStruct((STEPS, 1, FIELDS, CELLS0), F32),
            jax.ShapeDtypeStruct((1, C1, CELLS1), F32),
        ),
        in_specs=[hbm] * (4 + len(weights)),
        out_specs=(hbm, hbm),
        scratch_shapes=scratch,
        compiler_params=pltpu.CompilerParams(
            collective_id=0, has_side_effects=True, vmem_limit_bytes=56 * 1024 * 1024
        ),
    )(states.transpose(1, 0, 2), gru_state.transpose(1, 0, 2), neighbours, orient, *weights)


def solution(mesh):
    in_specs = (
        P("segment", None, "face"),
        P("segment", None, "face"),
        P("face", None),
        P("face", None),
    ) + (P(),) * 18
    out_specs = (P(None, "segment", None, "face"), P("segment", None, "face"))
    return jax.shard_map(local, mesh=mesh, in_specs=in_specs, out_specs=out_specs, check_vma=False)
```

```python
import jax
import jax.numpy as jnp
from jax import lax
from jax.experimental import pallas as pl
from jax.experimental.pallas import tpu as pltpu
from jax.sharding import PartitionSpec as P

FIELDS = 9
C0 = 90
C1 = 180
SIDE0 = 16
SIDE1 = 8
TILES = 2
STEPS = 2
CELLS0 = TILES * SIDE0 * SIDE0
CELLS1 = TILES * SIDE1 * SIDE1
RIM0 = TILES * 3 * SIDE0
RIM1 = TILES * 3 * SIDE1
ROWS = 16
F32, BF16 = jnp.float32, jnp.bfloat16
NORTH, EAST, SOUTH, WEST = range(4)
ROW = 16


def dot_nt(a, b):
    return lax.dot_general(a, b, (((1,), (1,)), ((), ())), preferred_element_type=F32)


def dot_nn(a, b):
    return jnp.dot(a, b, preferred_element_type=F32)


def one_hot(index, cells, axis):
    shape = (index.shape[0], cells) if axis == 1 else (cells, index.shape[1])
    hit = lax.broadcasted_iota(jnp.int32, shape, axis) == index
    return jnp.where(hit, 1.0, 0.0)


def rim_line(nbr, orient, tile, side, p):
    o = orient[tile, p]
    from_side = lax.shift_right_logical(o, 1)
    per_depth = jnp.where(
        from_side == 0, side, jnp.where(from_side == 1, -1, jnp.where(from_side == 2, -side, 1))
    )
    base = jnp.where(from_side == 1, side - 1, jnp.where(from_side == 2, side * (side - 1), 0))
    per_step = jnp.where((from_side & 1) == 0, 1, side)
    turned = (o & 1) == 1
    base = base + jnp.where(turned, per_step * (side - 1), 0)
    per_step = jnp.where(turned, -per_step, per_step)
    return base + (nbr[tile, p] & 1) * side * side, per_depth, per_step


def far_index(m, nbr, orient, side, p):
    index = jnp.full(m.shape, -1, jnp.int32)
    for tile in range(TILES):
        base, per_depth, per_step = rim_line(nbr, orient, tile, side, p)
        local = m - tile * 3 * side
        row = jnp.where(local >= 2 * side, 2, jnp.where(local >= side, 1, 0))
        depth = 2 - row if p == NORTH else row
        value = base + per_depth * depth + per_step * (local - row * side)
        index = jnp.where((local >= 0) & (local < 3 * side), value, index)
    return index


def near_index(m, nbr, orient, side):
    index = jnp.full(m.shape, -1, jnp.int32)
    for tile in range(TILES):
        base_e, depth_e, step_e = rim_line(nbr, orient, tile, side, EAST)
        base_w, depth_w, step_w = rim_line(nbr, orient, tile, side, WEST)
        local = m - tile * side * 8
        row, place = lax.shift_right_arithmetic(local, 3), local & 7
        east = base_e + depth_e * place + step_e * row
        west = base_w + depth_w * (7 - place) + step_w * row
        value = jnp.where(place < 3, east, jnp.where(place >= 5, west, -1))
        index = jnp.where((local >= 0) & (local < 8 * side), value, index)
    return index


def host_of(segment, block, size):
    core, odd = segment & 1, block & 1
    face = block - odd + (1 - core)
    last = lax.rem(block, ROW) == ROW - 1
    return segment - core + (1 - odd), jnp.where(last, lax.rem(face + ROW, size), face)


def block_of(segment, face, size):
    core, odd = segment & 1, face & 1
    block = face - odd + (1 - core)
    last = lax.rem(block, ROW) == ROW - 1
    return segment - core + (1 - odd), jnp.where(last, lax.rem(block + size - ROW, size), block)


def spread_taps(weight):
    return jnp.broadcast_to(weight.astype(F32)[:, None, :], (49, 8, weight.shape[1]))


def halves(x):
    high = x.astype(BF16)
    return jnp.concatenate([high, (x - high.astype(F32)).astype(BF16)], 0)


def normalise(y, channels):
    centred = y - jnp.sum(y, 1, keepdims=True) * (1.0 / channels)
    var = jnp.sum(centred * centred, 1, keepdims=True) * (1.0 / channels)
    return (centred * lax.rsqrt(var + 1e-6)).astype(BF16)


def gelu(x):
    return (0.5 * x) * (1.0 + lax.erf(x * 0.7071067811865476))


def finish(y, r, expand, shrink):
    normed = normalise(y, y.shape[1])
    expanded = gelu(dot_nn(normed, expand)).astype(BF16)
    return (r + dot_nt(expanded, shrink)).astype(BF16)


def conv_tile(pad, tile, rows, first, taps):
    total = [None] * rows
    for q in range(7):
        x = pad[tile, 3 : 3 + rows, first + q - 3 : first + q + 5, :]
        for u in range(7):
            low, high = max(0, 3 - u), min(rows, rows + 3 - u)
            term = taps[7 * u + q][None] * x[low + u - 3 : high + u - 3]
            for o in range(low, high):
                one = term[o - low]
                total[o] = one if total[o] is None else total[o] + one
    return jnp.stack(total, 0)


def conv_halo(halo, side, tile, first, taps, rows):
    rows = list(rows)
    for q in range(7):
        for h in range(3):
            x = halo[side, tile, h, first + q - 3 : first + q + 5, :]
            for o in range(3):
                u = h - o if side == 0 else 6 + h - o
                if 0 <= u <= 6:
                    rows[o] = rows[o] + taps[7 * u + q] * x
    return rows


WEIGHTS = 18


def kernel(
    states, gru_state, nbr_hbm, orient_hbm, *refs,
):
    (
        embed_w, ef_depth, ef_expand, ef_shrink, down_w, ec_depth, ec_expand, ec_shrink,
        gru_w, dc_depth, dc_expand, dc_shrink, up_w, combine_w, df_depth, df_expand,
        df_shrink, head_w,
    ) = refs[:WEIGHTS]
    forecast, gru_final = refs[WEIGHTS : WEIGHTS + 2]
    (
        nbr, orient, states_in, gru_in, states_moved, gru_moved, info_moved,
        result_out, gru_out,
        weather, carried, embed, gru_a, gru_b, lift_w, comb_b,
        taps_ef, taps_df, taps_ec, taps_dc,
        near0, near1, own_far, far1, far0, grow, pool, far_pool, far_grow,
        pad0, pad1, halo0, halo1, y0, y1, edge_y, edge_r, skip, merged,
        part, far_part, held_gates,
        info_out, info_in, w_out, w_in, f_out, f_in, c_out, c_in,
        load, store,
        m_send, m_recv, r_send, r_recv, info_send, info_recv, w_send, w_recv, f_send, f_recv, c_send, c_recv,
    ) = refs[2 + WEIGHTS :]
    size = lax.axis_size("face")
    here = lax.axis_index("segment"), lax.axis_index("face")
    mine = block_of(*here, size)
    away = host_of(*here, size)
    moved = (away[0] != here[0]) | (away[1] != here[1])

    def beside(place, step):
        return place[0], lax.rem(place[1] + step + size, size)

    home_after, home_before = beside(mine, 1), beside(mine, -1)
    after, before = host_of(*home_after, size), host_of(*home_before, size)
    odd = (mine[1] & 1) == 1
    far = jnp.where(odd, 0, 1)
    ways = (
        (far, tuple(jnp.where(odd, a, b) for a, b in zip(after, before))),
        (1 - far, tuple(jnp.where(odd, b, a) for a, b in zip(after, before))),
    )
    first_targets = host_of(*beside(here, 1), size), host_of(*beside(here, -1), size)

    def greet(target):
        pl.semaphore_signal(
            barrier, inc=1, device_id={"segment": target[0], "face": target[1]},
            device_id_type=pl.DeviceIdType.MESH,
        )

    def remote(src, dst, send, recv, target):
        return pltpu.make_async_remote_copy(
            src_ref=src, dst_ref=dst, send_sem=send, recv_sem=recv,
            device_id={"segment": target[0], "face": target[1]},
            device_id_type=pl.DeviceIdType.MESH,
        )

    def pair(out, into, send, recv, slot):
        return [
            remote(out.at[slot, w], into.at[slot, w], send.at[slot, w], recv.at[slot, w], target)
            for w, target in ways
        ]

    def info_copies():
        return [
            remote(info_out, info_in.at[w], info_send.at[w], info_recv.at[w], target)
            for w, target in enumerate(first_targets)
        ]

    def weather_copies(step, ways):
        return [
            remote(w_out.at[step], w_in.at[step, w], w_send.at[step, w], w_recv.at[step, w], target)
            for w, target in ways
        ]

    def state_copy():
        return remote(states_in, states_moved, m_send.at[0], m_recv.at[0], away)

    def own_info_copy():
        return remote(info_out, info_moved, m_send.at[1], m_recv.at[1], away)

    def gru_copy():
        return remote(gru_in, gru_moved, m_send.at[2], m_recv.at[2], away)

    def result_copy(step):
        return remote(
            result_out.at[step], forecast.at[step, 0], r_send.at[step], r_recv.at[step], mine
        )

    def gru_result_copy():
        return remote(gru_out, gru_final.at[0], m_send.at[3], m_recv.at[3], mine)

    def result_store(step):
        return pltpu.make_async_copy(result_out.at[step], forecast.at[step, 0], store.at[step])

    def gru_result_store():
        return pltpu.make_async_copy(gru_out, gru_final.at[0], store.at[STEPS])

    def start(copies):
        for copy in copies:
            copy.start()

    def wait(copies):
        for copy in copies:
            copy.wait()

    barrier = pltpu.get_barrier_semaphore()
    for target in (home_after, home_before, after, before):
        greet(target)

    @pl.when(moved)
    def _():
        greet(mine)
        greet(away)

    loads = [
        pltpu.make_async_copy(nbr_hbm, nbr, load.at[2]),
        pltpu.make_async_copy(orient_hbm, orient, load.at[3]),
        pltpu.make_async_copy(states, states_in, load.at[0]),
    ]
    loads.append(pltpu.make_async_copy(gru_state, gru_in, load.at[1]))
    start(loads[:3])

    loads[0].wait()
    loads[1].wait()
    lane = lax.broadcasted_iota(jnp.int32, (1, 256), 1)
    for row, p in ((0, NORTH), (2, SOUTH)):
        info_out[row : row + 1] = far_index(lane, nbr, orient, SIDE0, p)
        info_out[row + 1 : row + 2] = far_index(lane, nbr, orient, SIDE1, p)
    info_out[4:5] = near_index(lane, nbr, orient, SIDE0)
    info_out[5:6] = near_index(lane, nbr, orient, SIDE1)
    info_out[6:8] = jnp.zeros((2, 256), jnp.int32)
    weather[...] = jnp.zeros_like(weather)
    loads[2].wait()
    weather[:FIELDS] = states_in[:, 0, :]
    w_out[0] = weather[...].astype(BF16)
    pl.semaphore_wait(barrier, jnp.where(moved, 6, 4))

    @pl.when(moved)
    def _():
        own_info_copy().start()
        state_copy().start()

    start(weather_copies(0, tuple(enumerate(first_targets))))
    start(info_copies())
    start(loads[3:])

    def coarse_of(cell):
        tile = lax.shift_right_logical(cell, 8)
        row = lax.shift_right_logical(cell, 5) & 7
        return tile * 64 + row * 8 + (lax.shift_right_logical(cell, 1) & 7)

    pad0[...] = jnp.zeros_like(pad0)
    halo0[...] = jnp.zeros_like(halo0)
    pad1[...] = jnp.zeros_like(pad1)
    halo1[...] = jnp.zeros_like(halo1)
    cell = lax.broadcasted_iota(jnp.int32, (CELLS0, 1), 0)
    one = one_hot(coarse_of(cell), CELLS1, 1).astype(BF16)
    grow[:, :CELLS1] = one
    grow[:, CELLS1:] = one
    cell = lax.broadcasted_iota(jnp.int32, (1, CELLS0), 1)
    pool[...] = (0.25 * one_hot(coarse_of(cell), CELLS1, 0)).astype(BF16)
    for copy in loads[3:]:
        copy.wait()

    @pl.when(moved)
    def _():
        gru_copy().start()

    embed[...] = jnp.zeros_like(embed)
    embed[:FIELDS] = embed_w[...].astype(F32)
    taps_ef[...] = spread_taps(ef_depth[...])
    taps_df[...] = spread_taps(df_depth[...])
    taps_ec[...] = spread_taps(ec_depth[...])
    taps_dc[...] = spread_taps(dc_depth[...])
    for g in range(3):
        wide = gru_w[g].astype(F32)
        gru_a[g] = wide[:, :C1].astype(BF16)
        gru_b[g] = wide[:, C1:].astype(BF16)
    wide = combine_w[...].astype(F32)
    comb_b[...] = wide[C0:].astype(BF16)
    lift_w[...] = dot_nn(up_w[...], wide[:C0].astype(BF16)).astype(BF16)

    @pl.when(moved)
    def _():
        own_info_copy().wait()

    @pl.when(jnp.logical_not(moved))
    def _():
        info_moved[...] = info_out[...]

    near0[...] = one_hot(info_moved[4:5], CELLS0, 0).T.astype(BF16)
    for way in range(2):
        wanted = info_moved[2 * way : 2 * way + 1, :128]
        own_far[way] = one_hot(wanted, CELLS0, 0).T[:RIM0].astype(BF16)

    @pl.when(moved)
    def _():
        state_copy().wait()
        weather[:FIELDS] = states_moved[:, 0, :]

    def prepare_gather():
        for way in range(2):
            wanted = info_in[1 - way, 2 * way + 1 : 2 * way + 2, :128]
            far1[way] = one_hot(wanted, CELLS1, 0).T[:RIM1].astype(BF16)
            far_pool[way] = dot_nn(far1[way], pool[...]).astype(BF16)

    def prepare_rest():
        for way in range(2):
            wanted = info_in[1 - way, 2 * way : 2 * way + 1, :128]
            far0[way] = one_hot(wanted, CELLS0, 0).T[:RIM0].astype(BF16)
            one = dot_nn(far0[way], grow[:, :CELLS1]).astype(BF16)
            far_grow[way, :, :CELLS1] = one
            far_grow[way, :, CELLS1:] = one

        @pl.when(moved)
        def _():
            gru_copy().wait()
            gru_in[...] = gru_moved[...]

        state = jnp.concatenate(
            [gru_in[...].reshape(C1, CELLS1), jnp.zeros((256 - C1, CELLS1), F32)], 0
        )
        carried[...] = state.T[:, :C1]

    def fill0(r):
        pad0[:, 3 : 3 + SIDE0, 8:24, :] = r.astype(F32).reshape(TILES, SIDE0, SIDE0, C0)
        sides = dot_nn(near0[...], r).reshape(TILES, SIDE0, 8, C0)
        pad0[:, 3 : 3 + SIDE0, 0:8, :] = sides
        pad0[:, 3 : 3 + SIDE0, 24:32, :] = sides

    def fill1(r):
        pad1[:, 3 : 3 + SIDE1, 8:16, :] = r.astype(F32).reshape(TILES, SIDE1, SIDE1, C1)
        sides = dot_nn(near1[...], r).reshape(TILES, SIDE1, 8, C1)
        pad1[:, 3 : 3 + SIDE1, 0:8, :] = sides
        pad1[:, 3 : 3 + SIDE1, 16:24, :] = sides

    def fine_block_inner(taps, expand, shrink, out):
        for tile in range(TILES):
            for half in range(2):
                total = conv_tile(pad0, tile, SIDE0, 8 + 8 * half, taps)
                y0[tile, :, 8 * half : 8 * half + 8, :] = total
        y = y0[:, 3:13].reshape(TILES * 10 * SIDE0, C0)
        r = pad0[:, 6:16, 8:24, :].reshape(TILES * 10 * SIDE0, C0)
        done = finish(y, r, expand[...], shrink[...])
        out[:, 3:13] = done.reshape(TILES, 10, SIDE0, C0)
        for tile in range(TILES):
            for side, top in ((0, 3), (1, 16)):
                edge_r[tile, side] = pad0[tile, top : top + 3, 8:24, :]

    def fine_block_outer(taps, expand, shrink, out):
        def body(tile, _):
            for side, top in ((0, 0), (1, 13)):
                for half in range(2):
                    columns = slice(8 * half, 8 * half + 8)
                    rows = [y0[tile, top + o, columns, :] for o in range(3)]
                    rows = conv_halo(halo0, side, tile, 8 + 8 * half, taps, rows)
                    for o in range(3):
                        edge_y[tile, side, o, columns, :] = rows[o]
            return 0

        lax.fori_loop(0, TILES, body, 0, unroll=True)
        y = edge_y[...].reshape(2 * RIM0, C0)
        r = edge_r[...].reshape(2 * RIM0, C0)
        done = finish(y, r, expand[...], shrink[...]).reshape(TILES, 2, 3, SIDE0, C0)
        for tile in range(TILES):
            out[tile, 0:3] = done[tile, 0]
            out[tile, 13:16] = done[tile, 1]

    def coarse_block(r, slot, copies, taps, expand, shrink, meanwhile):
        fill1(r)

        def body(tile, _):
            y1[tile] = conv_tile(pad1, tile, SIDE1, 8, taps)
            return 0

        lax.fori_loop(0, TILES, body, 0, unroll=True)
        meanwhile()
        wait(copies)
        for way in range(2):
            arrived = c_in[slot, way].astype(F32).reshape(TILES, 3, SIDE1, C1)
            halo1[way, :, :, 8:16, :] = arrived

        def edge(tile, _):
            for side, top in ((0, 0), (1, 5)):
                rows = [y1[tile, top + o] for o in range(3)]
                rows = conv_halo(halo1, side, tile, 8, taps, rows)
                for o in range(3):
                    y1[tile, top + o] = rows[o]
            return 0

        lax.fori_loop(0, TILES, edge, 0, unroll=True)
        y = y1[...].reshape(CELLS1, C1)
        return finish(y, r.astype(F32), expand[...], shrink[...])

    def step_body(step, _):
        fields = weather[...].astype(BF16).astype(F32).T.astype(BF16)
        lift = embed[...].astype(BF16)
        fill0(dot_nn(fields, lift).astype(BF16))
        fine_block_inner(taps_ef, ef_expand, ef_shrink, skip)

        @pl.when(step == 0)
        def _():
            near1[...] = one_hot(info_moved[5:6, :128], CELLS1, 0).T.astype(BF16)
            wait(info_copies())
            prepare_gather()

        wait(weather_copies(step, ways))
        for way in range(2):
            rim = dot_nt(own_far[way], w_in[step, way]).astype(BF16)
            rim = dot_nn(rim, lift).astype(BF16).astype(F32)
            halo0[way, :, :, 8:24, :] = rim.reshape(TILES, 3, SIDE0, C0)
        fine_block_outer(taps_ef, ef_expand, ef_shrink, skip)

        kept = skip[...].reshape(CELLS0, C0)
        copies = pair(c_out, c_in, c_send, c_recv, 2 * step)
        for (way, _), copy in zip(ways, copies):
            wanted = dot_nn(far_pool[way], kept).astype(BF16)
            c_out[2 * step, way] = dot_nt(wanted, down_w[...]).astype(BF16)
            copy.start()
        coarse = dot_nn(pool[...], kept).astype(BF16)
        coarse = dot_nt(coarse, down_w[...]).astype(BF16)

        def after_skip():
            @pl.when(step == 0)
            def _():
                prepare_rest()

            kept = skip[...].reshape(CELLS0, C0)
            part[...] = dot_nn(kept, comb_b[...])
            for way in range(2):
                far_part[way] = dot_nn(dot_nn(far0[way], kept).astype(BF16), comb_b[...])
            held = carried[...].astype(BF16)
            for g in range(2):
                held_gates[g] = dot_nt(held, gru_b[g])

        coarse = coarse_block(
            coarse, 2 * step, copies, taps_ec, ec_expand, ec_shrink, after_skip
        )

        old = carried[...]
        update = jax.nn.sigmoid(dot_nt(coarse, gru_a[0]) + held_gates[0])
        reset = jax.nn.sigmoid(dot_nt(coarse, gru_a[1]) + held_gates[1])
        gated = (reset * old).astype(BF16)
        candidate = jnp.tanh(dot_nt(coarse, gru_a[2]) + dot_nt(gated, gru_b[2]))
        new = (1.0 - update) * old + update * candidate
        carried[...] = new

        new = new.astype(BF16)
        copies = pair(c_out, c_in, c_send, c_recv, 2 * step + 1)
        for (way, _), copy in zip(ways, copies):
            c_out[2 * step + 1, way] = dot_nn(far1[way], new).astype(BF16)
            copy.start()

        def after_update():
            @pl.when(step == STEPS - 1)
            def _():
                last = jnp.concatenate([carried[...], jnp.zeros((CELLS1, 256 - C1), F32)], 1)
                gru_out[...] = last.T[:C1]

                @pl.when(moved)
                def _():
                    gru_result_copy().start()

                @pl.when(jnp.logical_not(moved))
                def _():
                    gru_result_store().start()

        decoded = coarse_block(
            new, 2 * step + 1, copies, taps_dc, dc_expand, dc_shrink, after_update
        )

        lifted = halves(dot_nn(decoded, lift_w[...]))
        copies = pair(f_out, f_in, f_send, f_recv, step)
        for (way, _), copy in zip(ways, copies):
            f_out[step, way] = (dot_nn(far_grow[way], lifted) + far_part[way]).astype(BF16)
            copy.start()
        fill0((dot_nn(grow[...], lifted) + part[...]).astype(BF16))
        fine_block_inner(taps_df, df_expand, df_shrink, merged)
        wait(copies)
        for way in range(2):
            arrived = f_in[step, way].astype(F32).reshape(TILES, 3, SIDE0, C0)
            halo0[way, :, :, 8:24, :] = arrived
        fine_block_outer(taps_df, df_expand, df_shrink, merged)

        change = dot_nt(head_w[...], merged[...].reshape(CELLS0, C0))
        now = weather[:FIELDS] + change
        weather[:FIELDS] = now

        @pl.when(step < STEPS - 1)
        def _():
            w_out[step + 1] = weather[...].astype(BF16)
            start(weather_copies(step + 1, ways))

        result_out[step] = now

        @pl.when(moved)
        def _():
            result_copy(step).start()

        @pl.when(jnp.logical_not(moved))
        def _():
            result_store(step).start()

        return 0

    lax.fori_loop(0, STEPS, step_body, 0)

    @pl.when(moved)
    def _():
        gru_result_copy().wait()
        for step in range(STEPS):
            result_copy(step).wait()

    @pl.when(jnp.logical_not(moved))
    def _():
        gru_result_store().wait()
        for step in range(STEPS):
            result_store(step).wait()


def local(states, gru_state, neighbours, orient, *weights):
    (
        embed_w, ef_depth, ef_expand, ef_shrink, down_w, ec_depth, ec_expand, ec_shrink,
        gru_w, dc_depth, dc_expand, dc_shrink, up_w, combine_w, df_depth, df_expand,
        df_shrink, head_w,
    ) = weights
    weights = (
        embed_w.T, ef_depth.T, ef_expand.T, ef_shrink, down_w, ec_depth.T, ec_expand.T, ec_shrink,
        gru_w, dc_depth.T, dc_expand.T, dc_shrink, up_w.T, combine_w.T, df_depth.T, df_expand.T,
        df_shrink, head_w,
    )
    hbm = pl.BlockSpec(memory_space=pltpu.HBM)
    scratch = [
        pltpu.SMEM((TILES, 4), jnp.int32),
        pltpu.SMEM((TILES, 4), jnp.int32),
        pltpu.VMEM((FIELDS, 1, CELLS0), F32),
        pltpu.VMEM((C1, 1, CELLS1), F32),
        pltpu.VMEM((FIELDS, 1, CELLS0), F32),
        pltpu.VMEM((C1, 1, CELLS1), F32),
        pltpu.VMEM((8, 256), jnp.int32),
        pltpu.VMEM((STEPS, FIELDS, CELLS0), F32),
        pltpu.VMEM((C1, CELLS1), F32),
        pltpu.VMEM((ROWS, CELLS0), F32),
        pltpu.VMEM((CELLS1, C1), F32),
        pltpu.VMEM((ROWS, C0), F32),
        pltpu.VMEM((3, C1, C1), BF16),
        pltpu.VMEM((3, C1, C1), BF16),
        pltpu.VMEM((C1, C0), BF16),
        pltpu.VMEM((C0, C0), BF16),
        pltpu.VMEM((49, 8, C0), F32),
        pltpu.VMEM((49, 8, C0), F32),
        pltpu.VMEM((49, 8, C1), F32),
        pltpu.VMEM((49, 8, C1), F32),
        pltpu.VMEM((TILES * SIDE0 * 8, CELLS0), BF16),
        pltpu.VMEM((TILES * SIDE1 * 8, CELLS1), BF16),
        pltpu.VMEM((2, RIM0, CELLS0), BF16),
        pltpu.VMEM((2, RIM1, CELLS1), BF16),
        pltpu.VMEM((2, RIM0, CELLS0), BF16),
        pltpu.VMEM((CELLS0, 2 * CELLS1), BF16),
        pltpu.VMEM((CELLS1, CELLS0), BF16),
        pltpu.VMEM((2, RIM1, CELLS0), BF16),
        pltpu.VMEM((2, RIM0, 2 * CELLS1), BF16),
        pltpu.VMEM((TILES, SIDE0 + 6, 32, C0), F32),
        pltpu.VMEM((TILES, SIDE1 + 6, 24, C1), F32),
        pltpu.VMEM((2, TILES, 3, 32, C0), F32),
        pltpu.VMEM((2, TILES, 3, 24, C1), F32),
        pltpu.VMEM((TILES, SIDE0, SIDE0, C0), F32),
        pltpu.VMEM((TILES, SIDE1, SIDE1, C1), F32),
        pltpu.VMEM((TILES, 2, 3, SIDE0, C0), F32),
        pltpu.VMEM((TILES, 2, 3, SIDE0, C0), F32),
        pltpu.VMEM((TILES, SIDE0, SIDE0, C0), BF16),
        pltpu.VMEM((TILES, SIDE0, SIDE0, C0), BF16),
        pltpu.VMEM((CELLS0, C0), F32),
        pltpu.VMEM((2, RIM0, C0), F32),
        pltpu.VMEM((2, CELLS1, C1), F32),
        pltpu.VMEM((8, 256), jnp.int32),
        pltpu.VMEM((2, 8, 256), jnp.int32),
        pltpu.VMEM((STEPS, ROWS, CELLS0), BF16),
        pltpu.VMEM((STEPS, 2, ROWS, CELLS0), BF16),
        pltpu.VMEM((STEPS, 2, RIM0, C0), BF16),
        pltpu.VMEM((STEPS, 2, RIM0, C0), BF16),
        pltpu.VMEM((2 * STEPS, 2, RIM1, C1), BF16),
        pltpu.VMEM((2 * STEPS, 2, RIM1, C1), BF16),
        pltpu.SemaphoreType.DMA((4,)),
        pltpu.SemaphoreType.DMA((STEPS + 1,)),
        pltpu.SemaphoreType.DMA((4,)),
        pltpu.SemaphoreType.DMA((4,)),
        pltpu.SemaphoreType.DMA((STEPS,)),
        pltpu.SemaphoreType.DMA((STEPS,)),
        pltpu.SemaphoreType.DMA((2,)),
        pltpu.SemaphoreType.DMA((2,)),
        pltpu.SemaphoreType.DMA((STEPS, 2)),
        pltpu.SemaphoreType.DMA((STEPS, 2)),
        pltpu.SemaphoreType.DMA((STEPS, 2)),
        pltpu.SemaphoreType.DMA((STEPS, 2)),
        pltpu.SemaphoreType.DMA((2 * STEPS, 2)),
        pltpu.SemaphoreType.DMA((2 * STEPS, 2)),
    ]
    return pl.pallas_call(
        kernel,
        out_shape=(
            jax.ShapeDtypeStruct((STEPS, 1, FIELDS, CELLS0), F32),
            jax.ShapeDtypeStruct((1, C1, CELLS1), F32),
        ),
        in_specs=[hbm] * 4 + [pl.BlockSpec(memory_space=pltpu.VMEM)] * len(weights),
        out_specs=(hbm, hbm),
        scratch_shapes=scratch,
        compiler_params=pltpu.CompilerParams(
            collective_id=0, has_side_effects=True, vmem_limit_bytes=56 * 1024 * 1024
        ),
    )(states.transpose(1, 0, 2), gru_state.transpose(1, 0, 2), neighbours, orient, *weights)


def solution(mesh):
    in_specs = (
        P("segment", None, "face"),
        P("segment", None, "face"),
        P("face", None),
        P("face", None),
    ) + (P(),) * 18
    out_specs = (P(None, "segment", None, "face"), P("segment", None, "face"))
    return jax.shard_map(local, mesh=mesh, in_specs=in_specs, out_specs=out_specs, check_vma=False)
```
